256 devices in a mesh: ctx: 64 (over x, y, z_hi), head: 4 (over z_lo, core).
Axes of the slice: x: 4, y: 4, z: 8 (z_hi: 4, z_lo: 2; z = z_hi * 2 + z_lo), core: 2. Of those that a mesh axis runs over, the one named last changes fastest.
Arguments:
- queries: bfloat16 [16384, 2048], P('ctx', 'head'), may hold values from -160 to 160
- key_rows: bfloat16 [16384, 2048], P('ctx', 'head'), may hold values from -30 to 30
- value_rows: bfloat16 [16384, 2048], P('ctx', 'head'), may hold values from -6 to 6
- out_weight: bfloat16 [2048, 4096], P('head'), may hold values from -0.125 to 0.125
- upstream: bfloat16 [16384, 4096], P('ctx', 'head'), may hold values from -6 to 6
- summary_index: int32 [64, 128], P('ctx'), may hold values from 0 to 255, as said below
- stride_offset: int32 [64, 4], replicated, may hold values from 0 to 15
Outputs:
- layer_out: bfloat16 [16384, 4096], P('ctx', 'head')
- query_grad: bfloat16 [16384, 2048], P('ctx', 'head')
- key_grad: bfloat16 [16384, 2048], P('ctx', 'head')
- value_grad: bfloat16 [16384, 2048], P('ctx', 'head')
The draws below stay inside these ranges and needn't reach their ends.
Inputs may be any that keep to these rules, and one draw needn't show every extreme that they name: `summary_index`: each row t lists 128 distinct positions within shard t.
All inputs are finite; a program needn't handle non-finite values.
Results may differ from the reference program's by a relative error of at most 0.015.
Values may be sent and summed in bfloat16 or wider, within the bound.
No kernel may reach another device: no remote copies, remote signals or barrier semaphores. Data moves between devices by JAX's collectives and lax.ppermute only.
A program may use at most 128 MiB of HBM per device.

```python
import jax
import jax.numpy as jnp
from jax import lax

D = 4096
HEADS = 16
HEAD_DIM = 128
SUMM = 128
STRIDE = 16
TOK_DEV = 256
SEQ = 16384
SHARDS = 64
N_CTX = 64


def pair_draw(key):
    base = jax.random.fold_in(key, 101)
    first, second = jax.random.split(base, 2)
    shape = (SEQ, HEADS, HEAD_DIM)
    query_vals = jax.random.truncated_normal(first, -6.0, 6.0, shape, jnp.float32)
    key_vals = jax.random.truncated_normal(second, -6.0, 6.0, shape, jnp.float32)
    return (query_vals.reshape(SEQ, HEADS * HEAD_DIM), key_vals.reshape(SEQ, HEADS * HEAD_DIM))


def draw_queries(key, part):
    return pair_draw(key)[0].astype(jnp.bfloat16)


def draw_key_rows(key, part):
    return pair_draw(key)[1].astype(jnp.bfloat16)


def draw_summary_index(key, part):
    row_keys = jax.random.split(jax.random.fold_in(key, 11), SHARDS)
    return jax.vmap(lambda row_key: jax.random.permutation(row_key, TOK_DEV)[:SUMM])(row_keys).astype(jnp.int32)


def with_ends(entries, own_key, smallest, top_value):
    index_at = [jax.random.randint(jax.random.fold_in(own_key, axis), (), 0, length) for axis, length in enumerate(entries.shape)]
    widest = entries.shape.index(max(entries.shape))
    beside = index_at[:widest] + [(index_at[widest] + 1) % entries.shape[widest]] + index_at[widest + 1:]
    return entries.at[tuple(index_at)].set(smallest).at[tuple(beside)].set(top_value)


def steps_of(stream_key, extent, cuts, smallest, high):
    def one(dim, shards_of):
        steps = jax.random.uniform(jax.random.fold_in(jax.random.fold_in(stream_key, 6), dim), (shards_of,), jnp.float32, smallest / len(cuts), high / len(cuts))
        return jnp.repeat(jnp.exp(steps), extent[dim] // shards_of).reshape((-1,) + (1,) * (len(extent) - dim - 1))

    loudness = one(*cuts[0])
    for cut in cuts[1:]:
        loudness = loudness * one(*cut)
    return loudness


def scatter_about(key, dims, width, bound, shards=(), kind=jnp.bfloat16):
    entries = width * jax.random.normal(key, dims, jnp.float32)
    if shards:
        entries = entries * steps_of(key, dims, shards, -0.22, 0.18)
    return jnp.clip(entries, -bound, bound).astype(kind)


def setup_inputs(seed: int = 0) -> dict:
    key_of = jax.random.split(jax.random.key(seed), 8)
    queries = draw_queries(jax.random.fold_in(key_of[7], 71), 0)
    key_rows = draw_key_rows(jax.random.fold_in(key_of[7], 71), 0)
    value_rows = scatter_about(key_of[2], (SEQ, HEADS * HEAD_DIM), 1.0, 6.0, ((0, 64), (1, 4)))
    out_weight = scatter_about(key_of[3], (HEADS * HEAD_DIM, D), (HEADS * HEAD_DIM) ** -0.5, 0.125, ((0, 4),))
    upstream = scatter_about(key_of[4], (SEQ, D), 1.0, 6.0, ((0, 64), (1, 4)))
    summary_index = draw_summary_index(jax.random.fold_in(key_of[7], 71), 0)
    stride_offset = with_ends(jax.random.randint(key_of[6], (SHARDS, 4), 0, STRIDE), jax.random.fold_in(key_of[6], 1), 0, STRIDE - 1).astype(jnp.int32)
    return dict(queries=queries, key_rows=key_rows, value_rows=value_rows, out_weight=out_weight, upstream=upstream, summary_index=summary_index, stride_offset=stride_offset)


masked_fill = -1.0e30


def attend(query_block, key_block, value_block, grad_block, allowed):
    scale_factor = HEAD_DIM ** -0.5
    scores = jnp.einsum('thd,khd->htk', query_block.astype(jnp.float32), key_block.astype(jnp.float32)) * scale_factor
    scores = jnp.where(allowed[None], scores, masked_fill)
    row_max = jnp.max(scores, axis=-1, keepdims=True)
    exp_scores = jnp.exp(scores - row_max)
    row_sum = jnp.sum(exp_scores, axis=-1, keepdims=True)
    normed = exp_scores / row_sum
    weights = normed.astype(jnp.bfloat16)
    attended = jnp.einsum('htk,khd->thd', weights.astype(jnp.float32), value_block.astype(jnp.float32)).astype(jnp.bfloat16)
    dprob = jnp.einsum('thd,khd->htk', grad_block.astype(jnp.float32), value_block.astype(jnp.float32))
    row_delta = jnp.einsum('thd,thd->ht', grad_block.astype(jnp.float32), attended.astype(jnp.float32))[..., None]
    dscore = (normed * (dprob - row_delta) * scale_factor).astype(jnp.bfloat16)
    query_part = jnp.einsum('htk,khd->thd', dscore.astype(jnp.float32), key_block.astype(jnp.float32))
    key_part = jnp.einsum('htk,thd->khd', dscore.astype(jnp.float32), query_block.astype(jnp.float32))
    value_part = jnp.einsum('htk,thd->khd', weights.astype(jnp.float32), grad_block.astype(jnp.float32))
    return attended, query_part, key_part, value_part


def split_heads(block):
    groups = HEADS // 4
    shaped = block.reshape(N_CTX, TOK_DEV, groups, 4, HEAD_DIM)
    return shaped[:, :, :, 0, :], shaped[:, :, :, 1:, :].reshape(N_CTX, TOK_DEV, groups * 3, HEAD_DIM)


def join_heads(fixed, strided):
    groups = HEADS // 4
    joined = jnp.concatenate([fixed[:, :, :, None, :], strided.reshape(N_CTX, TOK_DEV, groups, 3, HEAD_DIM)], 3)
    return joined.reshape(SEQ, HEADS * HEAD_DIM)


def reference(queries, key_rows, value_rows, out_weight, upstream, summary_index, stride_offset):
    groups = HEADS // 4
    reach = TOK_DEV // STRIDE
    attn_grad = jnp.dot(upstream, out_weight.T, preferred_element_type=jnp.float32).astype(jnp.bfloat16)
    fixed_q, strided_q = split_heads(queries)
    fixed_k, strided_k = split_heads(key_rows)
    fixed_v, strided_v = split_heads(value_rows)
    fixed_g, strided_g = split_heads(attn_grad)
    positions = jnp.arange(TOK_DEV, dtype=jnp.int32)
    causal = positions[:, None] >= positions[None, :]
    picked = summary_index.astype(jnp.int32)
    summary_keys = jnp.take_along_axis(fixed_k, picked[:, :, None, None], axis=1).reshape(N_CTX * SUMM, groups, HEAD_DIM)
    summary_vals = jnp.take_along_axis(fixed_v, picked[:, :, None, None], axis=1).reshape(N_CTX * SUMM, groups, HEAD_DIM)
    owners = jnp.arange(N_CTX * SUMM, dtype=jnp.int32) // SUMM

    def fixed_step(carry, shard_at):
        key_acc, value_acc = carry
        key_set = jnp.concatenate([fixed_k[shard_at], summary_keys], 0)
        value_set = jnp.concatenate([fixed_v[shard_at], summary_vals], 0)
        allowed = jnp.concatenate([causal, jnp.broadcast_to((owners < shard_at)[None], (TOK_DEV, N_CTX * SUMM))], 1)
        attended, query_part, key_part, value_part = attend(fixed_q[shard_at], key_set, value_set, fixed_g[shard_at], allowed)
        return (key_acc + key_part[TOK_DEV:], value_acc + value_part[TOK_DEV:]), (attended, query_part, key_part[:TOK_DEV], value_part[:TOK_DEV])

    empty_sum = jnp.zeros((N_CTX * SUMM, groups, HEAD_DIM), jnp.float32)
    shard_ids = jnp.arange(N_CTX, dtype=jnp.int32)
    (sum_kgrad, sum_vgrad), (fixed_out, fixed_qgrad, fixed_kgrad, fixed_vgrad) = lax.scan(fixed_step, (empty_sum, empty_sum), shard_ids)
    fixed_kgrad = fixed_kgrad.at[shard_ids[:, None], picked].add(sum_kgrad.reshape(N_CTX, SUMM, groups, HEAD_DIM))
    fixed_vgrad = fixed_vgrad.at[shard_ids[:, None], picked].add(sum_vgrad.reshape(N_CTX, SUMM, groups, HEAD_DIM))

    phases = jnp.arange(reach, dtype=jnp.int32) * STRIDE

    def strided_step(carry, shard_at):
        key_acc, value_acc = carry
        key_list = [strided_k[shard_at]]
        value_list = [strided_v[shard_at]]
        mask_list = [causal]
        sources = []
        for slot_num in range(4):
            source = shard_at - 1 - slot_num
            clamped = jnp.maximum(source, 0).astype(jnp.int32)
            rows_at = (stride_offset[shard_at, slot_num] + phases).astype(jnp.int32)
            key_list.append(strided_k[clamped][rows_at])
            value_list.append(strided_v[clamped][rows_at])
            mask_list.append(jnp.broadcast_to(source >= 0, (TOK_DEV, reach)))
            sources.append((clamped, rows_at))
        allowed = jnp.concatenate(mask_list, 1)
        attended, query_part, key_part, value_part = attend(strided_q[shard_at], jnp.concatenate(key_list, 0), jnp.concatenate(value_list, 0), strided_g[shard_at], allowed)
        key_acc = key_acc.at[shard_at].add(key_part[:TOK_DEV])
        value_acc = value_acc.at[shard_at].add(value_part[:TOK_DEV])
        for slot_num in range(4):
            clamped, rows_at = sources[slot_num]
            low = TOK_DEV + slot_num * reach
            key_acc = key_acc.at[clamped, rows_at].add(key_part[low:low + reach])
            value_acc = value_acc.at[clamped, rows_at].add(value_part[low:low + reach])
        return (key_acc, value_acc), (attended, query_part)

    empty_all = jnp.zeros((N_CTX, TOK_DEV, groups * 3, HEAD_DIM), jnp.float32)
    (strided_kgrad, strided_vgrad), (strided_out, strided_qgrad) = lax.scan(strided_step, (empty_all, empty_all), shard_ids)

    attended_all = join_heads(fixed_out.astype(jnp.float32), strided_out.astype(jnp.float32)).astype(jnp.bfloat16)
    layer_out = jnp.dot(attended_all, out_weight, preferred_element_type=jnp.float32).astype(jnp.bfloat16)
    query_grad = join_heads(fixed_qgrad, strided_qgrad).astype(jnp.bfloat16)
    key_grad = join_heads(fixed_kgrad, strided_kgrad).astype(jnp.bfloat16)
    value_grad = join_heads(fixed_vgrad, strided_vgrad).astype(jnp.bfloat16)
    return layer_out, query_grad, key_grad, value_grad
```

```python
import functools

import jax
import jax.numpy as jnp
from jax import lax
from jax.experimental import pallas as pl
from jax.experimental.pallas import tpu as pltpu
from jax.sharding import Mesh
from jax.sharding import PartitionSpec as P

HEAD = 128
TOK = 256
SUMM = 128
STRIDE = 16
REACH = TOK // STRIDE
ROWS = 16
GROUP = 4
STAT = 64
FAR = 6 * REACH
SCALE = HEAD ** (-0.5)
NEG = -1e30
F32 = jnp.float32
BF = jnp.bfloat16

VM = pl.BlockSpec(memory_space=pltpu.VMEM)
SM = pl.BlockSpec(memory_space=pltpu.SMEM)


def nn(a, b):
    return lax.dot_general(a, b, (((1,), (0,)), ((), ())), preferred_element_type=F32)


def nt(a, b):
    return lax.dot_general(a, b, (((1,), (1,)), ((), ())), preferred_element_type=F32)


def tn(a, b):
    return lax.dot_general(a, b, (((0,), (0,)), ((), ())), preferred_element_type=F32)


def iota(shape, dim):
    return lax.broadcasted_iota(jnp.int32, shape, dim)


def summary_select(sidx):
    return (iota((TOK, SUMM), 0) == sidx).astype(F32).astype(BF)


def stride_select(soff, shard):
    row, col = iota((4 * REACH, TOK), 0), iota((4 * REACH, TOK), 1)
    slot = row // REACH
    want = (row % REACH) * STRIDE
    for u in range(4):
        there = jnp.minimum(shard + 1 + u, ROWS * GROUP - 1)
        want = want + jnp.where(slot == u, soff[there, u], 0)
    return (want == col).astype(F32).astype(BF)


def call(kernel, outs, ins, flops, scratch=(), name=None, vmem=50):
    moved = sum(
        s.size * jnp.dtype(s.dtype).itemsize for s in list(outs) + list(ins)
    )
    return pl.pallas_call(
        kernel,
        out_shape=tuple(outs),
        in_specs=[SM if s.dtype == jnp.int32 and s.shape != (1, SUMM) else VM for s in ins],
        out_specs=tuple(VM for _ in outs),
        scratch_shapes=list(scratch),
        compiler_params=pltpu.CompilerParams(vmem_limit_bytes=vmem * 2**20),
        cost_estimate=pl.CostEstimate(
            flops=flops, bytes_accessed=moved, transcendentals=0
        ),
        name=name,
    )(*ins)


def sds(shape, dtype=BF):
    return jax.ShapeDtypeStruct(shape, dtype)


def prep_kernel(meta, soff, sidx, q, k, v, kvb, qb, picks):
    pick = summary_select(sidx[...])
    kv = jnp.concatenate([k[:, :HEAD], v[:, :HEAD]], 1)
    kv = tn(pick, kv).astype(BF)
    for i in range(ROWS):
        kvb[i] = kv
    for i in range(GROUP):
        qb[i] = q[:, :HEAD]
    shard = GROUP * meta[0] + meta[1]
    sel = stride_select(soff, shard)
    got = nn(sel, jnp.concatenate([k[:, HEAD:], v[:, HEAD:]], 1)).astype(BF)
    for u in range(4):
        for h in range(6):
            picks[u, h * REACH : (h + 1) * REACH, :] = got[
                u * REACH : (u + 1) * REACH, h * HEAD : (h + 1) * HEAD
            ]


def grad_kernel(meta, up, up_c, up_z, up_zc, w, picks, before, g, gb):
    zl, c = meta[2], meta[3]
    wide = up.shape[1]
    acc = None
    for ref, z, core in (
        (up, zl, c),
        (up_c, zl, 1 - c),
        (up_z, 1 - zl, c),
        (up_zc, 1 - zl, 1 - c),
    ):
        at = pl.multiple_of((2 * z + core) * wide, wide)
        part = nt(ref[...], w[:, pl.ds(at, wide)])
        acc = part if acc is None else acc + part
    full = acc.astype(BF)
    g[...] = full
    zh = meta[1]
    for t in range(GROUP):
        gb[t, :TOK, :] = full[:, :HEAD]
        u = lax.rem(t - zh - 1 + 2 * GROUP, GROUP)

        @pl.when(t > zh)
        def _(t=t, u=u):
            gb[t, TOK:, :] = picks[u]

        @pl.when(t <= zh)
        def _(t=t, u=u):
            gb[t, TOK:, :] = before[u]


def causal_mask():
    return iota((TOK, TOK), 0) >= iota((TOK, TOK), 1)


def lanes(a):
    return jnp.broadcast_to(a, (a.shape[0], HEAD))


def fold(a, how):
    out = a[:, :HEAD]
    for j in range(1, a.shape[1] // HEAD):
        out = how(out, a[:, j * HEAD : (j + 1) * HEAD])
    return out


def split3(a):
    hi = a.astype(BF).astype(F32)
    mid = (a - hi).astype(BF).astype(F32)
    return hi, mid, (a - hi - mid).astype(BF).astype(F32)


def stat_rows(log_sums, dots):
    eye = (iota((TOK, TOK), 0) == iota((TOK, TOK), 1)).astype(F32).astype(BF)
    lane = iota((TOK, HEAD), 1)
    total = None
    for z in range(GROUP):
        parts = split3(log_sums[z]) + split3(dots[z])
        cols = jnp.zeros((TOK, HEAD), F32)
        for j, part in enumerate(parts):
            cols = jnp.where(lane == 8 * z + j, part, cols)
        rows = tn(cols.astype(BF), eye)[: 8 * GROUP]
        total = rows if total is None else total + rows
    return jnp.concatenate([total[:, :HEAD], total[:, HEAD:]], 0).astype(BF)


def read_stats(stats, z):
    row = iota((8 * GROUP, 2 * HEAD), 0)
    col = iota((8 * GROUP, 2 * HEAD), 1)
    first = jnp.where(col < HEAD, 8 * z, 8 * z + 3)
    pick = ((row >= first) & (row < first + 3)).astype(F32).astype(BF)
    both = jnp.concatenate(
        [tn(stats[: STAT // 2], pick), tn(stats[STAT // 2 :], pick)], 0
    )
    return both[:, :HEAD], both[:, HEAD:]


def forward_kernel(meta, qa, kva, ga, k, v, ob, s_ref):
    row, zh = meta[0], meta[1]
    total = GROUP * TOK
    q = qa[...].reshape(total, HEAD)
    g = ga[:, :TOK, :].reshape(total, HEAD)
    limit = HEAD * (row + (iota((total, 1), 0) // TOK > zh).astype(jnp.int32))
    wide = 2 * SUMM
    tiles = ROWS * SUMM // wide
    top = jnp.full((total, HEAD), NEG, F32)
    for j in range(tiles):
        s = nt(q, kva[j * wide : (j + 1) * wide, :HEAD]) * SCALE
        s = jnp.where(iota((total, wide), 1) + j * wide < limit, s, NEG)
        s_ref[:, j * wide : (j + 1) * wide] = s
        top = jnp.maximum(top, fold(s, jnp.maximum))
    top = jnp.max(top, axis=1, keepdims=True)
    shift = jnp.maximum(top, 0.5 * NEG)
    sums = jnp.zeros((total, HEAD), F32)
    dots = jnp.zeros((total, HEAD), F32)
    out = jnp.zeros((total, HEAD), F32)
    for j in range(tiles):
        at = slice(j * wide, (j + 1) * wide)
        e = jnp.exp(s_ref[:, at] - shift)
        value = kva[at, HEAD:]
        sums = sums + fold(e, jnp.add)
        dots = dots + fold(e * nt(g, value), jnp.add)
        out = out + nn(e.astype(BF), value)
    sums = jnp.sum(sums, axis=1, keepdims=True)
    dots = jnp.sum(dots, axis=1, keepdims=True)
    some = sums > 0
    safe = jnp.where(some, sums, 1.0)
    log_sum = lanes(jnp.where(some, top + jnp.log(safe), NEG))
    inv = 1.0 / safe
    dots = lanes(dots * inv)
    out = out * inv

    own_q, own_g = qa[zh], ga[zh, :TOK, :]
    s = jnp.where(causal_mask(), nt(own_q, k[...]) * SCALE, NEG)
    own_top = jnp.max(s, axis=1, keepdims=True)
    e = jnp.exp(s - own_top)
    own_sum = jnp.sum(e, axis=1, keepdims=True)
    own_inv = 1.0 / own_sum
    own_dot = lanes(
        jnp.sum(e * nt(own_g, v[...]), axis=1, keepdims=True) * own_inv
    )
    own_out = nn(e.astype(BF), v[...]) * own_inv
    own_log = lanes(own_top + jnp.log(own_sum))

    all_logs, all_dots = [], []
    for z in range(GROUP):
        at = slice(z * TOK, (z + 1) * TOK)
        la = log_sum[at]
        lb = jnp.where(zh == z, own_log, NEG)
        most = jnp.maximum(la, lb)
        wa, wb = jnp.exp(la - most), jnp.exp(lb - most)
        both = wa + wb
        wa, wb = wa / both, wb / both
        all_logs.append(most + jnp.log(both))
        all_dots.append(wa * dots[at] + wb * own_dot)
        ob[z, :TOK, :] = (wa * out[at] + wb * own_out).astype(BF)
    stats = stat_rows(all_logs, all_dots)
    for z in range(GROUP):
        ob[z, TOK:, :] = stats


def merged(oa, z):
    parts = [read_stats(oa[d, TOK:, :], z) for d in range(GROUP)]
    most = functools.reduce(jnp.maximum, [p[0] for p in parts])
    shares = [jnp.exp(p[0] - most) for p in parts]
    both = functools.reduce(jnp.add, shares)
    shares = [s / both for s in shares]
    dot = functools.reduce(jnp.add, [s * p[1] for s, p in zip(shares, parts)])
    return most + jnp.log(both), dot, shares


def backward_kernel(meta, oa, qa, kva, ga, k, v, far, dkv, dqb, own, dq_ref, stat_ref):
    row, zh = meta[0], meta[1]
    total = GROUP * TOK
    for z in range(GROUP):
        at = slice(z * TOK, (z + 1) * TOK)
        log_sum, dot, _ = merged(oa, z)
        stat_ref[0, at] = log_sum
        stat_ref[1, at] = dot
        dqb[z, TOK:, :] = far[z]
    dq_ref[...] = jnp.zeros((total, HEAD), F32)
    wide = 2 * SUMM
    for j in range(ROWS * SUMM // wide):
        at = slice(j * wide, (j + 1) * wide)

        @pl.when(2 * j <= row)
        def _(j=j, at=at):
            q = qa[...].reshape(total, HEAD)
            g = ga[:, :TOK, :].reshape(total, HEAD)
            limit = HEAD * (row + (iota((total, 1), 0) // TOK > zh).astype(jnp.int32))
            key, value = kva[at, :HEAD], kva[at, HEAD:]
            log_sum = jnp.concatenate([stat_ref[0]] * 2, 1)
            dot = jnp.concatenate([stat_ref[1]] * 2, 1)
            s = nt(q, key) * SCALE
            s = jnp.where(iota((total, wide), 1) + j * wide < limit, s, NEG)
            p = jnp.exp(s - log_sum)
            dv = tn(p.astype(BF), g)
            ds = (p * (nt(g, value) - dot) * SCALE).astype(BF)
            dk = tn(ds, q)
            dq_ref[...] += nn(ds, key)
            dkv[at, :HEAD] = dk.astype(BF)
            dkv[at, HEAD:] = dv.astype(BF)

        @pl.when(2 * j > row)
        def _(at=at):
            dkv[at, :] = jnp.zeros((wide, 2 * HEAD), BF)

    own_at = pl.ds(pl.multiple_of(zh * TOK, TOK), TOK)
    own_q, own_g = qa[zh], ga[zh, :TOK, :]
    log_sum = jnp.concatenate([stat_ref[0, own_at]] * 2, 1)
    dot = jnp.concatenate([stat_ref[1, own_at]] * 2, 1)
    s = jnp.where(causal_mask(), nt(own_q, k[...]) * SCALE, NEG)
    p = jnp.exp(s - log_sum)
    own[:, HEAD:] = tn(p.astype(BF), own_g)
    ds = (p * (nt(own_g, v[...]) - dot) * SCALE).astype(BF)
    own[:, :HEAD] = tn(ds, own_q)
    dq_ref[own_at] += nn(ds, k[...])
    for z in range(GROUP):
        dqb[z, :TOK, :] = dq_ref[z * TOK : (z + 1) * TOK].astype(BF)


def strided_kernel(meta, q, k, v, g, ga, o, dq, dkv, far):
    row, zh = meta[0], meta[1]
    source = iota((TOK, 4 * REACH), 1) // REACH
    far_ok = (source < zh) | (jnp.full((TOK, 4 * REACH), row, jnp.int32) > 0)
    near_ok = causal_mask()
    for h in range(3):
        at = slice((h + 1) * HEAD, (h + 2) * HEAD)
        to = slice(h * HEAD, (h + 1) * HEAD)
        qh, kh, vh, gh = q[:, at], k[:, at], v[:, at], g[:, at]
        kf = ga[:, TOK + h * REACH : TOK + (h + 1) * REACH, :]
        vf = ga[:, TOK + (h + 3) * REACH : TOK + (h + 4) * REACH, :]
        kf, vf = kf.reshape(4 * REACH, HEAD), vf.reshape(4 * REACH, HEAD)
        s = jnp.where(near_ok, nt(qh, kh) * SCALE, NEG)
        sf = jnp.where(far_ok, nt(qh, kf) * SCALE, NEG)
        top = jnp.maximum(
            jnp.max(s, axis=1, keepdims=True), jnp.max(sf, axis=1, keepdims=True)
        )
        e, ef = jnp.exp(s - top), jnp.exp(sf - top)
        inv = 1.0 / (
            jnp.sum(e, axis=1, keepdims=True) + jnp.sum(ef, axis=1, keepdims=True)
        )
        p, pf = e * inv, ef * inv
        w, wf = p.astype(BF), pf.astype(BF)
        out = (nn(w, vh) + nn(wf, vf)).astype(BF)
        o[:, to] = out
        delta = jnp.sum(gh.astype(F32) * out.astype(F32), axis=1, keepdims=True)
        ds = (p * (nt(gh, vh) - delta) * SCALE).astype(BF)
        dsf = (pf * (nt(gh, vf) - delta) * SCALE).astype(BF)
        dq[:, to] = (nn(ds, kh) + nn(dsf, kf)).astype(BF)
        dkv[:, to] = tn(ds, qh)
        dkv[:, 3 * HEAD + h * HEAD : 3 * HEAD + (h + 1) * HEAD] = tn(w, gh)
        dkf = tn(dsf, qh).astype(BF)
        dvf = tn(wf, gh).astype(BF)
        for z in range(GROUP):
            rows = slice(z * REACH, (z + 1) * REACH)
            far[z, h * REACH : (h + 1) * REACH, :] = dkf[rows]
            far[z, (h + 3) * REACH : (h + 4) * REACH, :] = dvf[rows]


def project_kernel(meta, oa, o, w, keep, keep_z, send, send_z):
    zh, zl, c = meta[1], meta[2], meta[3]
    _, _, shares = merged(oa, zh)
    fixed = functools.reduce(
        jnp.add, [shares[d] * oa[d, :TOK, :].astype(F32) for d in range(GROUP)]
    )
    att = jnp.concatenate([fixed.astype(BF), o[...]], 1)
    wide = keep.shape[1]
    for ref, z, core in (
        (send_z, 1 - zl, 1 - c),
        (send, zl, 1 - c),
        (keep_z, 1 - zl, c),
        (keep, zl, c),
    ):
        at = pl.multiple_of((2 * z + core) * wide, wide)
        ref[...] = nn(att, w[:, pl.ds(at, wide)]).astype(BF)


def final_kernel(
    meta, soff, sidx, dkv, own, dq, after, strided_dq, strided, qg, kg, vg
):
    zh = meta[1]
    shard = GROUP * meta[0] + meta[1]
    pick = summary_select(sidx[...])
    fixed = own[...] + nn(jnp.concatenate([pick] * ROWS, 1), dkv[...])
    kg[:, :HEAD] = fixed[:, :HEAD].astype(BF)
    vg[:, :HEAD] = fixed[:, HEAD:].astype(BF)
    fixed = functools.reduce(
        jnp.add, [dq[z, :TOK, :].astype(F32) for z in range(GROUP)]
    )
    qg[:, :HEAD] = fixed.astype(BF)
    qg[:, HEAD:] = strided_dq[...]
    sel = stride_select(soff, shard)
    slots = []
    for u in range(4):
        t = lax.rem(zh + 1 + u, GROUP)
        here = dq[t, TOK:, :].astype(F32)
        there = after[t].astype(F32)
        block = jnp.where(t > zh, here, there).astype(BF)
        slots.append(
            jnp.concatenate(
                [block[h * REACH : (h + 1) * REACH] for h in range(6)], 1
            )
        )
    total = strided[...] + tn(sel, jnp.concatenate(slots, 0))
    kg[:, HEAD:] = total[:, : 3 * HEAD].astype(BF)
    vg[:, HEAD:] = total[:, 3 * HEAD :].astype(BF)


def swap(a, axis):
    return lax.ppermute(a, axis, [(0, 1), (1, 0)])


def shards(queries, key_rows, value_rows, out_weight, upstream, summary_index, soff):
    row = lax.axis_index(("x", "y"))
    zh, zl, c = lax.axis_index("zh"), lax.axis_index("zl"), lax.axis_index("c")
    meta = jnp.stack([row, zh, zl, c]).astype(jnp.int32)
    width = queries.shape[1]
    quarter = upstream.shape[1]
    plane = ("x", "y")
    matmul = 2 * GROUP * TOK * ROWS * SUMM * HEAD

    up_z = swap(upstream, "zl")
    up_c = swap(upstream, "c")
    kvb, qb, picks = call(
        prep_kernel,
        [sds((ROWS, SUMM, 2 * HEAD)), sds((GROUP, TOK, HEAD)), sds((4, FAR, HEAD))],
        [meta, soff, summary_index, queries, key_rows, value_rows],
        10**8,
        name="pick_rows",
    )
    before = lax.ppermute(picks, plane, [(i, i + 1) for i in range(ROWS - 1)])
    qa = lax.all_to_all(qb, "zh", 0, 0, tiled=True)
    kva = lax.all_to_all(kvb, plane, 0, 0, tiled=True).reshape(ROWS * SUMM, 2 * HEAD)
    up_zc = swap(up_z, "c")
    g, gb = call(
        grad_kernel,
        [sds((TOK, width)), sds((GROUP, TOK + FAR, HEAD))],
        [meta, upstream, up_c, up_z, up_zc, out_weight, picks, before],
        2 * TOK * 4 * quarter * width,
        name="attention_grad",
    )
    ga = lax.all_to_all(gb, "zh", 0, 0, tiled=True)
    key0, value0 = key_rows[:, :HEAD], value_rows[:, :HEAD]
    (ob,) = call(
        forward_kernel,
        [sds((GROUP, TOK + STAT, HEAD))],
        [meta, qa, kva, ga, key0, value0],
        3 * matmul,
        [pltpu.VMEM((GROUP * TOK, ROWS * SUMM), F32)],
        name="fixed_forward",
    )
    oa = lax.all_to_all(ob, "zh", 0, 0, tiled=True)
    o_s, dq_s, dkv_s, far = call(
        strided_kernel,
        [
            sds((TOK, 3 * HEAD)),
            sds((TOK, 3 * HEAD)),
            sds((TOK, 6 * HEAD), F32),
            sds((GROUP, FAR, HEAD)),
        ],
        [meta, queries, key_rows, value_rows, g, ga],
        3 * 6 * 2 * TOK * 320 * HEAD,
        name="strided_heads",
    )
    keep, keep_z, send, send_z = call(
        project_kernel,
        [sds((TOK, quarter))] * 4,
        [meta, oa, o_s, out_weight],
        2 * TOK * 4 * quarter * width,
        name="project",
    )
    dkv, dqb, own = call(
        backward_kernel,
        [
            sds((ROWS * SUMM, 2 * HEAD)),
            sds((GROUP, TOK + FAR, HEAD)),
            sds((TOK, 2 * HEAD), F32),
        ],
        [meta, oa, qa, kva, ga, key0, value0, far],
        5 * matmul,
        [
            pltpu.VMEM((GROUP * TOK, HEAD), F32),
            pltpu.VMEM((2, GROUP * TOK, HEAD), F32),
        ],
        name="fixed_backward",
    )
    got_z = swap(send_z, "c")
    got = swap(send, "c")
    over = swap((keep_z.astype(F32) + got_z.astype(F32)).astype(BF), "zl")
    dkva = lax.all_to_all(
        dkv.reshape(ROWS, SUMM, 2 * HEAD), plane, 0, 0, tiled=True
    ).reshape(ROWS * SUMM, 2 * HEAD)
    dqa = lax.all_to_all(dqb, "zh", 0, 0, tiled=True)
    after = lax.ppermute(
        dqa[:, TOK:, :], plane, [(i + 1, i) for i in range(ROWS - 1)]
    )
    layer_out = (keep.astype(F32) + got.astype(F32) + over.astype(F32)).astype(BF)
    query_grad, key_grad, value_grad = call(
        final_kernel,
        [sds((TOK, width))] * 3,
        [meta, soff, summary_index, dkva, own, dqa, after, dq_s, dkv_s],
        3 * 10**8,
        name="join_grads",
    )
    return layer_out, query_grad, key_grad, value_grad


def solution(mesh):
    grid = Mesh(mesh.devices.reshape(4, 4, 4, 2, 2), ("x", "y", "zh", "zl", "c"))
    ctx, head = ("x", "y", "zh"), ("zl", "c")
    return jax.shard_map(
        shards,
        mesh=grid,
        in_specs=(
            P(ctx, head),
            P(ctx, head),
            P(ctx, head),
            P(head, None),
            P(ctx, head),
            P(ctx, None),
            P(),
        ),
        out_specs=(P(ctx, head),) * 4,
        check_vma=False,
    )
```

```python
import functools

import jax
import jax.numpy as jnp
from jax import lax
from jax.experimental import pallas as pl
from jax.experimental.pallas import tpu as pltpu
from jax.sharding import Mesh
from jax.sharding import PartitionSpec as P

HEAD = 128
TOK = 256
SUMM = 128
STRIDE = 16
REACH = TOK // STRIDE
ROWS = 16
GROUP = 4
ALL = GROUP * TOK
KEYS = ROWS * SUMM
TILE = 256
STAT = 64
FAR = 6 * REACH
SCALE = HEAD ** (-0.5)
LOG2E = 1.4426950408889634
SCALE2 = SCALE * LOG2E
NEG = -1e30
F32 = jnp.float32
BF = jnp.bfloat16

VM = pl.BlockSpec(memory_space=pltpu.VMEM)
SM = pl.BlockSpec(memory_space=pltpu.SMEM)
ANY = pl.BlockSpec(memory_space=pl.ANY)


def nn(a, b):
    return lax.dot_general(a, b, (((1,), (0,)), ((), ())), preferred_element_type=F32)


def nt(a, b):
    return lax.dot_general(a, b, (((1,), (1,)), ((), ())), preferred_element_type=F32)


def tn(a, b):
    return lax.dot_general(a, b, (((0,), (0,)), ((), ())), preferred_element_type=F32)


def iota(shape, dim):
    return lax.broadcasted_iota(jnp.int32, shape, dim)


def ones_where(condition):
    return condition.astype(F32).astype(BF)


def summary_select(sidx):
    return ones_where(iota((TOK, SUMM), 0) == sidx)


def stride_select(soff_t, shard):
    there = jnp.minimum(shard + 1 + iota((4, ROWS * GROUP), 0), ROWS * GROUP - 1)
    offset = jnp.where(iota((4, ROWS * GROUP), 1) == there, soff_t, 0)
    offset = jnp.sum(offset.astype(F32), axis=1, keepdims=True).astype(jnp.int32)
    row, col = iota((4 * REACH, TOK), 0), iota((4 * REACH, TOK), 1)
    slot = row // REACH
    want = (row % REACH) * STRIDE
    for u in range(4):
        want = want + jnp.where(slot == u, offset[u : u + 1], 0)
    return ones_where(want == col)


def call(kernel, outs, ins, flops, scratch=(), name=None, vmem=24, specs=None):
    moved = sum(
        s.size * jnp.dtype(s.dtype).itemsize for s in list(outs) + list(ins)
    )
    return pl.pallas_call(
        kernel,
        out_shape=tuple(outs),
        in_specs=specs or [SM] + [VM] * (len(ins) - 1),
        out_specs=tuple(VM for _ in outs),
        scratch_shapes=list(scratch),
        compiler_params=pltpu.CompilerParams(vmem_limit_bytes=vmem * 2**20),
        cost_estimate=pl.CostEstimate(
            flops=flops, bytes_accessed=moved, transcendentals=0
        ),
        name=name,
    )(*ins)


def sds(shape, dtype=BF):
    return jax.ShapeDtypeStruct(shape, dtype)


def prep_kernel(
    meta, soff_t, sidx, q, k, v, kvb, q0, kv0, picks, kb, vb, ib, sb, sems
):
    copies = [
        pltpu.make_async_copy(k, kb, sems.at[0]),
        pltpu.make_async_copy(v, vb, sems.at[1]),
        pltpu.make_async_copy(sidx, ib, sems.at[2]),
        pltpu.make_async_copy(soff_t, sb, sems.at[3]),
        pltpu.make_async_copy(q.at[:, pl.ds(0, HEAD)], q0, sems.at[4]),
    ]
    for copy in copies:
        copy.start()
    for copy in copies:
        copy.wait()
    pick = summary_select(ib[...])
    kv = jnp.concatenate([kb[:, :HEAD], vb[:, :HEAD]], 1)
    kv0[...] = kv
    kv = tn(pick, kv).astype(BF)
    for i in range(ROWS):
        kvb[i] = kv
    sel = stride_select(sb[...], GROUP * meta[0] + meta[1])
    got = nn(sel, jnp.concatenate([kb[:, HEAD:], vb[:, HEAD:]], 1)).astype(BF)
    for u in range(4):
        for h in range(6):
            picks[u, h * REACH : (h + 1) * REACH, :] = got[
                u * REACH : (u + 1) * REACH, h * HEAD : (h + 1) * HEAD
            ]


def bundle_kernel(meta, q0, picks, before, *outs):
    zh = meta[1]
    for d in (1, 2, 3):
        outs[d - 1][:TOK, :] = q0[...]

        @pl.when(zh + d < GROUP)
        def _(d=d):
            outs[d - 1][TOK:, :] = picks[d - 1]

        @pl.when(zh + d >= GROUP)
        def _(d=d):
            outs[d - 1][TOK:, :] = before[d - 1]


def grad_near_kernel(meta, up, up_c, w, acc):
    zl, c = meta[2], meta[3]
    wide = up.shape[1]
    here = pl.multiple_of((2 * zl + c) * wide, wide)
    beside = pl.multiple_of((2 * zl + 1 - c) * wide, wide)
    acc[...] = nt(up[...], w[:, pl.ds(here, wide)]) + nt(
        up_c[...], w[:, pl.ds(beside, wide)]
    )


def grad_far_kernel(meta, up_z, up_zc, w, acc, g, g0):
    zl, c = 1 - meta[2], meta[3]
    wide = up_z.shape[1]
    here = pl.multiple_of((2 * zl + c) * wide, wide)
    beside = pl.multiple_of((2 * zl + 1 - c) * wide, wide)
    full = acc[...] + nt(up_z[...], w[:, pl.ds(here, wide)])
    full = (full + nt(up_zc[...], w[:, pl.ds(beside, wide)])).astype(BF)
    g[...] = full
    g0[...] = full[:, :HEAD]


def fold8(a, how):
    return how(a.reshape(a.shape[0] // 8, 8, a.shape[1]), axis=0)


def causal_t():
    return iota((TOK, TOK), 0) <= iota((TOK, TOK), 1)


def block_masks(row, zh):
    slot = iota((1, ALL), 1) // TOK
    edge = jnp.where(slot > zh, 0.0, NEG)
    none = jnp.full((1, ALL), NEG, F32)
    return [
        jnp.where(jnp.full((1, ALL), b, jnp.int32) < row, 0.0,
                  jnp.where(jnp.full((1, ALL), b, jnp.int32) == row, edge, none))
        for b in range(ROWS)
    ]


def split3(a):
    hi = a.astype(BF).astype(F32)
    mid = (a - hi).astype(BF).astype(F32)
    return [hi, mid, (a - hi - mid).astype(BF).astype(F32)]


def halves(a):
    return jnp.concatenate([a[:, :HEAD], a[:, HEAD:]], 0)


def whole(a):
    n = a.shape[0] // 2
    return jnp.concatenate([a[:n], a[n:]], 1)


def forward_kernel(
    meta, q0, q1, q2, q3, g0, g1, g2, g3, kva, kv0, far, ob, s_ref
):
    row, zh = meta[0], meta[1]
    q = jnp.concatenate([q0[...], q1[:TOK], q2[:TOK], q3[:TOK]], 0)
    g = jnp.concatenate([g0[...], g1[...], g2[...], g3[...]], 0)
    masks = block_masks(row, zh)
    per = TILE // SUMM
    top = jnp.full((8, ALL), NEG, F32)
    for j in range(KEYS // TILE):
        s = nt(kva[j * TILE : (j + 1) * TILE, :HEAD], q)
        s_ref[j * TILE : (j + 1) * TILE, :] = s
        for i in range(per):
            most = fold8(s[i * SUMM : (i + 1) * SUMM], jnp.max)
            top = jnp.maximum(top, most + masks[per * j + i])
    top = jnp.max(top, axis=0, keepdims=True) * SCALE2
    sums = jnp.zeros((8, ALL), F32)
    dots = jnp.zeros((8, ALL), F32)
    out = jnp.zeros((HEAD, ALL), F32)
    for j in range(KEYS // TILE):
        at = slice(j * TILE, (j + 1) * TILE)
        value = kva[at, HEAD:]
        parts = []
        for i in range(per):
            b = per * j + i
            shift = jnp.where(masks[b] < 0, -NEG, top)
            parts.append(
                jnp.exp2(s_ref[b * SUMM : (b + 1) * SUMM, :] * SCALE2 - shift)
            )
        e = jnp.concatenate(parts, 0)
        sums = sums + fold8(e, jnp.sum)
        dots = dots + fold8(e * nt(value, g), jnp.sum)
        out = out + tn(value, e.astype(BF))
    sums = jnp.sum(sums, axis=0, keepdims=True)
    dots = jnp.sum(dots, axis=0, keepdims=True)
    some = sums > 0
    safe = jnp.where(some, sums, 1.0)
    inv = 1.0 / safe
    log_sum = jnp.where(some, top + jnp.log(safe) * LOG2E, NEG)
    dots = dots * inv
    out = out * inv

    key, value = kv0[:, :HEAD], kv0[:, HEAD:]
    s = jnp.where(causal_t(), nt(key, q0[...]) * SCALE2, NEG)
    own_top = jnp.max(s, axis=0, keepdims=True)
    e = jnp.exp2(s - own_top)
    own_sum = jnp.sum(e, axis=0, keepdims=True)
    own_dot = jnp.sum(e * nt(value, g0[...]), axis=0, keepdims=True)
    own_out = tn(value, e.astype(BF))
    own_log = own_top + jnp.log(own_sum) * LOG2E
    near = log_sum[:, :TOK]
    most = jnp.maximum(near, own_log)
    wa, wb = jnp.exp2(near - most), jnp.exp2(own_log - most)
    inv = 1.0 / (wa + wb)
    wa, wb = wa * inv, wb * inv / own_sum
    log_sum = jnp.concatenate(
        [most - jnp.log(inv) * LOG2E, log_sum[:, TOK:]], 1
    )
    dots = jnp.concatenate(
        [wa * dots[:, :TOK] + wb * own_dot, dots[:, TOK:]], 1
    )

    stats = jnp.concatenate(
        split3(log_sum) + split3(dots) + [jnp.zeros((2, ALL), F32)], 0
    )
    stats = jnp.concatenate(
        [stats[:, i * HEAD : (i + 1) * HEAD] for i in range(ALL // HEAD)], 0
    ).astype(BF)
    for d in range(GROUP):
        part = out[:, d * TOK : (d + 1) * TOK]
        if d == 0:
            part = wa * part + wb * own_out
        to = lax.rem(zh - d + GROUP, GROUP)
        ob[to, :TOK, :] = halves(part).astype(BF)
        ob[to, TOK : TOK + STAT, :] = stats
        ob[to, TOK + STAT :, :] = far[(d + 3) % 4]


def combine_kernel(meta, oa, o, stat):
    zh = meta[1]
    got = []
    for f in range(GROUP):
        rows = oa[lax.rem(zh - f + GROUP, GROUP), TOK : TOK + STAT, :].astype(F32)
        got.append(
            jnp.concatenate([rows[8 * i : 8 * i + 8] for i in range(STAT // 8)], 1)
        )
    for d in range(GROUP):
        logs, dots = [], []
        for f in range(GROUP):
            e = (d - f) % GROUP
            part = got[f][:, e * TOK : (e + 1) * TOK]
            logs.append(part[0:1] + part[1:2] + part[2:3])
            dots.append(part[3:4] + part[4:5] + part[5:6])
        most = functools.reduce(jnp.maximum, logs)
        shares = [jnp.exp2(x - most) for x in logs]
        both = functools.reduce(jnp.add, shares)
        shares = [x / both for x in shares]
        at = slice(d * TOK, (d + 1) * TOK)
        stat[0:1, at] = most + jnp.log(both) * LOG2E
        stat[1:2, at] = functools.reduce(
            jnp.add, [x * y for x, y in zip(shares, dots)]
        )
        if d == 0:
            full = functools.reduce(
                jnp.add,
                [
                    shares[f]
                    * whole(oa[lax.rem(zh - f + GROUP, GROUP), :TOK, :].astype(F32))
                    for f in range(GROUP)
                ],
            )
            eye = ones_where(iota((HEAD, HEAD), 0) == iota((HEAD, HEAD), 1))
            o[...] = tn(full.astype(BF), eye).astype(BF)
    stat[2:8, :] = jnp.zeros((6, ALL), F32)


def backward_kernel(
    meta, q0, q1, q2, q3, g0, g1, g2, g3, kva, kv0, stat, dkv, own, dq0, dq1, dq2, dq3
):
    row, zh = meta[0], meta[1]
    q = jnp.concatenate([q0[...], q1[:TOK], q2[:TOK], q3[:TOK]], 0)
    g = jnp.concatenate([g0[...], g1[...], g2[...], g3[...]], 0)
    masks = block_masks(row, zh)
    log_sum, dot = stat[0:1, :], stat[1:2, :]
    per = TILE // SUMM
    dq = jnp.zeros((HEAD, ALL), F32)
    for j in range(KEYS // TILE):
        at = slice(j * TILE, (j + 1) * TILE)
        key, value = kva[at, :HEAD], kva[at, HEAD:]
        s = nt(key, q)
        parts = []
        for i in range(per):
            shift = jnp.where(masks[per * j + i] < 0, -NEG, log_sum)
            parts.append(
                jnp.exp2(s[i * SUMM : (i + 1) * SUMM] * SCALE2 - shift)
            )
        p = jnp.concatenate(parts, 0)
        dkv[at, HEAD:] = nn(p.astype(BF), g).astype(BF)
        ds = (p * (nt(value, g) - dot)).astype(BF)
        dkv[at, :HEAD] = (nn(ds, q) * SCALE).astype(BF)
        dq = dq + tn(key, ds)
    key, value = kv0[:, :HEAD], kv0[:, HEAD:]
    s = jnp.where(causal_t(), nt(key, q0[...]) * SCALE2, NEG)
    p = jnp.exp2(s - log_sum[:, :TOK])
    own[:, HEAD:] = nn(p.astype(BF), g0[...])
    ds = (p * (nt(value, g0[...]) - dot[:, :TOK])).astype(BF)
    own[:, :HEAD] = nn(ds, q0[...]) * SCALE
    dq0[...] = (dq[:, :TOK] + tn(key, ds)) * SCALE
    for d, ref in ((1, dq1), (2, dq2), (3, dq3)):
        ref[...] = (halves(dq[:, d * TOK : (d + 1) * TOK]) * SCALE).astype(BF)


def strided_kernel(meta, q, k, v, g, f1, f2, f3, before, o, dq, dkv, far):
    row, zh = meta[0], meta[1]
    slot = iota((TOK, 4 * REACH), 1) // REACH
    far_ok = (slot < zh) | (jnp.full((TOK, 4 * REACH), row, jnp.int32) > 0)
    near_ok = iota((TOK, TOK), 0) >= iota((TOK, TOK), 1)

    def far_rows(i):
        at = slice(TOK + i * REACH, TOK + (i + 1) * REACH)
        last = before[3, i * REACH : (i + 1) * REACH, :]
        return jnp.concatenate([f1[at], f2[at], f3[at], last], 0)

    for h in range(3):
        at = slice((h + 1) * HEAD, (h + 2) * HEAD)
        to = slice(h * HEAD, (h + 1) * HEAD)
        qh, kh, vh, gh = q[:, at], k[:, at], v[:, at], g[:, at]
        kf, vf = far_rows(h), far_rows(h + 3)
        s = jnp.where(near_ok, nt(qh, kh) * SCALE, NEG)
        sf = jnp.where(far_ok, nt(qh, kf) * SCALE, NEG)
        top = jnp.maximum(
            jnp.max(s, axis=1, keepdims=True), jnp.max(sf, axis=1, keepdims=True)
        )
        e, ef = jnp.exp(s - top), jnp.exp(sf - top)
        inv = 1.0 / (
            jnp.sum(e, axis=1, keepdims=True) + jnp.sum(ef, axis=1, keepdims=True)
        )
        p, pf = e * inv, ef * inv
        w, wf = p.astype(BF), pf.astype(BF)
        out = (nn(w, vh) + nn(wf, vf)).astype(BF)
        o[:, to] = out
        delta = jnp.sum(gh.astype(F32) * out.astype(F32), axis=1, keepdims=True)
        ds = (p * (nt(gh, vh) - delta) * SCALE).astype(BF)
        dsf = (pf * (nt(gh, vf) - delta) * SCALE).astype(BF)
        dq[:, to] = (nn(ds, kh) + nn(dsf, kf)).astype(BF)
        dkv[:, to] = tn(ds, qh)
        dkv[:, 3 * HEAD + h * HEAD : 3 * HEAD + (h + 1) * HEAD] = tn(w, gh)
        dkf = tn(dsf, qh).astype(BF)
        dvf = tn(wf, gh).astype(BF)
        for u in range(4):
            rows = slice(u * REACH, (u + 1) * REACH)
            far[u, h * REACH : (h + 1) * REACH, :] = dkf[rows]
            far[u, (h + 3) * REACH : (h + 4) * REACH, :] = dvf[rows]


def project_strided_kernel(meta, o, o_c, w, w_c, acc, wa, wb, sems):
    zl, c = meta[2], meta[3]
    wide = wa.shape[2]
    copies = []
    for i, z in enumerate((zl, 1 - zl)):
        at = pl.ds(pl.multiple_of((2 * z + c) * wide, wide), wide)
        rows = pl.ds(HEAD, 3 * HEAD)
        copies.append(
            (
                pltpu.make_async_copy(w.at[rows, at], wa.at[i], sems.at[2 * i]),
                pltpu.make_async_copy(w_c.at[rows, at], wb.at[i], sems.at[2 * i + 1]),
            )
        )
    for pair in copies:
        for copy in pair:
            copy.start()
    for i, pair in enumerate(copies):
        for copy in pair:
            copy.wait()
        acc[i] = nn(o[...], wa[i]) + nn(o_c[...], wb[i])


def project_fixed_kernel(meta, o, o_c, w, w_c, acc, keep, send, wa, wb, sems):
    zl, c = meta[2], meta[3]
    wide = wa.shape[2]
    copies = []
    for i, z in enumerate((zl, 1 - zl)):
        at = pl.ds(pl.multiple_of((2 * z + c) * wide, wide), wide)
        rows = pl.ds(0, HEAD)
        copies.append(
            (
                pltpu.make_async_copy(w.at[rows, at], wa.at[i], sems.at[2 * i]),
                pltpu.make_async_copy(w_c.at[rows, at], wb.at[i], sems.at[2 * i + 1]),
            )
        )
    for pair in copies:
        for copy in pair:
            copy.start()
    for i, ref in ((1, send), (0, keep)):
        for copy in copies[i]:
            copy.wait()
        total = acc[i] + nn(o[...], wa[i]) + nn(o_c[...], wb[i])
        ref[...] = total.astype(ref.dtype)


def final_kernel(
    meta,
    soff_t,
    sidx,
    dkv,
    own,
    dq0,
    dq1,
    dq2,
    dq3,
    oa,
    after,
    strided_dq,
    strided,
    keep,
    over,
    out,
    qg,
    kg,
    vg,
):
    zh = meta[1]
    shard = GROUP * meta[0] + meta[1]
    out[...] = (keep[...] + over[...].astype(F32)).astype(BF)
    pick = summary_select(sidx[...])
    fixed = own[...] + nn(jnp.concatenate([pick] * ROWS, 1), dkv[...])
    kg[:, :HEAD] = fixed[:, :HEAD].astype(BF)
    vg[:, :HEAD] = fixed[:, HEAD:].astype(BF)
    fixed = dq0[...]
    for ref in (dq1, dq2, dq3):
        fixed = fixed + whole(ref[...].astype(F32))
    eye = ones_where(iota((HEAD, HEAD), 0) == iota((HEAD, HEAD), 1))
    qg[:, :HEAD] = tn(fixed.astype(BF), eye).astype(BF)
    qg[:, HEAD:] = strided_dq[...]
    sel = stride_select(soff_t[...], shard)
    slots = []
    for u in range(4):
        t = lax.rem(zh + 1 + u, GROUP)
        here = oa[t, TOK + STAT :, :].astype(F32)
        there = after[t].astype(F32)
        block = jnp.where(zh + 1 + u < GROUP, here, there).astype(BF)
        slots.append(
            jnp.concatenate(
                [block[h * REACH : (h + 1) * REACH] for h in range(6)], 1
            )
        )
    total = strided[...] + tn(sel, jnp.concatenate(slots, 0))
    kg[:, HEAD:] = total[:, : 3 * HEAD].astype(BF)
    vg[:, HEAD:] = total[:, 3 * HEAD :].astype(BF)


def swap(a, axis):
    return lax.ppermute(a, axis, [(0, 1), (1, 0)])


def turn(a, by):
    return lax.ppermute(a, "zh", [(i, (i + by) % GROUP) for i in range(GROUP)])


def dma(n):
    return pltpu.SemaphoreType.DMA((n,))


def shards(queries, key_rows, value_rows, out_weight, upstream, summary_index, soff):
    row = lax.axis_index(("x", "y"))
    zh, zl, c = lax.axis_index("zh"), lax.axis_index("zl"), lax.axis_index("c")
    meta = jnp.stack([row, zh, zl, c]).astype(jnp.int32)
    soff_t = soff.T
    width = queries.shape[1]
    quarter = upstream.shape[1]
    plane = ("x", "y")
    matmul = 2 * ALL * KEYS * HEAD
    half_grad = 2 * TOK * 2 * quarter * width

    up_z = swap(upstream, "zl")
    up_c = swap(upstream, "c")
    kvb, q0, kv0, picks = call(
        prep_kernel,
        [
            sds((ROWS, SUMM, 2 * HEAD)),
            sds((TOK, HEAD)),
            sds((TOK, 2 * HEAD)),
            sds((4, FAR, HEAD)),
        ],
        [meta, soff_t, summary_index, queries, key_rows, value_rows],
        10**8,
        [
            pltpu.VMEM((TOK, width), BF),
            pltpu.VMEM((TOK, width), BF),
            pltpu.VMEM((1, SUMM), jnp.int32),
            pltpu.VMEM((4, ROWS * GROUP), jnp.int32),
            dma(5),
        ],
        name="pick_rows",
        specs=[SM] + [ANY] * 5,
    )
    before = lax.ppermute(picks, plane, [(i, i + 1) for i in range(ROWS - 1)])
    kva = lax.all_to_all(kvb, plane, 0, 0, tiled=True).reshape(KEYS, 2 * HEAD)
    sent = call(
        bundle_kernel,
        [sds((TOK + FAR, HEAD))] * 3,
        [meta, q0, picks, before],
        10**5,
        name="bundle_queries",
    )
    qs = [q0] + [turn(sent[d - 1], d) for d in (1, 2, 3)]
    (acc,) = call(
        grad_near_kernel,
        [sds((TOK, width), F32)],
        [meta, upstream, up_c, out_weight],
        half_grad,
        name="attention_grad_near",
    )
    up_zc = swap(up_z, "c")
    g, g0 = call(
        grad_far_kernel,
        [sds((TOK, width)), sds((TOK, HEAD))],
        [meta, up_z, up_zc, out_weight, acc],
        half_grad,
        name="attention_grad_far",
    )
    gs = [g0] + [turn(g0, d) for d in (1, 2, 3)]
    o_s, dq_s, dkv_s, far = call(
        strided_kernel,
        [
            sds((TOK, 3 * HEAD)),
            sds((TOK, 3 * HEAD)),
            sds((TOK, 6 * HEAD), F32),
            sds((4, FAR, HEAD)),
        ],
        [meta, queries, key_rows, value_rows, g, *qs[1:], before],
        3 * 6 * 2 * TOK * 320 * HEAD,
        name="strided_heads",
    )
    late_weight, _ = lax.optimization_barrier((out_weight, g0))
    weight_c = swap(late_weight, "c")
    o_sc = swap(o_s, "c")
    (ob,) = call(
        forward_kernel,
        [sds((GROUP, TOK + STAT + FAR, HEAD))],
        [meta, *qs, *gs, kva, kv0, far],
        3 * matmul,
        [pltpu.VMEM((KEYS, ALL), F32)],
        name="fixed_forward",
    )
    oa = lax.all_to_all(ob, "zh", 0, 0, tiled=True)
    (acc_out,) = call(
        project_strided_kernel,
        [sds((2, TOK, quarter), F32)],
        [meta, o_s, o_sc, out_weight, weight_c],
        2 * TOK * 6 * HEAD * 2 * quarter,
        [
            pltpu.VMEM((2, 3 * HEAD, quarter), BF),
            pltpu.VMEM((2, 3 * HEAD, quarter), BF),
            dma(4),
        ],
        name="project_strided",
        specs=[SM, VM, VM, ANY, ANY],
    )
    o_f, stat = call(
        combine_kernel,
        [sds((TOK, HEAD)), sds((8, ALL), F32)],
        [meta, oa],
        10**6,
        name="combine",
    )
    o_fc = swap(o_f, "c")
    after = lax.ppermute(
        oa[:, TOK + STAT :, :], plane, [(i + 1, i) for i in range(ROWS - 1)]
    )
    dkv, own, dq0, *dqs = call(
        backward_kernel,
        [
            sds((KEYS, 2 * HEAD)),
            sds((TOK, 2 * HEAD), F32),
            sds((HEAD, TOK), F32),
        ]
        + [sds((TOK, HEAD))] * 3,
        [meta, *qs, *gs, kva, kv0, stat],
        5 * matmul,
        name="fixed_backward",
    )
    dkva = lax.all_to_all(
        dkv.reshape(ROWS, SUMM, 2 * HEAD), plane, 0, 0, tiled=True
    ).reshape(KEYS, 2 * HEAD)
    dqs = [turn(dqs[d - 1], -d) for d in (1, 2, 3)]
    keep, send = call(
        project_fixed_kernel,
        [sds((TOK, quarter), F32), sds((TOK, quarter))],
        [meta, o_f, o_fc, out_weight, weight_c, acc_out],
        2 * TOK * 2 * HEAD * 2 * quarter,
        [
            pltpu.VMEM((2, HEAD, quarter), BF),
            pltpu.VMEM((2, HEAD, quarter), BF),
            dma(4),
        ],
        name="project_fixed",
        specs=[SM, VM, VM, ANY, ANY, VM],
    )
    over = swap(send, "zl")
    return call(
        final_kernel,
        [sds((TOK, quarter))] + [sds((TOK, width))] * 3,
        [meta, soff_t, summary_index, dkva, own, dq0, *dqs, oa, after, dq_s, dkv_s]
        + [keep, over],
        3 * 10**8,
        name="join_results",
    )


def solution(mesh):
    grid = Mesh(mesh.devices.reshape(4, 4, 4, 2, 2), ("x", "y", "zh", "zl", "c"))
    ctx, head = ("x", "y", "zh"), ("zl", "c")
    return jax.shard_map(
        shards,
        mesh=grid,
        in_specs=(
            P(ctx, head),
            P(ctx, head),
            P(ctx, head),
            P(head, None),
            P(ctx, head),
            P(ctx, None),
            P(),
        ),
        out_specs=(P(ctx, head),) * 4,
        check_vma=False,
    )
```

```python
import functools

import jax
import jax.numpy as jnp
from jax import lax
from jax.experimental import pallas as pl
from jax.experimental.pallas import tpu as pltpu
from jax.sharding import Mesh
from jax.sharding import PartitionSpec as P

HEAD = 128
TOK = 256
SUMM = 128
STRIDE = 16
REACH = TOK // STRIDE
ROWS = 16
GROUP = 4
ALL = GROUP * TOK
KEYS = ROWS * SUMM
TILE = 256
STAT = 64
FAR = 6 * REACH
SCALE = HEAD ** (-0.5)
LOG2E = 1.4426950408889634
SCALE2 = SCALE * LOG2E
NEG = -1e30
F32 = jnp.float32
BF = jnp.bfloat16

VM = pl.BlockSpec(memory_space=pltpu.VMEM)
SM = pl.BlockSpec(memory_space=pltpu.SMEM)


def nn(a, b):
    return lax.dot_general(a, b, (((1,), (0,)), ((), ())), preferred_element_type=F32)


def nt(a, b):
    return lax.dot_general(a, b, (((1,), (1,)), ((), ())), preferred_element_type=F32)


def tn(a, b):
    return lax.dot_general(a, b, (((0,), (0,)), ((), ())), preferred_element_type=F32)


def iota(shape, dim):
    return lax.broadcasted_iota(jnp.int32, shape, dim)


def ones_where(condition):
    return condition.astype(F32).astype(BF)


def summary_select(sidx):
    return ones_where(iota((TOK, SUMM), 0) == sidx)


def stride_select(soff_t, shard):
    there = jnp.minimum(shard + 1 + iota((4, ROWS * GROUP), 0), ROWS * GROUP - 1)
    offset = jnp.where(iota((4, ROWS * GROUP), 1) == there, soff_t, 0)
    offset = jnp.sum(offset.astype(F32), axis=1, keepdims=True).astype(jnp.int32)
    row, col = iota((4 * REACH, TOK), 0), iota((4 * REACH, TOK), 1)
    slot = row // REACH
    want = (row % REACH) * STRIDE
    for u in range(4):
        want = want + jnp.where(slot == u, offset[u : u + 1], 0)
    return ones_where(want == col)


def call(kernel, outs, ins, scratch=(), name=None, vmem=24, fetch=(), raw=(), store=()):
    fetch, raw, store = sorted(fetch), set(raw), sorted(store)
    n_in, n_out, n_own = len(ins), len(outs), len(scratch)
    hbm = pl.BlockSpec(memory_space=pltpu.HBM)

    def body(*refs):
        given = list(refs[:n_in])
        made = list(refs[n_in : n_in + n_out])
        own = list(refs[n_in + n_out : n_in + n_out + n_own])
        rest = list(refs[n_in + n_out + n_own :])
        here = rest[: len(fetch)]
        there = rest[len(fetch) : len(fetch) + len(store)]
        sems = rest[-1] if fetch or store else None
        copies = []
        for n, (i, ref) in enumerate(zip(fetch, here)):
            copies.append(pltpu.make_async_copy(given[i], ref, sems.at[n]))
            given[i] = ref
        for copy in copies:
            copy.start()
        for copy in copies:
            copy.wait()
        copies = []
        for n, (i, ref) in enumerate(zip(store, there)):
            copies.append(
                pltpu.make_async_copy(ref, made[i], sems.at[len(fetch) + n])
            )
            made[i] = ref
        kernel(*given, *made, *own)
        for copy in copies:
            copy.start()
        for copy in copies:
            copy.wait()

    extra = [pltpu.VMEM(ins[i].shape, ins[i].dtype) for i in fetch]
    extra += [pltpu.VMEM(outs[i].shape, outs[i].dtype) for i in store]
    if extra:
        extra.append(dma(len(extra)))
    return pl.pallas_call(
        body,
        out_shape=tuple(
            pltpu.HBM(s.shape, s.dtype) if i in store else s
            for i, s in enumerate(outs)
        ),
        in_specs=[SM]
        + [hbm if i in fetch or i in raw else VM for i in range(1, n_in)],
        out_specs=tuple(hbm if i in store else VM for i in range(n_out)),
        scratch_shapes=list(scratch) + extra,
        compiler_params=pltpu.CompilerParams(vmem_limit_bytes=vmem * 2**20),
        cost_estimate=pl.CostEstimate(flops=1, bytes_accessed=1, transcendentals=0),
        name=name,
    )(
        *(
            pltpu.with_memory_space_constraint(x, pltpu.HBM)
            if i in fetch or i in raw
            else x
            for i, x in enumerate(ins)
        )
    )


def sds(shape, dtype=BF):
    return jax.ShapeDtypeStruct(shape, dtype)


def prep_kernel(
    meta, soff_t, sidx, q, k, v, kvb, q0, picks, q0_own, kv0, picks_own
):
    q0[...] = q[:, :HEAD]
    q0_own[...] = q[:, :HEAD]
    pick = summary_select(sidx[...])
    kv = jnp.concatenate([k[:, :HEAD], v[:, :HEAD]], 1)
    kv0[...] = kv
    kv = tn(pick, kv).astype(BF)
    for i in range(ROWS):
        kvb[i] = kv
    sel = stride_select(soff_t[...], GROUP * meta[0] + meta[1])
    got = nn(sel, jnp.concatenate([k[:, HEAD:], v[:, HEAD:]], 1)).astype(BF)
    for u in range(4):
        for h in range(6):
            part = got[u * REACH : (u + 1) * REACH, h * HEAD : (h + 1) * HEAD]
            picks[u, h * REACH : (h + 1) * REACH, :] = part
            picks_own[u, h * REACH : (h + 1) * REACH, :] = part


def grad_near_kernel(meta, up, up_c, w, order, acc, far_w, near_w, sems):
    zl, c = meta[2], meta[3]
    wide = up.shape[1]
    copies = []
    for i, (z, core) in enumerate(
        ((zl, c), (zl, 1 - c), (1 - zl, c), (1 - zl, 1 - c))
    ):
        at = pl.ds(pl.multiple_of((2 * z + core) * wide, wide), wide)
        to = near_w.at[i] if i < 2 else far_w.at[i - 2]
        copies.append(pltpu.make_async_copy(w.at[:, at], to, sems.at[i]))
    for copy in copies:
        copy.start()
    copies[0].wait()
    total = nt(up[...], near_w[0])
    copies[1].wait()
    acc[...] = total + nt(up_c[...], near_w[1])
    copies[2].wait()
    copies[3].wait()


def grad_far_kernel(meta, up_z, up_zc, far_w, acc, picks, before, g, last, *sent):
    zh = meta[1]
    full = acc[...] + nt(up_z[...], far_w[0])
    full = (full + nt(up_zc[...], far_w[1])).astype(BF)
    g[...] = full
    last[...] = before[3]
    for d in (1, 2, 3):
        ref = sent[d - 1]
        ref[:TOK, :] = full[:, :HEAD]

        @pl.when(zh + d < GROUP)
        def _(d=d, ref=ref):
            ref[TOK:, :] = picks[d - 1]

        @pl.when(zh + d >= GROUP)
        def _(d=d, ref=ref):
            ref[TOK:, :] = before[d - 1]


def fold8(a, how):
    return how(a.reshape(a.shape[0] // 8, 8, a.shape[1]), axis=0)


def causal_t():
    return iota((TOK, TOK), 0) <= iota((TOK, TOK), 1)


def block_masks(row, zh):
    slot = iota((1, ALL), 1) // TOK
    edge = jnp.where(slot > zh, 0.0, NEG)
    none = jnp.full((1, ALL), NEG, F32)
    return [
        jnp.where(jnp.full((1, ALL), b, jnp.int32) < row, 0.0,
                  jnp.where(jnp.full((1, ALL), b, jnp.int32) == row, edge, none))
        for b in range(ROWS)
    ]


def split3(a):
    hi = a.astype(BF).astype(F32)
    mid = (a - hi).astype(BF).astype(F32)
    return [hi, mid, (a - hi - mid).astype(BF).astype(F32)]


def halves(a):
    return jnp.concatenate([a[:, :HEAD], a[:, HEAD:]], 0)


def whole(a):
    n = a.shape[0] // 2
    return jnp.concatenate([a[:n], a[n:]], 1)


def forward_kernel(
    meta, q0, q1, q2, q3, g0, g1, g2, g3, kva, kv0, ob, q_all, g_all, kv_all, near, s_ref
):
    row, zh = meta[0], meta[1]
    q = jnp.concatenate([q0[...], q1[...], q2[...], q3[...]], 0)
    g = jnp.concatenate([g0[:, :HEAD], g1[:TOK], g2[:TOK], g3[:TOK]], 0)
    q_all[...] = q
    g_all[...] = g
    for d, ref in ((1, g1), (2, g2), (3, g3)):
        near[d - 1] = ref[TOK:]
    masks = block_masks(row, zh)
    per = TILE // SUMM
    top = jnp.full((8, ALL), NEG, F32)
    for j in range(KEYS // TILE):
        s = nt(kva[j * TILE : (j + 1) * TILE, :HEAD], q)
        kv_all[j * TILE : (j + 1) * TILE, :] = kva[j * TILE : (j + 1) * TILE, :]
        s_ref[j * TILE : (j + 1) * TILE, :] = s
        for i in range(per):
            most = fold8(s[i * SUMM : (i + 1) * SUMM], jnp.max)
            top = jnp.maximum(top, most + masks[per * j + i])
    top = jnp.max(top, axis=0, keepdims=True) * SCALE2
    sums = jnp.zeros((8, ALL), F32)
    dots = jnp.zeros((8, ALL), F32)
    out = jnp.zeros((HEAD, ALL), F32)
    for j in range(KEYS // TILE):
        at = slice(j * TILE, (j + 1) * TILE)
        value = kva[at, HEAD:]
        parts = []
        for i in range(per):
            b = per * j + i
            shift = jnp.where(masks[b] < 0, -NEG, top)
            parts.append(
                jnp.exp2(s_ref[b * SUMM : (b + 1) * SUMM, :] * SCALE2 - shift)
            )
        e = jnp.concatenate(parts, 0)
        sums = sums + fold8(e, jnp.sum)
        dots = dots + fold8(e * nt(value, g), jnp.sum)
        out = out + tn(value, e.astype(BF))
    sums = jnp.sum(sums, axis=0, keepdims=True)
    dots = jnp.sum(dots, axis=0, keepdims=True)
    some = sums > 0
    safe = jnp.where(some, sums, 1.0)
    inv = 1.0 / safe
    log_sum = jnp.where(some, top + jnp.log(safe) * LOG2E, NEG)
    dots = dots * inv
    out = out * inv

    key, value = kv0[:, :HEAD], kv0[:, HEAD:]
    s = jnp.where(causal_t(), nt(key, q0[...]) * SCALE2, NEG)
    own_top = jnp.max(s, axis=0, keepdims=True)
    e = jnp.exp2(s - own_top)
    own_sum = jnp.sum(e, axis=0, keepdims=True)
    own_dot = jnp.sum(e * nt(value, g0[:, :HEAD]), axis=0, keepdims=True)
    own_out = tn(value, e.astype(BF))
    own_log = own_top + jnp.log(own_sum) * LOG2E
    near = log_sum[:, :TOK]
    most = jnp.maximum(near, own_log)
    wa, wb = jnp.exp2(near - most), jnp.exp2(own_log - most)
    inv = 1.0 / (wa + wb)
    wa, wb = wa * inv, wb * inv / own_sum
    log_sum = jnp.concatenate(
        [most - jnp.log(inv) * LOG2E, log_sum[:, TOK:]], 1
    )
    dots = jnp.concatenate(
        [wa * dots[:, :TOK] + wb * own_dot, dots[:, TOK:]], 1
    )

    stats = jnp.concatenate(
        split3(log_sum) + split3(dots) + [jnp.zeros((2, ALL), F32)], 0
    )
    stats = jnp.concatenate(
        [stats[:, i * HEAD : (i + 1) * HEAD] for i in range(ALL // HEAD)], 0
    ).astype(BF)
    for d in range(GROUP):
        part = out[:, d * TOK : (d + 1) * TOK]
        if d == 0:
            part = wa * part + wb * own_out
        to = lax.rem(zh - d + GROUP, GROUP)
        ob[to, :TOK, :] = halves(part).astype(BF)
        ob[to, TOK:, :] = stats


def combine_kernel(meta, oa, o_sc, o, stat, o_own, o_beside):
    o_beside[...] = o_sc[...]
    zh = meta[1]
    got = []
    for f in range(GROUP):
        rows = oa[lax.rem(zh - f + GROUP, GROUP), TOK:, :].astype(F32)
        got.append(
            jnp.concatenate([rows[8 * i : 8 * i + 8] for i in range(STAT // 8)], 1)
        )
    for d in range(GROUP):
        logs, dots = [], []
        for f in range(GROUP):
            e = (d - f) % GROUP
            part = got[f][:, e * TOK : (e + 1) * TOK]
            logs.append(part[0:1] + part[1:2] + part[2:3])
            dots.append(part[3:4] + part[4:5] + part[5:6])
        most = functools.reduce(jnp.maximum, logs)
        shares = [jnp.exp2(x - most) for x in logs]
        both = functools.reduce(jnp.add, shares)
        shares = [x / both for x in shares]
        at = slice(d * TOK, (d + 1) * TOK)
        stat[0:1, at] = most + jnp.log(both) * LOG2E
        stat[1:2, at] = functools.reduce(
            jnp.add, [x * y for x, y in zip(shares, dots)]
        )
        if d == 0:
            full = functools.reduce(
                jnp.add,
                [
                    shares[f]
                    * whole(oa[lax.rem(zh - f + GROUP, GROUP), :TOK, :].astype(F32))
                    for f in range(GROUP)
                ],
            )
            eye = ones_where(iota((HEAD, HEAD), 0) == iota((HEAD, HEAD), 1))
            full = tn(full.astype(BF), eye).astype(BF)
            o[...] = full
            o_own[...] = full
    stat[2:8, :] = jnp.zeros((6, ALL), F32)


def backward_kernel(
    meta, q_all, g_all, kva, kv0, stat, far, dkv, dq1, dq2, dq3, own, dq0
):
    row, zh = meta[0], meta[1]
    q, g = q_all[...], g_all[...]
    q0, g0 = q[:TOK], g[:TOK]
    masks = block_masks(row, zh)
    log_sum, dot = stat[0:1, :], stat[1:2, :]
    per = TILE // SUMM
    dq = jnp.zeros((HEAD, ALL), F32)
    for j in range(KEYS // TILE):
        at = slice(j * TILE, (j + 1) * TILE)
        key, value = kva[at, :HEAD], kva[at, HEAD:]
        s = nt(key, q)
        parts = []
        for i in range(per):
            shift = jnp.where(masks[per * j + i] < 0, -NEG, log_sum)
            parts.append(
                jnp.exp2(s[i * SUMM : (i + 1) * SUMM] * SCALE2 - shift)
            )
        p = jnp.concatenate(parts, 0)
        dkv[at, HEAD:] = nn(p.astype(BF), g).astype(BF)
        ds = (p * (nt(value, g) - dot)).astype(BF)
        dkv[at, :HEAD] = (nn(ds, q) * SCALE).astype(BF)
        dq = dq + tn(key, ds)
    key, value = kv0[:, :HEAD], kv0[:, HEAD:]
    s = jnp.where(causal_t(), nt(key, q0) * SCALE2, NEG)
    p = jnp.exp2(s - log_sum[:, :TOK])
    own[:, HEAD:] = nn(p.astype(BF), g0)
    ds = (p * (nt(value, g0) - dot[:, :TOK])).astype(BF)
    own[:, :HEAD] = nn(ds, q0) * SCALE
    dq0[...] = (dq[:, :TOK] + tn(key, ds)) * SCALE
    for d, ref in ((1, dq1), (2, dq2), (3, dq3)):
        ref[:TOK, :] = (halves(dq[:, d * TOK : (d + 1) * TOK]) * SCALE).astype(BF)
        ref[TOK:, :] = far[d - 1]


def strided_kernel(meta, q, k, v, g, near, last, o, dq, dkv, far, o_own):
    row, zh = meta[0], meta[1]
    slot = iota((TOK, 4 * REACH), 1) // REACH
    far_ok = (slot < zh) | (jnp.full((TOK, 4 * REACH), row, jnp.int32) > 0)
    near_ok = iota((TOK, TOK), 0) >= iota((TOK, TOK), 1)

    def far_rows(i):
        at = slice(i * REACH, (i + 1) * REACH)
        return jnp.concatenate([near[0, at], near[1, at], near[2, at], last[at]], 0)

    for h in range(3):
        at = slice((h + 1) * HEAD, (h + 2) * HEAD)
        to = slice(h * HEAD, (h + 1) * HEAD)
        qh, kh, vh, gh = q[:, at], k[:, at], v[:, at], g[:, at]
        kf, vf = far_rows(h), far_rows(h + 3)
        s = jnp.where(near_ok, nt(qh, kh) * SCALE, NEG)
        sf = jnp.where(far_ok, nt(qh, kf) * SCALE, NEG)
        top = jnp.maximum(
            jnp.max(s, axis=1, keepdims=True), jnp.max(sf, axis=1, keepdims=True)
        )
        e, ef = jnp.exp(s - top), jnp.exp(sf - top)
        inv = 1.0 / (
            jnp.sum(e, axis=1, keepdims=True) + jnp.sum(ef, axis=1, keepdims=True)
        )
        p, pf = e * inv, ef * inv
        w, wf = p.astype(BF), pf.astype(BF)
        out = (nn(w, vh) + nn(wf, vf)).astype(BF)
        o[:, to] = out
        o_own[:, to] = out
        delta = jnp.sum(gh.astype(F32) * out.astype(F32), axis=1, keepdims=True)
        ds = (p * (nt(gh, vh) - delta) * SCALE).astype(BF)
        dsf = (pf * (nt(gh, vf) - delta) * SCALE).astype(BF)
        dq[:, to] = (nn(ds, kh) + nn(dsf, kf)).astype(BF)
        dkv[:, to] = tn(ds, qh)
        dkv[:, 3 * HEAD + h * HEAD : 3 * HEAD + (h + 1) * HEAD] = tn(w, gh)
        dkf = tn(dsf, qh).astype(BF)
        dvf = tn(wf, gh).astype(BF)
        for u in range(4):
            rows = slice(u * REACH, (u + 1) * REACH)
            far[u, h * REACH : (h + 1) * REACH, :] = dkf[rows]
            far[u, (h + 3) * REACH : (h + 4) * REACH, :] = dvf[rows]


def project_kernel(meta, o_f, o_fc, o, o_c, w, w_c, order, send, keep, wa, wb, sems):
    zl, c = meta[2], meta[3]
    wide = wa.shape[2]
    copies = []
    for i, z in enumerate((1 - zl, zl)):
        at = pl.ds(pl.multiple_of((2 * z + c) * wide, wide), wide)
        copies.append(
            (
                pltpu.make_async_copy(w.at[:, at], wa.at[i], sems.at[2 * i]),
                pltpu.make_async_copy(w_c.at[:, at], wb.at[i], sems.at[2 * i + 1]),
            )
        )
    for pair in copies:
        for copy in pair:
            copy.start()
    here = jnp.concatenate([o_f[...], o[...]], 1)
    beside = jnp.concatenate([o_fc[...], o_c[...]], 1)
    for i, ref in ((0, send), (1, keep)):
        copies[i][0].wait()
        total = nn(here, wa[i])
        copies[i][1].wait()
        ref[...] = (total + nn(beside, wb[i])).astype(ref.dtype)


def back_kernel(meta, dq0, b1, b2, b3, far, sent, here, dq):
    for u, ref in ((0, b1), (1, b2), (2, b3)):
        sent[u] = ref[TOK:, :]
        here[u] = ref[TOK:, :]
    sent[3] = far[3]
    total = dq0[...]
    for ref in (b1, b2, b3):
        total = total + whole(ref[:TOK, :].astype(F32))
    eye = ones_where(iota((HEAD, HEAD), 0) == iota((HEAD, HEAD), 1))
    dq[...] = tn(total.astype(BF), eye).astype(BF)


def final_kernel(
    meta,
    soff_t,
    sidx,
    dkv,
    own,
    dq,
    here,
    after,
    strided_dq,
    strided,
    keep,
    over,
    out,
    qg,
    kg,
    vg,
):
    zh = meta[1]
    shard = GROUP * meta[0] + meta[1]
    out[...] = (keep[...].astype(F32) + over[...].astype(F32)).astype(BF)
    pick = summary_select(sidx[...])
    fixed = own[...] + nn(jnp.concatenate([pick] * ROWS, 1), dkv[...])
    kg[:, :HEAD] = fixed[:, :HEAD].astype(BF)
    vg[:, :HEAD] = fixed[:, HEAD:].astype(BF)
    qg[:, :HEAD] = dq[...]
    qg[:, HEAD:] = strided_dq[...]
    sel = stride_select(soff_t[...], shard)
    slots = []
    for u in range(4):
        block = after[u]
        if u < 3:
            block = jnp.where(
                zh + 1 + u < GROUP, here[u].astype(F32), block.astype(F32)
            ).astype(BF)
        slots.append(
            jnp.concatenate(
                [block[h * REACH : (h + 1) * REACH] for h in range(6)], 1
            )
        )
    total = strided[...] + tn(sel, jnp.concatenate(slots, 0))
    kg[:, HEAD:] = total[:, : 3 * HEAD].astype(BF)
    vg[:, HEAD:] = total[:, 3 * HEAD :].astype(BF)


def swap(a, axis):
    return lax.ppermute(a, axis, [(0, 1), (1, 0)])


def turn(a, by):
    return lax.ppermute(a, "zh", [(i, (i + by) % GROUP) for i in range(GROUP)])


def after(a, other):
    return lax.optimization_barrier((a, other))[0]


def dma(n):
    return pltpu.SemaphoreType.DMA((n,))


def shards(queries, key_rows, value_rows, out_weight, upstream, summary_index, soff):
    row = lax.axis_index(("x", "y"))
    zh, zl, c = lax.axis_index("zh"), lax.axis_index("zl"), lax.axis_index("c")
    meta = jnp.stack([row, zh, zl, c]).astype(jnp.int32)
    soff_t = soff.T
    width = queries.shape[1]
    quarter = upstream.shape[1]
    plane = ("x", "y")

    up_z = swap(upstream, "zl")
    up_c = swap(upstream, "c")
    block = sds((4, FAR, HEAD))
    kvb, q0, picks, q0_own, kv0, picks_own = call(
        prep_kernel,
        [
            sds((ROWS, SUMM, 2 * HEAD)),
            sds((TOK, HEAD)),
            block,
            sds((TOK, HEAD)),
            sds((TOK, 2 * HEAD)),
            block,
        ],
        [meta, soff_t, summary_index, queries, key_rows, value_rows],
        name="pick_rows",
        fetch=range(1, 6),
        store=[3, 4, 5],
    )
    kva = lax.all_to_all(kvb, plane, 0, 0, tiled=True).reshape(KEYS, 2 * HEAD)
    before = lax.ppermute(picks, plane, [(i, i + 1) for i in range(ROWS - 1)])
    acc, far_w = call(
        grad_near_kernel,
        [sds((TOK, width), F32), sds((2, width, quarter))],
        [meta, upstream, up_c, out_weight, kv0],
        [pltpu.VMEM((2, width, quarter), BF), dma(4)],
        name="attention_grad_near",
        fetch=[1],
        raw=[3, 4],
    )
    up_zc = swap(after(up_z, kv0), "c")
    qs = [q0_own] + [turn(q0, d) for d in (1, 2, 3)]
    g, last, *gs = call(
        grad_far_kernel,
        [sds((TOK, width)), sds((FAR, HEAD))] + [sds((TOK + FAR, HEAD))] * 3,
        [meta, up_z, up_zc, far_w, acc, picks_own, before],
        name="attention_grad_far",
        fetch=[5],
        store=[0, 1],
    )
    gs = [g] + [turn(gs[d - 1], d) for d in (1, 2, 3)]
    ob, q_all, g_all, kv_all, near = call(
        forward_kernel,
        [
            sds((GROUP, TOK + STAT, HEAD)),
            sds((ALL, HEAD)),
            sds((ALL, HEAD)),
            sds((KEYS, 2 * HEAD)),
            sds((3, FAR, HEAD)),
        ],
        [meta, *qs, *gs, kva, kv0],
        [pltpu.VMEM((KEYS, ALL), F32)],
        name="fixed_forward",
        fetch=[1, 5, 10],
        store=[1, 2, 3, 4],
    )
    weight_c = swap(after(out_weight, near), "c")
    oa = lax.all_to_all(ob, "zh", 0, 0, tiled=True)
    o_s, dq_s, dkv_s, far, o_own = call(
        strided_kernel,
        [
            sds((TOK, 3 * HEAD)),
            sds((TOK, 3 * HEAD)),
            sds((TOK, 6 * HEAD), F32),
            block,
            sds((TOK, 3 * HEAD)),
        ],
        [meta, queries, key_rows, value_rows, g, near, last],
        name="strided_heads",
        fetch=range(1, 7),
        store=[1, 2, 3, 4],
    )
    o_sc = swap(o_s, "c")
    o_f, stat, o_f_own, o_beside = call(
        combine_kernel,
        [
            sds((TOK, HEAD)),
            sds((8, ALL), F32),
            sds((TOK, HEAD)),
            sds((TOK, 3 * HEAD)),
        ],
        [meta, oa, o_sc],
        name="combine",
        store=[2, 3],
    )
    o_fc = swap(o_f, "c")
    dkv, *dqs, own, dq0 = call(
        backward_kernel,
        [sds((KEYS, 2 * HEAD))]
        + [sds((TOK + FAR, HEAD))] * 3
        + [sds((TOK, 2 * HEAD), F32), sds((HEAD, TOK), F32)],
        [meta, q_all, g_all, kv_all, kv0, stat, far],
        name="fixed_backward",
        fetch=[1, 2, 3, 4, 6],
        store=[4, 5],
    )
    dkva = lax.all_to_all(
        after(dkv, o_fc).reshape(ROWS, SUMM, 2 * HEAD), plane, 0, 0, tiled=True
    ).reshape(KEYS, 2 * HEAD)
    send, keep = call(
        project_kernel,
        [sds((TOK, quarter))] * 2,
        [meta, o_f_own, o_fc, o_own, o_beside, out_weight, weight_c, dq0],
        [
            pltpu.VMEM((2, width, quarter), BF),
            pltpu.VMEM((2, width, quarter), BF),
            dma(4),
        ],
        name="project",
        fetch=[1, 3, 4],
        raw=[5, 6, 7],
        store=[1],
    )
    over = swap(send, "zl")
    dqs = [turn(dqs[d - 1], -d) for d in (1, 2, 3)]
    sent, here, dq_f = call(
        back_kernel,
        [block, sds((3, FAR, HEAD)), sds((TOK, HEAD))],
        [meta, dq0, *dqs, far],
        name="bundle_back",
        fetch=[1, 5],
        store=[1, 2],
    )
    back = lax.ppermute(sent, plane, [(i + 1, i) for i in range(ROWS - 1)])
    return call(
        final_kernel,
        [sds((TOK, quarter))] + [sds((TOK, width))] * 3,
        [meta, soff_t, summary_index, dkva, own, dq_f, here, back, dq_s, dkv_s]
        + [keep, over],
        name="join_results",
        fetch=[1, 2, 4, 5, 6, 8, 9, 10],
    )


def solution(mesh):
    grid = Mesh(mesh.devices.reshape(4, 4, 4, 2, 2), ("x", "y", "zh", "zl", "c"))
    ctx, head = ("x", "y", "zh"), ("zl", "c")
    return jax.shard_map(
        shards,
        mesh=grid,
        in_specs=(
            P(ctx, head),
            P(ctx, head),
            P(ctx, head),
            P(head, None),
            P(ctx, head),
            P(ctx, None),
            P(),
        ),
        out_specs=(P(ctx, head),) * 4,
        check_vma=False,
    )
```

```python
import functools

import jax
import jax.numpy as jnp
from jax import lax
from jax.experimental import pallas as pl
from jax.experimental.pallas import tpu as pltpu
from jax.sharding import Mesh
from jax.sharding import PartitionSpec as P

HEAD = 128
TOK = 256
SUMM = 128
STRIDE = 16
REACH = TOK // STRIDE
ROWS = 16
GROUP = 4
ALL = GROUP * TOK
KEYS = ROWS * SUMM
TILE = 256
STAT = 64
FAR = 6 * REACH
SCALE = HEAD ** (-0.5)
LOG2E = 1.4426950408889634
SCALE2 = SCALE * LOG2E
NEG = -1e30
F32 = jnp.float32
BF = jnp.bfloat16

VM = pl.BlockSpec(memory_space=pltpu.VMEM)
SM = pl.BlockSpec(memory_space=pltpu.SMEM)


def nn(a, b):
    return lax.dot_general(a, b, (((1,), (0,)), ((), ())), preferred_element_type=F32)


def nt(a, b):
    return lax.dot_general(a, b, (((1,), (1,)), ((), ())), preferred_element_type=F32)


def tn(a, b):
    return lax.dot_general(a, b, (((0,), (0,)), ((), ())), preferred_element_type=F32)


def iota(shape, dim):
    return lax.broadcasted_iota(jnp.int32, shape, dim)


def ones_where(condition):
    return condition.astype(F32).astype(BF)


def summary_select(sidx):
    return ones_where(iota((TOK, SUMM), 0) == sidx)


def stride_select(soff_t, shard):
    there = jnp.minimum(shard + 1 + iota((4, ROWS * GROUP), 0), ROWS * GROUP - 1)
    offset = jnp.where(iota((4, ROWS * GROUP), 1) == there, soff_t, 0)
    offset = jnp.sum(offset.astype(F32), axis=1, keepdims=True).astype(jnp.int32)
    row, col = iota((4 * REACH, TOK), 0), iota((4 * REACH, TOK), 1)
    slot = row // REACH
    want = (row % REACH) * STRIDE
    for u in range(4):
        want = want + jnp.where(slot == u, offset[u : u + 1], 0)
    return ones_where(want == col)


def call(
    kernel, outs, ins, scratch=(), name=None, vmem=24, fetch=(), raw=(), store=(),
    direct=(), flops=1,
):
    fetch, raw, store = sorted(fetch), set(raw), sorted(store)
    pinned = set(store) | set(direct)
    n_in, n_out, n_own = len(ins), len(outs), len(scratch)
    hbm = pl.BlockSpec(memory_space=pltpu.HBM)

    def body(*refs):
        given = list(refs[:n_in])
        made = list(refs[n_in : n_in + n_out])
        own = list(refs[n_in + n_out : n_in + n_out + n_own])
        rest = list(refs[n_in + n_out + n_own :])
        here = rest[: len(fetch)]
        there = rest[len(fetch) : len(fetch) + len(store)]
        sems = rest[-1] if fetch or store else None
        copies = []
        for n, (i, ref) in enumerate(zip(fetch, here)):
            copies.append(pltpu.make_async_copy(given[i], ref, sems.at[n]))
            given[i] = ref
        for copy in copies:
            copy.start()
        for copy in copies:
            copy.wait()
        copies = []
        for n, (i, ref) in enumerate(zip(store, there)):
            copies.append(
                pltpu.make_async_copy(ref, made[i], sems.at[len(fetch) + n])
            )
            made[i] = ref
        kernel(*given, *made, *own)
        for copy in copies:
            copy.start()
        for copy in copies:
            copy.wait()

    extra = [pltpu.VMEM(ins[i].shape, ins[i].dtype) for i in fetch]
    extra += [pltpu.VMEM(outs[i].shape, outs[i].dtype) for i in store]
    if extra:
        extra.append(dma(len(extra)))
    return pl.pallas_call(
        body,
        out_shape=tuple(
            pltpu.HBM(s.shape, s.dtype) if i in pinned else s
            for i, s in enumerate(outs)
        ),
        in_specs=[SM]
        + [hbm if i in fetch or i in raw else VM for i in range(1, n_in)],
        out_specs=tuple(hbm if i in pinned else VM for i in range(n_out)),
        scratch_shapes=list(scratch) + extra,
        compiler_params=pltpu.CompilerParams(vmem_limit_bytes=vmem * 2**20),
        cost_estimate=pl.CostEstimate(
            flops=flops, bytes_accessed=1, transcendentals=0
        ),
        name=name,
    )(
        *(
            pltpu.with_memory_space_constraint(x, pltpu.HBM)
            if i in fetch or i in raw
            else x
            for i, x in enumerate(ins)
        )
    )


def sds(shape, dtype=BF):
    return jax.ShapeDtypeStruct(shape, dtype)


def prep_kernel(meta, soff_t, sidx, k, v, q, kvb, q0, picks, sem):
    copy = pltpu.make_async_copy(q.at[:, pl.ds(0, HEAD)], q0, sem.at[0])
    copy.start()
    pick = summary_select(sidx[...])
    kv = tn(pick, jnp.concatenate([k[:, :HEAD], v[:, :HEAD]], 1)).astype(BF)
    for i in range(ROWS):
        kvb[i] = kv
    sel = stride_select(soff_t[...], GROUP * meta[0] + meta[1])
    got = nn(sel, jnp.concatenate([k[:, HEAD:], v[:, HEAD:]], 1)).astype(BF)
    for u in range(4):
        for h in range(6):
            picks[u, h * REACH : (h + 1) * REACH, :] = got[
                u * REACH : (u + 1) * REACH, h * HEAD : (h + 1) * HEAD
            ]
    copy.wait()


def weight_blocks(w, blocks, places, sems):
    wide = blocks.shape[2]
    copies = []
    for i, (z, core) in enumerate(places):
        at = pl.ds(pl.multiple_of((2 * z + core) * wide, wide), wide)
        copies.append(pltpu.make_async_copy(w.at[:, at], blocks.at[i], sems.at[i]))
    for copy in copies:
        copy.start()
    return copies


def grad_near_kernel(meta, up, up_c, w, order, acc, blocks, sems):
    zl, c = meta[2], meta[3]
    copies = weight_blocks(w, blocks, ((zl, c), (zl, 1 - c)), sems)
    copies[0].wait()
    total = nt(up[...], blocks[0])
    copies[1].wait()
    acc[...] = total + nt(up_c[...], blocks[1])


def grad_far_kernel(
    meta, up_z, up_zc, w, acc, picks, before, q0, q1, q2, q3, g, last, q_all, *rest
):
    sent, blocks, sems = rest[:3], rest[3], rest[4]
    zh, zl, c = meta[1], meta[2], meta[3]
    copies = weight_blocks(w, blocks, ((1 - zl, c), (1 - zl, 1 - c)), sems)
    for d, ref in enumerate((q0, q1, q2, q3)):
        q_all[d * TOK : (d + 1) * TOK, :] = ref[...]
    copies[0].wait()
    full = acc[...] + nt(up_z[...], blocks[0])
    copies[1].wait()
    full = (full + nt(up_zc[...], blocks[1])).astype(BF)
    g[...] = full
    last[...] = before[3]
    for d in (1, 2, 3):
        ref = sent[d - 1]
        ref[:TOK, :] = full[:, :HEAD]

        @pl.when(zh + d < GROUP)
        def _(d=d, ref=ref):
            ref[TOK:, :] = picks[d - 1]

        @pl.when(zh + d >= GROUP)
        def _(d=d, ref=ref):
            ref[TOK:, :] = before[d - 1]


def fold8(a, how):
    return how(a.reshape(a.shape[0] // 8, 8, a.shape[1]), axis=0)


def causal_t():
    return iota((TOK, TOK), 0) <= iota((TOK, TOK), 1)


def block_masks(row, zh):
    slot = iota((1, ALL), 1) // TOK
    edge = jnp.where(slot > zh, 0.0, NEG)
    none = jnp.full((1, ALL), NEG, F32)
    return [
        jnp.where(jnp.full((1, ALL), b, jnp.int32) < row, 0.0,
                  jnp.where(jnp.full((1, ALL), b, jnp.int32) == row, edge, none))
        for b in range(ROWS)
    ]


def split3(a):
    hi = a.astype(BF).astype(F32)
    mid = (a - hi).astype(BF).astype(F32)
    return [hi, mid, (a - hi - mid).astype(BF).astype(F32)]


def halves(a):
    return jnp.concatenate([a[:, :HEAD], a[:, HEAD:]], 0)


def whole(a):
    n = a.shape[0] // 2
    return jnp.concatenate([a[:n], a[n:]], 1)


def forward_kernel(
    meta, q_all, g0, g1, g2, g3, kva, k, v, ob, g_all, kv_all, near, s_ref, gs, kv0, sems
):
    row, zh = meta[0], meta[1]
    first = pl.ds(0, HEAD)
    brought = [
        pltpu.make_async_copy(g0.at[:, first], gs.at[pl.ds(0, TOK)], sems.at[0]),
        pltpu.make_async_copy(k.at[:, first], kv0.at[:, first], sems.at[1]),
        pltpu.make_async_copy(
            v.at[:, first], kv0.at[:, pl.ds(HEAD, HEAD)], sems.at[2]
        ),
    ]
    for copy in brought:
        copy.start()
    for d, ref in ((1, g1), (2, g2), (3, g3)):
        gs[d * TOK : (d + 1) * TOK, :] = ref[:TOK, :]
    kept = [pltpu.make_async_copy(kva, kv_all, sems.at[3])]
    for d, ref in ((1, g1), (2, g2), (3, g3)):
        kept.append(
            pltpu.make_async_copy(
                ref.at[pl.ds(TOK, FAR)], near.at[d - 1], sems.at[3 + d]
            )
        )
    for copy in brought:
        copy.wait()
    kept.append(pltpu.make_async_copy(gs, g_all, sems.at[7]))
    for copy in kept:
        copy.start()
    q, g = q_all[...], gs[...]
    q0, g0 = q[:TOK], g[:TOK]
    masks = block_masks(row, zh)
    per = TILE // SUMM
    top = jnp.full((8, ALL), NEG, F32)
    for j in range(KEYS // TILE):
        s = nt(kva[j * TILE : (j + 1) * TILE, :HEAD], q)
        s_ref[j * TILE : (j + 1) * TILE, :] = s
        for i in range(per):
            most = fold8(s[i * SUMM : (i + 1) * SUMM], jnp.max)
            top = jnp.maximum(top, most + masks[per * j + i])
    top = jnp.max(top, axis=0, keepdims=True) * SCALE2
    sums = jnp.zeros((8, ALL), F32)
    dots = jnp.zeros((8, ALL), F32)
    out = jnp.zeros((HEAD, ALL), F32)
    for j in range(KEYS // TILE):
        at = slice(j * TILE, (j + 1) * TILE)
        value = kva[at, HEAD:]
        parts = []
        for i in range(per):
            b = per * j + i
            shift = jnp.where(masks[b] < 0, -NEG, top)
            parts.append(
                jnp.exp2(s_ref[b * SUMM : (b + 1) * SUMM, :] * SCALE2 - shift)
            )
        e = jnp.concatenate(parts, 0)
        sums = sums + fold8(e, jnp.sum)
        dots = dots + fold8(e * nt(value, g), jnp.sum)
        out = out + tn(value, e.astype(BF))
    sums = jnp.sum(sums, axis=0, keepdims=True)
    dots = jnp.sum(dots, axis=0, keepdims=True)
    some = sums > 0
    safe = jnp.where(some, sums, 1.0)
    inv = 1.0 / safe
    log_sum = jnp.where(some, top + jnp.log(safe) * LOG2E, NEG)
    dots = dots * inv
    out = out * inv

    key, value = kv0[:, :HEAD], kv0[:, HEAD:]
    s = jnp.where(causal_t(), nt(key, q0) * SCALE2, NEG)
    own_top = jnp.max(s, axis=0, keepdims=True)
    e = jnp.exp2(s - own_top)
    own_sum = jnp.sum(e, axis=0, keepdims=True)
    own_dot = jnp.sum(e * nt(value, g0), axis=0, keepdims=True)
    own_out = tn(value, e.astype(BF))
    own_log = own_top + jnp.log(own_sum) * LOG2E
    near = log_sum[:, :TOK]
    most = jnp.maximum(near, own_log)
    wa, wb = jnp.exp2(near - most), jnp.exp2(own_log - most)
    inv = 1.0 / (wa + wb)
    wa, wb = wa * inv, wb * inv / own_sum
    log_sum = jnp.concatenate(
        [most - jnp.log(inv) * LOG2E, log_sum[:, TOK:]], 1
    )
    dots = jnp.concatenate(
        [wa * dots[:, :TOK] + wb * own_dot, dots[:, TOK:]], 1
    )

    stats = jnp.concatenate(
        split3(log_sum) + split3(dots) + [jnp.zeros((2, ALL), F32)], 0
    )
    stats = jnp.concatenate(
        [stats[:, i * HEAD : (i + 1) * HEAD] for i in range(ALL // HEAD)], 0
    ).astype(BF)
    for d in range(GROUP):
        part = out[:, d * TOK : (d + 1) * TOK]
        if d == 0:
            part = wa * part + wb * own_out
        to = lax.rem(zh - d + GROUP, GROUP)
        ob[to, :TOK, :] = halves(part).astype(BF)
        ob[to, TOK:, :] = stats
    for copy in kept:
        copy.wait()


def combine_kernel(meta, oa, o_sc, o, stat, o_own, o_beside):
    o_beside[...] = o_sc[...]
    zh = meta[1]
    got = []
    for f in range(GROUP):
        rows = oa[lax.rem(zh - f + GROUP, GROUP), TOK:, :].astype(F32)
        got.append(
            jnp.concatenate([rows[8 * i : 8 * i + 8] for i in range(STAT // 8)], 1)
        )
    for d in range(GROUP):
        logs, dots = [], []
        for f in range(GROUP):
            e = (d - f) % GROUP
            part = got[f][:, e * TOK : (e + 1) * TOK]
            logs.append(part[0:1] + part[1:2] + part[2:3])
            dots.append(part[3:4] + part[4:5] + part[5:6])
        most = functools.reduce(jnp.maximum, logs)
        shares = [jnp.exp2(x - most) for x in logs]
        both = functools.reduce(jnp.add, shares)
        shares = [x / both for x in shares]
        at = slice(d * TOK, (d + 1) * TOK)
        stat[0:1, at] = most + jnp.log(both) * LOG2E
        stat[1:2, at] = functools.reduce(
            jnp.add, [x * y for x, y in zip(shares, dots)]
        )
        if d == 0:
            full = functools.reduce(
                jnp.add,
                [
                    shares[f]
                    * whole(oa[lax.rem(zh - f + GROUP, GROUP), :TOK, :].astype(F32))
                    for f in range(GROUP)
                ],
            )
            eye = ones_where(iota((HEAD, HEAD), 0) == iota((HEAD, HEAD), 1))
            full = tn(full.astype(BF), eye).astype(BF)
            o[...] = full
            o_own[...] = full
    stat[2:8, :] = jnp.zeros((6, ALL), F32)


def backward_kernel(
    meta, q_all, g_all, kv_all, k, v, stat, far, dkv, dq1, dq2, dq3, own, dq0,
    kva, kv0, sems
):
    row, zh = meta[0], meta[1]
    first = pl.ds(0, HEAD)
    half = KEYS // 2
    brought = [
        pltpu.make_async_copy(
            kv_all.at[pl.ds(i * half, half)], kva.at[pl.ds(i * half, half)], sems.at[i]
        )
        for i in range(2)
    ]
    brought += [
        pltpu.make_async_copy(k.at[:, first], kv0.at[:, first], sems.at[2]),
        pltpu.make_async_copy(
            v.at[:, first], kv0.at[:, pl.ds(HEAD, HEAD)], sems.at[3]
        ),
    ]
    for copy in brought:
        copy.start()
    brought[0].wait()
    q, g = q_all[...], g_all[...]
    q0, g0 = q[:TOK], g[:TOK]
    masks = block_masks(row, zh)
    log_sum, dot = stat[0:1, :], stat[1:2, :]
    per = TILE // SUMM
    dq = jnp.zeros((HEAD, ALL), F32)
    for j in range(KEYS // TILE):
        if j * TILE == half:
            brought[1].wait()
        at = slice(j * TILE, (j + 1) * TILE)
        key, value = kva[at, :HEAD], kva[at, HEAD:]
        s = nt(key, q)
        parts = []
        for i in range(per):
            shift = jnp.where(masks[per * j + i] < 0, -NEG, log_sum)
            parts.append(
                jnp.exp2(s[i * SUMM : (i + 1) * SUMM] * SCALE2 - shift)
            )
        p = jnp.concatenate(parts, 0)
        dkv[at, HEAD:] = nn(p.astype(BF), g).astype(BF)
        ds = (p * (nt(value, g) - dot)).astype(BF)
        dkv[at, :HEAD] = (nn(ds, q) * SCALE).astype(BF)
        dq = dq + tn(key, ds)
    for copy in brought[2:4]:
        copy.wait()
    key, value = kv0[:, :HEAD], kv0[:, HEAD:]
    s = jnp.where(causal_t(), nt(key, q0) * SCALE2, NEG)
    p = jnp.exp2(s - log_sum[:, :TOK])
    own[:, HEAD:] = nn(p.astype(BF), g0)
    ds = (p * (nt(value, g0) - dot[:, :TOK])).astype(BF)
    own[:, :HEAD] = nn(ds, q0) * SCALE
    dq0[...] = (dq[:, :TOK] + tn(key, ds)) * SCALE
    for d, ref in ((1, dq1), (2, dq2), (3, dq3)):
        ref[:TOK, :] = (halves(dq[:, d * TOK : (d + 1) * TOK]) * SCALE).astype(BF)
        ref[TOK:, :] = far[d - 1]


def strided_kernel(meta, q, k, v, g, near, last, o, dq, dkv, far, o_own):
    row, zh = meta[0], meta[1]
    slot = iota((TOK, 4 * REACH), 1) // REACH
    far_ok = (slot < zh) | (jnp.full((TOK, 4 * REACH), row, jnp.int32) > 0)
    near_ok = iota((TOK, TOK), 0) >= iota((TOK, TOK), 1)

    def far_rows(i):
        at = slice(i * REACH, (i + 1) * REACH)
        return jnp.concatenate([near[0, at], near[1, at], near[2, at], last[at]], 0)

    for h in range(3):
        at = slice((h + 1) * HEAD, (h + 2) * HEAD)
        to = slice(h * HEAD, (h + 1) * HEAD)
        qh, kh, vh, gh = q[:, at], k[:, at], v[:, at], g[:, at]
        kf, vf = far_rows(h), far_rows(h + 3)
        s = jnp.where(near_ok, nt(qh, kh) * SCALE, NEG)
        sf = jnp.where(far_ok, nt(qh, kf) * SCALE, NEG)
        top = jnp.maximum(
            jnp.max(s, axis=1, keepdims=True), jnp.max(sf, axis=1, keepdims=True)
        )
        e, ef = jnp.exp(s - top), jnp.exp(sf - top)
        inv = 1.0 / (
            jnp.sum(e, axis=1, keepdims=True) + jnp.sum(ef, axis=1, keepdims=True)
        )
        p, pf = e * inv, ef * inv
        w, wf = p.astype(BF), pf.astype(BF)
        out = (nn(w, vh) + nn(wf, vf)).astype(BF)
        o[:, to] = out
        o_own[:, to] = out
        delta = jnp.sum(gh.astype(F32) * out.astype(F32), axis=1, keepdims=True)
        ds = (p * (nt(gh, vh) - delta) * SCALE).astype(BF)
        dsf = (pf * (nt(gh, vf) - delta) * SCALE).astype(BF)
        dq[:, to] = (nn(ds, kh) + nn(dsf, kf)).astype(BF)
        dkv[:, to] = tn(ds, qh)
        dkv[:, 3 * HEAD + h * HEAD : 3 * HEAD + (h + 1) * HEAD] = tn(w, gh)
        dkf = tn(dsf, qh).astype(BF)
        dvf = tn(wf, gh).astype(BF)
        for u in range(4):
            rows = slice(u * REACH, (u + 1) * REACH)
            far[u, h * REACH : (h + 1) * REACH, :] = dkf[rows]
            far[u, (h + 3) * REACH : (h + 4) * REACH, :] = dvf[rows]


def project_kernel(
    meta, o_f, o_fc, o, o_c, w, w_c, send, keep, here_w, beside_w, here_s, beside_s
):
    zl, c = meta[2], meta[3]
    places = ((1 - zl, c), (zl, c))
    copies = weight_blocks(w, here_w, places, here_s)
    beside_copies = weight_blocks(w_c, beside_w, places, beside_s)
    here = jnp.concatenate([o_f[...], o[...]], 1)
    beside = jnp.concatenate([o_fc[...], o_c[...]], 1)
    for i, ref in ((0, send), (1, keep)):
        copies[i].wait()
        total = nn(here, here_w[i])
        beside_copies[i].wait()
        ref[...] = (total + nn(beside, beside_w[i])).astype(ref.dtype)


def back_kernel(meta, dq0, b1, b2, b3, far, sent, here, dq):
    for u, ref in ((0, b1), (1, b2), (2, b3)):
        sent[u] = ref[TOK:, :]
        here[u] = ref[TOK:, :]
    sent[3] = far[3]
    total = dq0[...]
    for ref in (b1, b2, b3):
        total = total + whole(ref[:TOK, :].astype(F32))
    eye = ones_where(iota((HEAD, HEAD), 0) == iota((HEAD, HEAD), 1))
    dq[...] = tn(total.astype(BF), eye).astype(BF)


def final_kernel(
    meta,
    soff_t,
    sidx,
    dkv,
    own,
    dq,
    here,
    after,
    strided_dq,
    strided,
    keep,
    over,
    out,
    qg,
    kg,
    vg,
):
    zh = meta[1]
    shard = GROUP * meta[0] + meta[1]
    out[...] = (keep[...].astype(F32) + over[...].astype(F32)).astype(BF)
    pick = summary_select(sidx[...])
    fixed = own[...] + nn(jnp.concatenate([pick] * ROWS, 1), dkv[...])
    kg[:, :HEAD] = fixed[:, :HEAD].astype(BF)
    vg[:, :HEAD] = fixed[:, HEAD:].astype(BF)
    qg[:, :HEAD] = dq[...]
    qg[:, HEAD:] = strided_dq[...]
    sel = stride_select(soff_t[...], shard)
    slots = []
    for u in range(4):
        block = after[u]
        if u < 3:
            block = jnp.where(
                zh + 1 + u < GROUP, here[u].astype(F32), block.astype(F32)
            ).astype(BF)
        slots.append(
            jnp.concatenate(
                [block[h * REACH : (h + 1) * REACH] for h in range(6)], 1
            )
        )
    total = strided[...] + tn(sel, jnp.concatenate(slots, 0))
    kg[:, HEAD:] = total[:, : 3 * HEAD].astype(BF)
    vg[:, HEAD:] = total[:, 3 * HEAD :].astype(BF)


def swap(a, axis):
    return lax.ppermute(a, axis, [(0, 1), (1, 0)])


def turn(a, by):
    return lax.ppermute(a, "zh", [(i, (i + by) % GROUP) for i in range(GROUP)])


def after(a, other):
    return lax.optimization_barrier((a, other))[0]


def dma(n):
    return pltpu.SemaphoreType.DMA((n,))


def shards(queries, key_rows, value_rows, out_weight, upstream, summary_index, soff):
    row = lax.axis_index(("x", "y"))
    zh, zl, c = lax.axis_index("zh"), lax.axis_index("zl"), lax.axis_index("c")
    meta = jnp.stack([row, zh, zl, c]).astype(jnp.int32)
    soff_t = soff.T
    width = queries.shape[1]
    quarter = upstream.shape[1]
    plane = ("x", "y")

    up_z = swap(upstream, "zl")
    up_c = swap(upstream, "c")
    block = sds((4, FAR, HEAD))
    kvb, q0, picks = call(
        prep_kernel,
        [sds((ROWS, SUMM, 2 * HEAD)), sds((TOK, HEAD)), block],
        [meta, soff_t, summary_index, key_rows, value_rows, queries],
        [dma(1)],
        name="pick_rows",
        fetch=range(1, 5),
        raw=[5],
    )
    before = lax.ppermute(picks, plane, [(i, i + 1) for i in range(ROWS - 1)])
    two_blocks = [pltpu.VMEM((2, width, quarter), BF), dma(2)]
    (acc,) = call(
        grad_near_kernel,
        [sds((TOK, width), F32)],
        [meta, upstream, up_c, out_weight, picks],
        two_blocks,
        name="attention_grad_near",
        fetch=[1],
        raw=[3],
        store=[0],
    )
    kvb = after(after(kvb, before), acc)
    kva = lax.all_to_all(kvb, plane, 0, 0, tiled=True).reshape(KEYS, 2 * HEAD)
    up_zc = swap(after(up_z, picks), "c")
    qs = [q0] + [turn(q0, d) for d in (1, 2, 3)]
    g, last, q_all, *gs = call(
        grad_far_kernel,
        [sds((TOK, width)), sds((FAR, HEAD)), sds((ALL, HEAD))]
        + [sds((TOK + FAR, HEAD))] * 3,
        [meta, up_z, up_zc, out_weight, acc, picks, before, *qs],
        two_blocks,
        name="attention_grad_far",
        fetch=[4],
        raw=[3],
        store=[0, 1, 2],
    )
    gs = [turn(gs[d - 1], d) for d in (1, 2, 3)]
    ob, g_all, kv_all, near = call(
        forward_kernel,
        [
            sds((GROUP, TOK + STAT, HEAD)),
            sds((ALL, HEAD)),
            sds((KEYS, 2 * HEAD)),
            sds((3, FAR, HEAD)),
        ],
        [meta, q_all, g, *gs, kva, key_rows, value_rows],
        [
            pltpu.VMEM((KEYS, ALL), F32),
            pltpu.VMEM((ALL, HEAD), BF),
            pltpu.VMEM((TOK, 2 * HEAD), BF),
            dma(8),
        ],
        name="fixed_forward",
        fetch=[1],
        raw=[2, 7, 8],
        direct=[1, 2, 3],
    )
    weight_c = swap(after(out_weight, near), "c")
    oa = lax.all_to_all(ob, "zh", 0, 0, tiled=True)
    o_s, dq_s, dkv_s, far, o_own = call(
        strided_kernel,
        [
            sds((TOK, 3 * HEAD)),
            sds((TOK, 3 * HEAD)),
            sds((TOK, 6 * HEAD), F32),
            block,
            sds((TOK, 3 * HEAD)),
        ],
        [meta, queries, key_rows, value_rows, g, near, last],
        name="strided_heads",
        fetch=range(1, 7),
        store=[1, 2, 3, 4],
    )
    o_sc = swap(o_s, "c")
    o_f, stat, o_f_own, o_beside = call(
        combine_kernel,
        [
            sds((TOK, HEAD)),
            sds((8, ALL), F32),
            sds((TOK, HEAD)),
            sds((TOK, 3 * HEAD)),
        ],
        [meta, oa, o_sc],
        name="combine",
        store=[2, 3],
    )
    o_fc = swap(o_f, "c")
    dkv, *dqs, own, dq0 = call(
        backward_kernel,
        [sds((KEYS, 2 * HEAD))]
        + [sds((TOK + FAR, HEAD))] * 3
        + [sds((TOK, 2 * HEAD), F32), sds((HEAD, TOK), F32)],
        [meta, q_all, g_all, kv_all, key_rows, value_rows, stat, far],
        [
            pltpu.VMEM((KEYS, 2 * HEAD), BF),
            pltpu.VMEM((TOK, 2 * HEAD), BF),
            dma(4),
        ],
        name="fixed_backward",
        fetch=[1, 2, 7],
        raw=[3, 4, 5],
        store=[4, 5],
    )
    dkva = lax.all_to_all(
        after(dkv, o_fc).reshape(ROWS, SUMM, 2 * HEAD), plane, 0, 0, tiled=True
    ).reshape(KEYS, 2 * HEAD)
    send, keep = call(
        project_kernel,
        [sds((TOK, quarter))] * 2,
        [meta, o_f_own, o_fc, o_own, o_beside, out_weight, weight_c],
        two_blocks[:1] * 2 + two_blocks[1:] * 2,
        name="project",
        fetch=[1, 3, 4],
        raw=[5, 6],
        store=[1],
    )
    over = swap(send, "zl")
    dqs = [turn(dqs[d - 1], -d) for d in (1, 2, 3)]
    sent, here, dq_f = call(
        back_kernel,
        [block, sds((3, FAR, HEAD)), sds((TOK, HEAD))],
        [meta, dq0, *dqs, far],
        name="bundle_back",
        fetch=[1, 5],
        store=[1, 2],
        flops=5 * 10**9,
    )
    back = lax.ppermute(sent, plane, [(i + 1, i) for i in range(ROWS - 1)])
    return call(
        final_kernel,
        [sds((TOK, quarter))] + [sds((TOK, width))] * 3,
        [meta, soff_t, summary_index, dkva, own, dq_f, here, back, dq_s, dkv_s]
        + [keep, over],
        name="join_results",
        fetch=[1, 2, 4, 5, 6, 8, 9, 10],
    )


def solution(mesh):
    grid = Mesh(mesh.devices.reshape(4, 4, 4, 2, 2), ("x", "y", "zh", "zl", "c"))
    ctx, head = ("x", "y", "zh"), ("zl", "c")
    return jax.shard_map(
        shards,
        mesh=grid,
        in_specs=(
            P(ctx, head),
            P(ctx, head),
            P(ctx, head),
            P(head, None),
            P(ctx, head),
            P(ctx, None),
            P(),
        ),
        out_specs=(P(ctx, head),) * 4,
        check_vma=False,
    )
```

```python
import functools

import jax
import jax.numpy as jnp
from jax import lax
from jax.experimental import pallas as pl
from jax.experimental.pallas import tpu as pltpu
from jax.sharding import Mesh
from jax.sharding import PartitionSpec as P

HEAD = 128
TOK = 256
SUMM = 128
STRIDE = 16
REACH = TOK // STRIDE
ROWS = 16
GROUP = 4
ALL = GROUP * TOK
KEYS = ROWS * SUMM
TILE = 256
STAT = 64
FAR = 6 * REACH
SCALE = HEAD ** (-0.5)
LOG2E = 1.4426950408889634
SCALE2 = SCALE * LOG2E
NEG = -1e30
F32 = jnp.float32
BF = jnp.bfloat16

VM = pl.BlockSpec(memory_space=pltpu.VMEM)
SM = pl.BlockSpec(memory_space=pltpu.SMEM)


def nn(a, b):
    return lax.dot_general(a, b, (((1,), (0,)), ((), ())), preferred_element_type=F32)


def nt(a, b):
    return lax.dot_general(a, b, (((1,), (1,)), ((), ())), preferred_element_type=F32)


def tn(a, b):
    return lax.dot_general(a, b, (((0,), (0,)), ((), ())), preferred_element_type=F32)


def iota(shape, dim):
    return lax.broadcasted_iota(jnp.int32, shape, dim)


def ones_where(condition):
    return condition.astype(F32).astype(BF)


def summary_select(sidx):
    return ones_where(iota((TOK, SUMM), 0) == sidx)


def stride_select(soff_t, shard):
    there = jnp.minimum(shard + 1 + iota((4, ROWS * GROUP), 0), ROWS * GROUP - 1)
    offset = jnp.where(iota((4, ROWS * GROUP), 1) == there, soff_t, 0)
    offset = jnp.sum(offset.astype(F32), axis=1, keepdims=True).astype(jnp.int32)
    row, col = iota((4 * REACH, TOK), 0), iota((4 * REACH, TOK), 1)
    slot = row // REACH
    want = (row % REACH) * STRIDE
    for u in range(4):
        want = want + jnp.where(slot == u, offset[u : u + 1], 0)
    return ones_where(want == col)


def call(
    kernel, outs, ins, scratch=(), name=None, vmem=24, fetch=(), raw=(), store=(),
    direct=(), flops=1,
):
    fetch, raw, store = sorted(fetch), set(raw), sorted(store)
    pinned = set(store) | set(direct)
    n_in, n_out, n_own = len(ins), len(outs), len(scratch)
    hbm = pl.BlockSpec(memory_space=pltpu.HBM)

    def body(*refs):
        given = list(refs[:n_in])
        made = list(refs[n_in : n_in + n_out])
        own = list(refs[n_in + n_out : n_in + n_out + n_own])
        rest = list(refs[n_in + n_out + n_own :])
        here = rest[: len(fetch)]
        there = rest[len(fetch) : len(fetch) + len(store)]
        sems = rest[-1] if fetch or store else None
        copies = []
        for n, (i, ref) in enumerate(zip(fetch, here)):
            copies.append(pltpu.make_async_copy(given[i], ref, sems.at[n]))
            given[i] = ref
        for copy in copies:
            copy.start()
        for copy in copies:
            copy.wait()
        copies = []
        for n, (i, ref) in enumerate(zip(store, there)):
            copies.append(
                pltpu.make_async_copy(ref, made[i], sems.at[len(fetch) + n])
            )
            made[i] = ref
        kernel(*given, *made, *own)
        for copy in copies:
            copy.start()
        for copy in copies:
            copy.wait()

    extra = [pltpu.VMEM(ins[i].shape, ins[i].dtype) for i in fetch]
    extra += [pltpu.VMEM(outs[i].shape, outs[i].dtype) for i in store]
    if extra:
        extra.append(dma(len(extra)))
    return pl.pallas_call(
        body,
        out_shape=tuple(
            pltpu.HBM(s.shape, s.dtype) if i in pinned else s
            for i, s in enumerate(outs)
        ),
        in_specs=[SM]
        + [hbm if i in fetch or i in raw else VM for i in range(1, n_in)],
        out_specs=tuple(hbm if i in pinned else VM for i in range(n_out)),
        scratch_shapes=list(scratch) + extra,
        compiler_params=pltpu.CompilerParams(vmem_limit_bytes=vmem * 2**20),
        cost_estimate=pl.CostEstimate(
            flops=flops, bytes_accessed=1, transcendentals=0
        ),
        name=name,
    )(
        *(
            pltpu.with_memory_space_constraint(x, pltpu.HBM)
            if i in fetch or i in raw
            else x
            for i, x in enumerate(ins)
        )
    )


def sds(shape, dtype=BF):
    return jax.ShapeDtypeStruct(shape, dtype)


def prep_kernel(meta, soff_t, sidx, k, v, q, kvb, q0, picks, sem):
    copy = pltpu.make_async_copy(q.at[:, pl.ds(0, HEAD)], q0, sem.at[0])
    copy.start()
    pick = summary_select(sidx[...])
    kv = tn(pick, jnp.concatenate([k[:, :HEAD], v[:, :HEAD]], 1)).astype(BF)
    for i in range(ROWS):
        kvb[i] = kv
    sel = stride_select(soff_t[...], GROUP * meta[0] + meta[1])
    got = nn(sel, jnp.concatenate([k[:, HEAD:], v[:, HEAD:]], 1)).astype(BF)
    for u in range(4):
        for h in range(6):
            picks[u, h * REACH : (h + 1) * REACH, :] = got[
                u * REACH : (u + 1) * REACH, h * HEAD : (h + 1) * HEAD
            ]
    copy.wait()


def weight_blocks(w, blocks, places, sems):
    wide = blocks.shape[2]
    copies = []
    for i, (z, core) in enumerate(places):
        at = pl.ds(pl.multiple_of((2 * z + core) * wide, wide), wide)
        copies.append(pltpu.make_async_copy(w.at[:, at], blocks.at[i], sems.at[i]))
    for copy in copies:
        copy.start()
    return copies


def bundle_kernel(meta, q0, picks, before, last, *sent):
    zh = meta[1]
    last[...] = before[3]
    for d in (1, 2, 3):
        ref = sent[d - 1]
        ref[:TOK, :] = q0[...]

        @pl.when(zh + d < GROUP)
        def _(d=d, ref=ref):
            ref[TOK:, :] = picks[d - 1]

        @pl.when(zh + d >= GROUP)
        def _(d=d, ref=ref):
            ref[TOK:, :] = before[d - 1]


def grad_near_kernel(meta, up, up_c, w, order, acc, far_w, near_w, sems, far_sems):
    zl, c = meta[2], meta[3]
    copies = weight_blocks(w, near_w, ((zl, c), (zl, 1 - c)), sems)
    far_copies = weight_blocks(w, far_w, ((1 - zl, c), (1 - zl, 1 - c)), far_sems)
    copies[0].wait()
    total = nt(up[...], near_w[0])
    copies[1].wait()
    acc[...] = total + nt(up_c[...], near_w[1])
    for copy in far_copies:
        copy.wait()


def grad_far_kernel(meta, up_z, up_zc, far_w, acc, g0, g):
    full = acc[...] + nt(up_z[...], far_w[0])
    full = (full + nt(up_zc[...], far_w[1])).astype(BF)
    g0[...] = full[:, :HEAD]
    g[...] = full


def fold8(a, how):
    return how(a.reshape(a.shape[0] // 8, 8, a.shape[1]), axis=0)


def causal_t():
    return iota((TOK, TOK), 0) <= iota((TOK, TOK), 1)


def block_masks(row, zh):
    slot = iota((1, ALL), 1) // TOK
    edge = jnp.where(slot > zh, 0.0, NEG)
    none = jnp.full((1, ALL), NEG, F32)
    return [
        jnp.where(jnp.full((1, ALL), b, jnp.int32) < row, 0.0,
                  jnp.where(jnp.full((1, ALL), b, jnp.int32) == row, edge, none))
        for b in range(ROWS)
    ]


def split3(a):
    hi = a.astype(BF).astype(F32)
    mid = (a - hi).astype(BF).astype(F32)
    return [hi, mid, (a - hi - mid).astype(BF).astype(F32)]


def halves(a):
    return jnp.concatenate([a[:, :HEAD], a[:, HEAD:]], 0)


def whole(a):
    n = a.shape[0] // 2
    return jnp.concatenate([a[:n], a[n:]], 1)


def forward_kernel(
    meta, q0, q1, q2, q3, g0, g1, g2, g3, kva, k, v, far, ob, q_all, g_all, kv_all,
    s_ref, kv0, sems
):
    row, zh = meta[0], meta[1]
    first = pl.ds(0, HEAD)
    kept = [
        pltpu.make_async_copy(k.at[:, first], kv0.at[:, first], sems.at[0]),
        pltpu.make_async_copy(
            v.at[:, first], kv0.at[:, pl.ds(HEAD, HEAD)], sems.at[1]
        ),
        pltpu.make_async_copy(kva, kv_all, sems.at[2]),
    ]
    for d, (q, g) in enumerate(((q0, g0), (q1, g1), (q2, g2), (q3, g3))):
        at = pl.ds(d * TOK, TOK)
        source = q.at[pl.ds(0, TOK)]
        kept.append(pltpu.make_async_copy(source, q_all.at[at], sems.at[3 + d]))
        kept.append(pltpu.make_async_copy(g, g_all.at[at], sems.at[7 + d]))
    for copy in kept:
        copy.start()
    q = jnp.concatenate([q0[...], q1[:TOK], q2[:TOK], q3[:TOK]], 0)
    g = jnp.concatenate([g0[...], g1[...], g2[...], g3[...]], 0)
    masks = block_masks(row, zh)
    per = TILE // SUMM
    top = jnp.full((8, ALL), NEG, F32)
    for j in range(KEYS // TILE):
        s = nt(kva[j * TILE : (j + 1) * TILE, :HEAD], q)
        s_ref[j * TILE : (j + 1) * TILE, :] = s
        for i in range(per):
            most = fold8(s[i * SUMM : (i + 1) * SUMM], jnp.max)
            top = jnp.maximum(top, most + masks[per * j + i])
    top = jnp.max(top, axis=0, keepdims=True) * SCALE2
    sums = jnp.zeros((8, ALL), F32)
    dots = jnp.zeros((8, ALL), F32)
    out = jnp.zeros((HEAD, ALL), F32)
    for j in range(KEYS // TILE):
        at = slice(j * TILE, (j + 1) * TILE)
        value = kva[at, HEAD:]
        parts = []
        for i in range(per):
            b = per * j + i
            shift = jnp.where(masks[b] < 0, -NEG, top)
            parts.append(
                jnp.exp2(s_ref[b * SUMM : (b + 1) * SUMM, :] * SCALE2 - shift)
            )
        e = jnp.concatenate(parts, 0)
        sums = sums + fold8(e, jnp.sum)
        dots = dots + fold8(e * nt(value, g), jnp.sum)
        out = out + tn(value, e.astype(BF))
    sums = jnp.sum(sums, axis=0, keepdims=True)
    dots = jnp.sum(dots, axis=0, keepdims=True)
    some = sums > 0
    safe = jnp.where(some, sums, 1.0)
    inv = 1.0 / safe
    log_sum = jnp.where(some, top + jnp.log(safe) * LOG2E, NEG)
    dots = dots * inv
    out = out * inv

    for copy in kept:
        copy.wait()
    key, value = kv0[:, :HEAD], kv0[:, HEAD:]
    s = jnp.where(causal_t(), nt(key, q0[...]) * SCALE2, NEG)
    own_top = jnp.max(s, axis=0, keepdims=True)
    e = jnp.exp2(s - own_top)
    own_sum = jnp.sum(e, axis=0, keepdims=True)
    own_dot = jnp.sum(e * nt(value, g0[...]), axis=0, keepdims=True)
    own_out = tn(value, e.astype(BF))
    own_log = own_top + jnp.log(own_sum) * LOG2E
    near = log_sum[:, :TOK]
    most = jnp.maximum(near, own_log)
    wa, wb = jnp.exp2(near - most), jnp.exp2(own_log - most)
    inv = 1.0 / (wa + wb)
    wa, wb = wa * inv, wb * inv / own_sum
    log_sum = jnp.concatenate(
        [most - jnp.log(inv) * LOG2E, log_sum[:, TOK:]], 1
    )
    dots = jnp.concatenate(
        [wa * dots[:, :TOK] + wb * own_dot, dots[:, TOK:]], 1
    )

    stats = jnp.concatenate(
        split3(log_sum) + split3(dots) + [jnp.zeros((2, ALL), F32)], 0
    )
    stats = jnp.concatenate(
        [stats[:, i * HEAD : (i + 1) * HEAD] for i in range(ALL // HEAD)], 0
    ).astype(BF)
    for d in range(GROUP):
        part = out[:, d * TOK : (d + 1) * TOK]
        if d == 0:
            part = wa * part + wb * own_out
        to = lax.rem(zh - d + GROUP, GROUP)
        ob[to, :TOK, :] = halves(part).astype(BF)
        ob[to, TOK : TOK + STAT, :] = stats
        ob[to, TOK + STAT :, :] = far[(d + 3) % 4]


def combine_kernel(meta, oa, order, o, stat, sent, here):
    zh = meta[1]
    for u in range(4):
        block = oa[lax.rem(zh + 1 + u, GROUP), TOK + STAT :, :]
        sent[u] = block
        here[u] = block
    got = []
    for f in range(GROUP):
        rows = oa[lax.rem(zh - f + GROUP, GROUP), TOK : TOK + STAT, :].astype(F32)
        got.append(
            jnp.concatenate([rows[8 * i : 8 * i + 8] for i in range(STAT // 8)], 1)
        )
    for d in range(GROUP):
        logs, dots = [], []
        for f in range(GROUP):
            e = (d - f) % GROUP
            part = got[f][:, e * TOK : (e + 1) * TOK]
            logs.append(part[0:1] + part[1:2] + part[2:3])
            dots.append(part[3:4] + part[4:5] + part[5:6])
        most = functools.reduce(jnp.maximum, logs)
        shares = [jnp.exp2(x - most) for x in logs]
        both = functools.reduce(jnp.add, shares)
        shares = [x / both for x in shares]
        at = slice(d * TOK, (d + 1) * TOK)
        stat[0:1, at] = most + jnp.log(both) * LOG2E
        stat[1:2, at] = functools.reduce(
            jnp.add, [x * y for x, y in zip(shares, dots)]
        )
        if d == 0:
            full = functools.reduce(
                jnp.add,
                [
                    shares[f]
                    * whole(oa[lax.rem(zh - f + GROUP, GROUP), :TOK, :].astype(F32))
                    for f in range(GROUP)
                ],
            )
            eye = ones_where(iota((HEAD, HEAD), 0) == iota((HEAD, HEAD), 1))
            o[...] = tn(full.astype(BF), eye).astype(BF)
    stat[2:8, :] = jnp.zeros((6, ALL), F32)


def backward_kernel(
    meta, q_all, g_all, kv_all, k, v, stat, dkv, dq1, dq2, dq3, own, dq0,
    qs, gs, kva, kv0, mine, made, sems
):
    row, zh = meta[0], meta[1]
    first = pl.ds(0, HEAD)
    steps = KEYS // TILE
    brought = [
        pltpu.make_async_copy(q_all, qs, sems.at[0]),
        pltpu.make_async_copy(g_all, gs, sems.at[1]),
        pltpu.make_async_copy(k.at[:, first], kv0.at[:, first], sems.at[2]),
        pltpu.make_async_copy(
            v.at[:, first], kv0.at[:, pl.ds(HEAD, HEAD)], sems.at[3]
        ),
    ]
    tiles, sent = [], []
    for j in range(steps):
        at = pl.ds(j * TILE, TILE)
        tiles.append(pltpu.make_async_copy(kv_all.at[at], kva.at[at], sems.at[4 + j]))
        sent.append(
            pltpu.make_async_copy(made.at[at], dkv.at[at], sems.at[4 + steps + j])
        )
    sent.append(pltpu.make_async_copy(mine, own, sems.at[4 + 2 * steps]))
    for copy in brought + tiles:
        copy.start()
    for copy in brought:
        copy.wait()
    log_sum, dot = stat[0:1, :], stat[1:2, :]
    q, g = qs[...], gs[...]
    q0, g0 = q[:TOK], g[:TOK]
    key, value = kv0[:, :HEAD], kv0[:, HEAD:]
    s = jnp.where(causal_t(), nt(key, q0) * SCALE2, NEG)
    p = jnp.exp2(s - log_sum[:, :TOK])
    mine[:, HEAD:] = nn(p.astype(BF), g0)
    ds = (p * (nt(value, g0) - dot[:, :TOK])).astype(BF)
    mine[:, :HEAD] = nn(ds, q0) * SCALE
    dq_own = tn(key, ds)
    sent[-1].start()
    masks = block_masks(row, zh)
    per = TILE // SUMM
    dq = jnp.zeros((HEAD, ALL), F32)
    for j in range(steps):
        at = slice(j * TILE, (j + 1) * TILE)
        tiles[j].wait()
        key, value = kva[at, :HEAD], kva[at, HEAD:]
        s = nt(key, q)
        parts = []
        for i in range(per):
            shift = jnp.where(masks[per * j + i] < 0, -NEG, log_sum)
            parts.append(
                jnp.exp2(s[i * SUMM : (i + 1) * SUMM] * SCALE2 - shift)
            )
        p = jnp.concatenate(parts, 0)
        made[at, HEAD:] = nn(p.astype(BF), g).astype(BF)
        ds = (p * (nt(value, g) - dot)).astype(BF)
        made[at, :HEAD] = (nn(ds, q) * SCALE).astype(BF)
        sent[j].start()
        dq = dq + tn(key, ds)
    dq0[...] = (dq[:, :TOK] + dq_own) * SCALE
    for d, ref in ((1, dq1), (2, dq2), (3, dq3)):
        ref[...] = (halves(dq[:, d * TOK : (d + 1) * TOK]) * SCALE).astype(BF)
    for copy in sent:
        copy.wait()


def strided_kernel(meta, q, k, v, g, f1, f2, f3, last, o, dq, dkv, far, o_own):
    row, zh = meta[0], meta[1]
    slot = iota((TOK, 4 * REACH), 1) // REACH
    far_ok = (slot < zh) | (jnp.full((TOK, 4 * REACH), row, jnp.int32) > 0)
    near_ok = iota((TOK, TOK), 0) >= iota((TOK, TOK), 1)

    def far_rows(i):
        at = slice(TOK + i * REACH, TOK + (i + 1) * REACH)
        to = slice(i * REACH, (i + 1) * REACH)
        return jnp.concatenate([f1[at], f2[at], f3[at], last[to]], 0)

    for h in range(3):
        at = slice((h + 1) * HEAD, (h + 2) * HEAD)
        to = slice(h * HEAD, (h + 1) * HEAD)
        qh, kh, vh, gh = q[:, at], k[:, at], v[:, at], g[:, at]
        kf, vf = far_rows(h), far_rows(h + 3)
        s = jnp.where(near_ok, nt(qh, kh) * SCALE, NEG)
        sf = jnp.where(far_ok, nt(qh, kf) * SCALE, NEG)
        top = jnp.maximum(
            jnp.max(s, axis=1, keepdims=True), jnp.max(sf, axis=1, keepdims=True)
        )
        e, ef = jnp.exp(s - top), jnp.exp(sf - top)
        inv = 1.0 / (
            jnp.sum(e, axis=1, keepdims=True) + jnp.sum(ef, axis=1, keepdims=True)
        )
        p, pf = e * inv, ef * inv
        w, wf = p.astype(BF), pf.astype(BF)
        out = (nn(w, vh) + nn(wf, vf)).astype(BF)
        o[:, to] = out
        o_own[:, to] = out
        delta = jnp.sum(gh.astype(F32) * out.astype(F32), axis=1, keepdims=True)
        ds = (p * (nt(gh, vh) - delta) * SCALE).astype(BF)
        dsf = (pf * (nt(gh, vf) - delta) * SCALE).astype(BF)
        dq[:, to] = (nn(ds, kh) + nn(dsf, kf)).astype(BF)
        dkv[:, to] = tn(ds, qh)
        dkv[:, 3 * HEAD + h * HEAD : 3 * HEAD + (h + 1) * HEAD] = tn(w, gh)
        dkf = tn(dsf, qh).astype(BF)
        dvf = tn(wf, gh).astype(BF)
        for u in range(4):
            rows = slice(u * REACH, (u + 1) * REACH)
            far[u, h * REACH : (h + 1) * REACH, :] = dkf[rows]
            far[u, (h + 3) * REACH : (h + 4) * REACH, :] = dvf[rows]


def project_blocks(meta, w, w_c, first, here_w, beside_w, here_s, beside_s):
    zl, c = meta[2], meta[3]
    places = ((1 - zl, c), (zl, c))
    rows = pl.ds(first, here_w.shape[1])
    return (
        weight_blocks(w.at[rows], here_w, places, here_s),
        weight_blocks(w_c.at[rows], beside_w, places, beside_s),
    )


def project_strided_kernel(meta, o, o_c, w, w_c, acc, *space):
    here_w, beside_w = space[:2]
    copies, beside_copies = project_blocks(meta, w, w_c, HEAD, *space)
    for i in range(2):
        copies[i].wait()
        total = nn(o[...], here_w[i])
        beside_copies[i].wait()
        acc[i] = total + nn(o_c[...], beside_w[i])


def project_fixed_kernel(meta, o, o_c, acc, w, w_c, send, keep, got, sems, *space):
    here_w, beside_w = space[:2]
    before = [pltpu.make_async_copy(acc.at[i], got.at[i], sems.at[i]) for i in range(2)]
    for copy in before:
        copy.start()
    copies, beside_copies = project_blocks(meta, w, w_c, 0, *space)
    for i, ref in ((0, send), (1, keep)):
        copies[i].wait()
        beside_copies[i].wait()
        total = nn(o[...], here_w[i]) + nn(o_c[...], beside_w[i])
        before[i].wait()
        ref[...] = (total + got[i]).astype(ref.dtype)


def final_kernel(
    meta,
    soff_t,
    sidx,
    dkv,
    own,
    dq0,
    dq1,
    dq2,
    dq3,
    here,
    after,
    strided_dq,
    strided,
    keep,
    over,
    out,
    qg,
    kg,
    vg,
):
    zh = meta[1]
    shard = GROUP * meta[0] + meta[1]
    out[...] = (keep[...].astype(F32) + over[...].astype(F32)).astype(BF)
    pick = summary_select(sidx[...])
    fixed = own[...] + nn(jnp.concatenate([pick] * ROWS, 1), dkv[...])
    kg[:, :HEAD] = fixed[:, :HEAD].astype(BF)
    vg[:, :HEAD] = fixed[:, HEAD:].astype(BF)
    total = dq0[...]
    for ref in (dq1, dq2, dq3):
        total = total + whole(ref[...].astype(F32))
    eye = ones_where(iota((HEAD, HEAD), 0) == iota((HEAD, HEAD), 1))
    qg[:, :HEAD] = tn(total.astype(BF), eye).astype(BF)
    qg[:, HEAD:] = strided_dq[...]
    sel = stride_select(soff_t[...], shard)
    slots = []
    for u in range(4):
        block = after[u]
        if u < 3:
            block = jnp.where(
                zh + 1 + u < GROUP, here[u].astype(F32), block.astype(F32)
            ).astype(BF)
        slots.append(
            jnp.concatenate(
                [block[h * REACH : (h + 1) * REACH] for h in range(6)], 1
            )
        )
    total = strided[...] + tn(sel, jnp.concatenate(slots, 0))
    kg[:, HEAD:] = total[:, : 3 * HEAD].astype(BF)
    vg[:, HEAD:] = total[:, 3 * HEAD :].astype(BF)


def swap(a, axis):
    return lax.ppermute(a, axis, [(0, 1), (1, 0)])


def turn(a, by):
    return lax.ppermute(a, "zh", [(i, (i + by) % GROUP) for i in range(GROUP)])


def after(a, other):
    return lax.optimization_barrier((a, other))[0]


def dma(n):
    return pltpu.SemaphoreType.DMA((n,))


def shards(queries, key_rows, value_rows, out_weight, upstream, summary_index, soff):
    row = lax.axis_index(("x", "y"))
    zh, zl, c = lax.axis_index("zh"), lax.axis_index("zl"), lax.axis_index("c")
    meta = jnp.stack([row, zh, zl, c]).astype(jnp.int32)
    soff_t = soff.T
    width = queries.shape[1]
    quarter = upstream.shape[1]
    plane = ("x", "y")

    up_z = swap(upstream, "zl")
    up_c = swap(upstream, "c")
    block = sds((4, FAR, HEAD))
    kvb, q0, picks = call(
        prep_kernel,
        [sds((ROWS, SUMM, 2 * HEAD)), sds((TOK, HEAD)), block],
        [meta, soff_t, summary_index, key_rows, value_rows, queries],
        [dma(1)],
        name="pick_rows",
        fetch=range(1, 5),
        raw=[5],
    )
    before = lax.ppermute(picks, plane, [(i, i + 1) for i in range(ROWS - 1)])
    last, *sent = call(
        bundle_kernel,
        [sds((FAR, HEAD))] + [sds((TOK + FAR, HEAD))] * 3,
        [meta, q0, picks, before],
        name="bundle_queries",
    )
    kvb = after(kvb, last)
    kva = lax.all_to_all(kvb, plane, 0, 0, tiled=True).reshape(KEYS, 2 * HEAD)
    qs = [q0] + [turn(sent[d - 1], d) for d in (1, 2, 3)]
    two_blocks = [pltpu.VMEM((2, width, quarter), BF), dma(2)]
    acc, far_w = call(
        grad_near_kernel,
        [sds((TOK, width), F32), sds((2, width, quarter))],
        [meta, upstream, up_c, out_weight, last],
        two_blocks + [dma(2)],
        name="attention_grad_near",
        fetch=[1],
        raw=[3],
    )
    up_zc = swap(after(up_z, last), "c")
    g0, g = call(
        grad_far_kernel,
        [sds((TOK, HEAD)), sds((TOK, width))],
        [meta, up_z, up_zc, far_w, acc],
        name="attention_grad_far",
    )
    gs = [g0] + [turn(g0, d) for d in (1, 2, 3)]
    o_s, dq_s, dkv_s, far, o_own = call(
        strided_kernel,
        [
            sds((TOK, 3 * HEAD)),
            sds((TOK, 3 * HEAD)),
            sds((TOK, 6 * HEAD), F32),
            block,
            sds((TOK, 3 * HEAD)),
        ],
        [meta, queries, key_rows, value_rows, g, *qs[1:], last],
        name="strided_heads",
        fetch=range(1, 4),
        store=[1, 2, 4],
    )
    o_sc = swap(o_s, "c")
    ob, q_all, g_all, kv_all = call(
        forward_kernel,
        [
            sds((GROUP, TOK + STAT + FAR, HEAD)),
            sds((ALL, HEAD)),
            sds((ALL, HEAD)),
            sds((KEYS, 2 * HEAD)),
        ],
        [meta, *qs, *gs, kva, key_rows, value_rows, far],
        [
            pltpu.VMEM((KEYS, ALL), F32),
            pltpu.VMEM((TOK, 2 * HEAD), BF),
            dma(11),
        ],
        name="fixed_forward",
        raw=[10, 11],
        direct=[1, 2, 3],
    )
    weight_c = swap(after(out_weight, q_all), "c")
    oa = lax.all_to_all(ob, "zh", 0, 0, tiled=True)
    (acc_out,) = call(
        project_strided_kernel,
        [sds((2, TOK, quarter), F32)],
        [meta, o_own, o_sc, out_weight, weight_c],
        [pltpu.VMEM((2, 3 * HEAD, quarter), BF)] * 2 + [dma(2)] * 2,
        name="project_strided",
        fetch=[1],
        raw=[3, 4],
        store=[0],
    )
    o_f, stat, sent, here = call(
        combine_kernel,
        [sds((TOK, HEAD)), sds((8, ALL), F32), block, block],
        [meta, oa, acc_out],
        name="combine",
        raw=[2],
        store=[3],
    )
    o_fc = swap(o_f, "c")
    back = lax.ppermute(sent, plane, [(i + 1, i) for i in range(ROWS - 1)])
    dkv, *dqs, own, dq0 = call(
        backward_kernel,
        [sds((KEYS, 2 * HEAD))]
        + [sds((TOK, HEAD))] * 3
        + [sds((TOK, 2 * HEAD), F32), sds((HEAD, TOK), F32)],
        [meta, q_all, g_all, kv_all, key_rows, value_rows, stat],
        [
            pltpu.VMEM((ALL, HEAD), BF),
            pltpu.VMEM((ALL, HEAD), BF),
            pltpu.VMEM((KEYS, 2 * HEAD), BF),
            pltpu.VMEM((TOK, 2 * HEAD), BF),
            pltpu.VMEM((TOK, 2 * HEAD), F32),
            pltpu.VMEM((KEYS, 2 * HEAD), BF),
            dma(5 + 2 * (KEYS // TILE)),
        ],
        name="fixed_backward",
        raw=range(1, 6),
        store=[5],
        direct=[0, 4],
    )
    send, keep = call(
        project_fixed_kernel,
        [sds((TOK, quarter))] * 2,
        [meta, o_f, o_fc, acc_out, out_weight, weight_c],
        [pltpu.VMEM((2, TOK, quarter), F32), dma(2)]
        + [pltpu.VMEM((2, HEAD, quarter), BF)] * 2
        + [dma(2)] * 2,
        name="project_fixed",
        raw=[3, 4, 5],
        store=[1],
    )
    over = swap(send, "zl")
    dkva = lax.all_to_all(
        after(dkv, o_fc).reshape(ROWS, SUMM, 2 * HEAD), plane, 0, 0, tiled=True
    ).reshape(KEYS, 2 * HEAD)
    dqs = [turn(dqs[d - 1], -d) for d in (1, 2, 3)]
    return call(
        final_kernel,
        [sds((TOK, quarter))] + [sds((TOK, width))] * 3,
        [meta, soff_t, summary_index, dkva, own, dq0, *dqs, here, back, dq_s, dkv_s]
        + [keep, over],
        name="join_results",
        fetch=[1, 2, 4, 5, 9, 11, 12, 13],
    )


def solution(mesh):
    grid = Mesh(mesh.devices.reshape(4, 4, 4, 2, 2), ("x", "y", "zh", "zl", "c"))
    ctx, head = ("x", "y", "zh"), ("zl", "c")
    return jax.shard_map(
        shards,
        mesh=grid,
        in_specs=(
            P(ctx, head),
            P(ctx, head),
            P(ctx, head),
            P(head, None),
            P(ctx, head),
            P(ctx, None),
            P(),
        ),
        out_specs=(P(ctx, head),) * 4,
        check_vma=False,
    )
```

```python
import functools

import jax
import jax.numpy as jnp
from jax import lax
from jax.experimental import pallas as pl
from jax.experimental.pallas import tpu as pltpu
from jax.sharding import Mesh
from jax.sharding import PartitionSpec as P

HEAD = 128
TOK = 256
SUMM = 128
STRIDE = 16
REACH = TOK // STRIDE
ROWS = 16
GROUP = 4
ALL = GROUP * TOK
KEYS = ROWS * SUMM
TILE = 256
STAT = 64
FAR = 6 * REACH
SCALE = HEAD ** (-0.5)
LOG2E = 1.4426950408889634
SCALE2 = SCALE * LOG2E
NEG = -1e30
F32 = jnp.float32
BF = jnp.bfloat16

VM = pl.BlockSpec(memory_space=pltpu.VMEM)
SM = pl.BlockSpec(memory_space=pltpu.SMEM)


def nn(a, b):
    return lax.dot_general(a, b, (((1,), (0,)), ((), ())), preferred_element_type=F32)


def nt(a, b):
    return lax.dot_general(a, b, (((1,), (1,)), ((), ())), preferred_element_type=F32)


def tn(a, b):
    return lax.dot_general(a, b, (((0,), (0,)), ((), ())), preferred_element_type=F32)


def iota(shape, dim):
    return lax.broadcasted_iota(jnp.int32, shape, dim)


def ones_where(condition):
    return condition.astype(F32).astype(BF)


def summary_select(sidx):
    return ones_where(iota((TOK, SUMM), 0) == sidx)


def stride_select(soff_t, shard):
    there = jnp.minimum(shard + 1 + iota((4, ROWS * GROUP), 0), ROWS * GROUP - 1)
    offset = jnp.where(iota((4, ROWS * GROUP), 1) == there, soff_t, 0)
    offset = jnp.sum(offset.astype(F32), axis=1, keepdims=True).astype(jnp.int32)
    row, col = iota((4 * REACH, TOK), 0), iota((4 * REACH, TOK), 1)
    slot = row // REACH
    want = (row % REACH) * STRIDE
    for u in range(4):
        want = want + jnp.where(slot == u, offset[u : u + 1], 0)
    return ones_where(want == col)


def call(
    kernel, outs, ins, scratch=(), name=None, vmem=24, fetch=(), raw=(), store=(),
    direct=(), flops=1,
):
    fetch, raw, store = sorted(fetch), set(raw), sorted(store)
    pinned = set(store) | set(direct)
    n_in, n_out, n_own = len(ins), len(outs), len(scratch)
    hbm = pl.BlockSpec(memory_space=pltpu.HBM)

    def body(*refs):
        given = list(refs[:n_in])
        made = list(refs[n_in : n_in + n_out])
        own = list(refs[n_in + n_out : n_in + n_out + n_own])
        rest = list(refs[n_in + n_out + n_own :])
        here = rest[: len(fetch)]
        there = rest[len(fetch) : len(fetch) + len(store)]
        sems = rest[-1] if fetch or store else None
        copies = []
        for n, (i, ref) in enumerate(zip(fetch, here)):
            copies.append(pltpu.make_async_copy(given[i], ref, sems.at[n]))
            given[i] = ref
        for copy in copies:
            copy.start()
        for copy in copies:
            copy.wait()
        copies = []
        for n, (i, ref) in enumerate(zip(store, there)):
            copies.append(
                pltpu.make_async_copy(ref, made[i], sems.at[len(fetch) + n])
            )
            made[i] = ref
        kernel(*given, *made, *own)
        for copy in copies:
            copy.start()
        for copy in copies:
            copy.wait()

    extra = [pltpu.VMEM(ins[i].shape, ins[i].dtype) for i in fetch]
    extra += [pltpu.VMEM(outs[i].shape, outs[i].dtype) for i in store]
    if extra:
        extra.append(dma(len(extra)))
    return pl.pallas_call(
        body,
        out_shape=tuple(
            pltpu.HBM(s.shape, s.dtype) if i in pinned else s
            for i, s in enumerate(outs)
        ),
        in_specs=[SM]
        + [hbm if i in fetch or i in raw else VM for i in range(1, n_in)],
        out_specs=tuple(hbm if i in pinned else VM for i in range(n_out)),
        scratch_shapes=list(scratch) + extra,
        compiler_params=pltpu.CompilerParams(vmem_limit_bytes=vmem * 2**20),
        cost_estimate=pl.CostEstimate(
            flops=flops, bytes_accessed=1, transcendentals=0
        ),
        name=name,
    )(
        *(
            pltpu.with_memory_space_constraint(x, pltpu.HBM)
            if i in fetch or i in raw
            else x
            for i, x in enumerate(ins)
        )
    )


def sds(shape, dtype=BF):
    return jax.ShapeDtypeStruct(shape, dtype)


def prep_kernel(meta, soff_t, sidx, k, v, q, kvb, q0, picks, sem):
    copy = pltpu.make_async_copy(q.at[:, pl.ds(0, HEAD)], q0, sem.at[0])
    copy.start()
    pick = summary_select(sidx[...])
    kv = tn(pick, jnp.concatenate([k[:, :HEAD], v[:, :HEAD]], 1)).astype(BF)
    for i in range(ROWS):
        kvb[i] = kv
    sel = stride_select(soff_t[...], GROUP * meta[0] + meta[1])
    got = nn(sel, jnp.concatenate([k[:, HEAD:], v[:, HEAD:]], 1)).astype(BF)
    for u in range(4):
        for h in range(6):
            picks[u, h * REACH : (h + 1) * REACH, :] = got[
                u * REACH : (u + 1) * REACH, h * HEAD : (h + 1) * HEAD
            ]
    copy.wait()


def weight_blocks(w, blocks, places, sems):
    wide = blocks.shape[2]
    copies = []
    for i, (z, core) in enumerate(places):
        at = pl.ds(pl.multiple_of((2 * z + core) * wide, wide), wide)
        copies.append(pltpu.make_async_copy(w.at[:, at], blocks.at[i], sems.at[i]))
    for copy in copies:
        copy.start()
    return copies


def bundle_kernel(meta, q0, picks, before, last, *sent):
    zh = meta[1]
    last[...] = before[3]
    for d in (1, 2, 3):
        ref = sent[d - 1]
        ref[:TOK, :] = q0[...]

        @pl.when(zh + d < GROUP)
        def _(d=d, ref=ref):
            ref[TOK:, :] = picks[d - 1]

        @pl.when(zh + d >= GROUP)
        def _(d=d, ref=ref):
            ref[TOK:, :] = before[d - 1]


def grad_near_kernel(meta, up, up_c, w, order, acc, far_w, near_w, sems, far_sems):
    zl, c = meta[2], meta[3]
    copies = weight_blocks(w, near_w, ((zl, c), (zl, 1 - c)), sems)
    far_copies = weight_blocks(w, far_w, ((1 - zl, c), (1 - zl, 1 - c)), far_sems)
    copies[0].wait()
    total = nt(up[...], near_w[0])
    copies[1].wait()
    acc[...] = total + nt(up_c[...], near_w[1])
    for copy in far_copies:
        copy.wait()


def grad_far_kernel(meta, up_z, up_zc, far_w, acc, g0, g):
    full = acc[...] + nt(up_z[...], far_w[0])
    full = (full + nt(up_zc[...], far_w[1])).astype(BF)
    g0[...] = full[:, :HEAD]
    g[...] = full


def fold8(a, how):
    return how(a.reshape(a.shape[0] // 8, 8, a.shape[1]), axis=0)


def causal_t():
    return iota((TOK, TOK), 0) <= iota((TOK, TOK), 1)


def block_masks(row, zh):
    slot = iota((1, ALL), 1) // TOK
    edge = jnp.where(slot > zh, 0.0, NEG)
    none = jnp.full((1, ALL), NEG, F32)
    return [
        jnp.where(jnp.full((1, ALL), b, jnp.int32) < row, 0.0,
                  jnp.where(jnp.full((1, ALL), b, jnp.int32) == row, edge, none))
        for b in range(ROWS)
    ]


def split3(a):
    hi = a.astype(BF).astype(F32)
    mid = (a - hi).astype(BF).astype(F32)
    return [hi, mid, (a - hi - mid).astype(BF).astype(F32)]


def halves(a):
    return jnp.concatenate([a[:, :HEAD], a[:, HEAD:]], 0)


def whole(a):
    n = a.shape[0] // 2
    return jnp.concatenate([a[:n], a[n:]], 1)


def own_keys(k, v, kv0, sems):
    first = pl.ds(0, HEAD)
    copies = [
        pltpu.make_async_copy(k.at[:, first], kv0.at[:, first], sems.at[0]),
        pltpu.make_async_copy(
            v.at[:, first], kv0.at[:, pl.ds(HEAD, HEAD)], sems.at[1]
        ),
    ]
    for copy in copies:
        copy.start()
    return copies


def forward_kernel(
    meta, q0, q1, q2, q3, g0, g1, g2, g3, kva, k, v, far, ob0, ob1, ob2, ob3,
    s_ref, kv0, sems
):
    row, zh = meta[0], meta[1]
    brought = own_keys(k, v, kv0, sems)
    q = jnp.concatenate([q0[...], q1[:TOK], q2[:TOK], q3[:TOK]], 0)
    g = jnp.concatenate([g0[...], g1[...], g2[...], g3[...]], 0)
    masks = block_masks(row, zh)
    per = TILE // SUMM
    top = jnp.full((8, ALL), NEG, F32)
    for j in range(KEYS // TILE):
        s = nt(kva[j * TILE : (j + 1) * TILE, :HEAD], q)
        s_ref[j * TILE : (j + 1) * TILE, :] = s
        for i in range(per):
            most = fold8(s[i * SUMM : (i + 1) * SUMM], jnp.max)
            top = jnp.maximum(top, most + masks[per * j + i])
    top = jnp.max(top, axis=0, keepdims=True) * SCALE2
    sums = jnp.zeros((8, ALL), F32)
    dots = jnp.zeros((8, ALL), F32)
    out = jnp.zeros((HEAD, ALL), F32)
    for j in range(KEYS // TILE):
        at = slice(j * TILE, (j + 1) * TILE)
        value = kva[at, HEAD:]
        parts = []
        for i in range(per):
            b = per * j + i
            shift = jnp.where(masks[b] < 0, -NEG, top)
            parts.append(
                jnp.exp2(s_ref[b * SUMM : (b + 1) * SUMM, :] * SCALE2 - shift)
            )
        e = jnp.concatenate(parts, 0)
        sums = sums + fold8(e, jnp.sum)
        dots = dots + fold8(e * nt(value, g), jnp.sum)
        out = out + tn(value, e.astype(BF))
    sums = jnp.sum(sums, axis=0, keepdims=True)
    dots = jnp.sum(dots, axis=0, keepdims=True)
    some = sums > 0
    safe = jnp.where(some, sums, 1.0)
    inv = 1.0 / safe
    log_sum = jnp.where(some, top + jnp.log(safe) * LOG2E, NEG)
    dots = dots * inv
    out = out * inv

    for copy in brought:
        copy.wait()
    key, value = kv0[:, :HEAD], kv0[:, HEAD:]
    s = jnp.where(causal_t(), nt(key, q0[...]) * SCALE2, NEG)
    own_top = jnp.max(s, axis=0, keepdims=True)
    e = jnp.exp2(s - own_top)
    own_sum = jnp.sum(e, axis=0, keepdims=True)
    own_dot = jnp.sum(e * nt(value, g0[...]), axis=0, keepdims=True)
    own_out = tn(value, e.astype(BF))
    own_log = own_top + jnp.log(own_sum) * LOG2E
    near = log_sum[:, :TOK]
    most = jnp.maximum(near, own_log)
    wa, wb = jnp.exp2(near - most), jnp.exp2(own_log - most)
    inv = 1.0 / (wa + wb)
    wa, wb = wa * inv, wb * inv / own_sum
    log_sum = jnp.concatenate(
        [most - jnp.log(inv) * LOG2E, log_sum[:, TOK:]], 1
    )
    dots = jnp.concatenate(
        [wa * dots[:, :TOK] + wb * own_dot, dots[:, TOK:]], 1
    )

    stats = jnp.concatenate(
        split3(log_sum) + split3(dots) + [jnp.zeros((2, ALL), F32)], 0
    )
    stats = jnp.concatenate(
        [stats[:, i * HEAD : (i + 1) * HEAD] for i in range(ALL // HEAD)], 0
    ).astype(BF)
    for d, ref in enumerate((ob0, ob1, ob2, ob3)):
        part = out[:, d * TOK : (d + 1) * TOK]
        if d == 0:
            part = wa * part + wb * own_out
        ref[:TOK, :] = halves(part).astype(BF)
        ref[TOK : TOK + STAT, :] = stats
        ref[TOK + STAT :, :] = far[(d + 3) % 4]


def combine_kernel(meta, ob0, r1, r2, r3, order, o, stat, sent, here):
    for u, ref in enumerate((r1, r2, r3, ob0)):
        sent[u] = ref[TOK + STAT :, :]
        here[u] = ref[TOK + STAT :, :]
    sources = (ob0, r3, r2, r1)
    got = []
    for f in range(GROUP):
        rows = sources[f][TOK : TOK + STAT, :].astype(F32)
        got.append(
            jnp.concatenate([rows[8 * i : 8 * i + 8] for i in range(STAT // 8)], 1)
        )
    for d in range(GROUP):
        logs, dots = [], []
        for f in range(GROUP):
            e = (d - f) % GROUP
            part = got[f][:, e * TOK : (e + 1) * TOK]
            logs.append(part[0:1] + part[1:2] + part[2:3])
            dots.append(part[3:4] + part[4:5] + part[5:6])
        most = functools.reduce(jnp.maximum, logs)
        shares = [jnp.exp2(x - most) for x in logs]
        both = functools.reduce(jnp.add, shares)
        shares = [x / both for x in shares]
        at = slice(d * TOK, (d + 1) * TOK)
        stat[0:1, at] = most + jnp.log(both) * LOG2E
        stat[1:2, at] = functools.reduce(
            jnp.add, [x * y for x, y in zip(shares, dots)]
        )
        if d == 0:
            full = functools.reduce(
                jnp.add,
                [
                    shares[f]
                    * whole(sources[f][:TOK, :].astype(F32))
                    for f in range(GROUP)
                ],
            )
            eye = ones_where(iota((HEAD, HEAD), 0) == iota((HEAD, HEAD), 1))
            o[...] = tn(full.astype(BF), eye).astype(BF)
    stat[2:8, :] = jnp.zeros((6, ALL), F32)


def backward_kernel(
    meta, q0, q1, q2, q3, g0, g1, g2, g3, kva, k, v, stat, dkv, dq1, dq2, dq3, own, dq0,
    kv0, mine, made, sems, kv_sems
):
    row, zh = meta[0], meta[1]
    brought = own_keys(k, v, kv0, kv_sems)
    steps = KEYS // TILE
    sent = []
    for j in range(steps):
        at = pl.ds(j * TILE, TILE)
        sent.append(pltpu.make_async_copy(made.at[at], dkv.at[at], sems.at[j]))
    sent.append(pltpu.make_async_copy(mine, own, sems.at[steps]))
    q = jnp.concatenate([q0[...], q1[:TOK], q2[:TOK], q3[:TOK]], 0)
    g = jnp.concatenate([g0[...], g1[...], g2[...], g3[...]], 0)
    log_sum, dot = stat[0:1, :], stat[1:2, :]
    masks = block_masks(row, zh)
    per = TILE // SUMM
    dq = jnp.zeros((HEAD, ALL), F32)
    for j in range(steps):
        at = slice(j * TILE, (j + 1) * TILE)
        key, value = kva[at, :HEAD], kva[at, HEAD:]
        s = nt(key, q)
        parts = []
        for i in range(per):
            shift = jnp.where(masks[per * j + i] < 0, -NEG, log_sum)
            parts.append(
                jnp.exp2(s[i * SUMM : (i + 1) * SUMM] * SCALE2 - shift)
            )
        p = jnp.concatenate(parts, 0)
        made[at, HEAD:] = nn(p.astype(BF), g).astype(BF)
        ds = (p * (nt(value, g) - dot)).astype(BF)
        made[at, :HEAD] = (nn(ds, q) * SCALE).astype(BF)
        sent[j].start()
        dq = dq + tn(key, ds)
        if j == steps // 2:
            for copy in brought:
                copy.wait()
            key, value = kv0[:, :HEAD], kv0[:, HEAD:]
            s = jnp.where(causal_t(), nt(key, q[:TOK]) * SCALE2, NEG)
            p = jnp.exp2(s - log_sum[:, :TOK])
            mine[:, HEAD:] = nn(p.astype(BF), g[:TOK])
            ds = (p * (nt(value, g[:TOK]) - dot[:, :TOK])).astype(BF)
            mine[:, :HEAD] = nn(ds, q[:TOK]) * SCALE
            dq_own = tn(key, ds)
            sent[-1].start()
    dq0[...] = (dq[:, :TOK] + dq_own) * SCALE
    for d, ref in ((1, dq1), (2, dq2), (3, dq3)):
        ref[...] = (halves(dq[:, d * TOK : (d + 1) * TOK]) * SCALE).astype(BF)
    for copy in sent:
        copy.wait()


def strided_kernel(
    meta, q, k, v, g, f1, f2, f3, last, o, far, dq, dkv, qs, ks, vs, dqs, dks, sems, out_s
):
    row, zh = meta[0], meta[1]
    brought, taken = [], []
    for h in range(3):
        for i, (ref, to) in enumerate(((q, qs), (k, ks), (v, vs))):
            at = pl.ds((h + 1) * HEAD, HEAD)
            brought.append(
                pltpu.make_async_copy(ref.at[:, at], to.at[h], sems.at[3 * h + i])
            )
            brought[-1].start()
        at = pl.ds(h * HEAD, HEAD)
        also = pl.ds((h + 3) * HEAD, HEAD)
        taken.append(
            [
                pltpu.make_async_copy(dqs.at[h], dq.at[:, at], out_s.at[3 * h]),
                pltpu.make_async_copy(dks.at[h], dkv.at[:, at], out_s.at[3 * h + 1]),
                pltpu.make_async_copy(
                    dks.at[h + 3], dkv.at[:, also], out_s.at[3 * h + 2]
                ),
            ]
        )
    slot = iota((TOK, 4 * REACH), 1) // REACH
    far_ok = (slot < zh) | (jnp.full((TOK, 4 * REACH), row, jnp.int32) > 0)
    near_ok = iota((TOK, TOK), 0) >= iota((TOK, TOK), 1)

    def far_rows(i):
        at = slice(TOK + i * REACH, TOK + (i + 1) * REACH)
        to = slice(i * REACH, (i + 1) * REACH)
        return jnp.concatenate([f1[at], f2[at], f3[at], last[to]], 0)

    for h in range(3):
        at = slice((h + 1) * HEAD, (h + 2) * HEAD)
        to = slice(h * HEAD, (h + 1) * HEAD)
        for copy in brought[3 * h : 3 * h + 3]:
            copy.wait()
        qh, kh, vh, gh = qs[h], ks[h], vs[h], g[:, at]
        kf, vf = far_rows(h), far_rows(h + 3)
        s = jnp.where(near_ok, nt(qh, kh) * SCALE, NEG)
        sf = jnp.where(far_ok, nt(qh, kf) * SCALE, NEG)
        top = jnp.maximum(
            jnp.max(s, axis=1, keepdims=True), jnp.max(sf, axis=1, keepdims=True)
        )
        e, ef = jnp.exp(s - top), jnp.exp(sf - top)
        inv = 1.0 / (
            jnp.sum(e, axis=1, keepdims=True) + jnp.sum(ef, axis=1, keepdims=True)
        )
        p, pf = e * inv, ef * inv
        w, wf = p.astype(BF), pf.astype(BF)
        out = (nn(w, vh) + nn(wf, vf)).astype(BF)
        o[:, to] = out
        delta = jnp.sum(gh.astype(F32) * out.astype(F32), axis=1, keepdims=True)
        ds = (p * (nt(gh, vh) - delta) * SCALE).astype(BF)
        dsf = (pf * (nt(gh, vf) - delta) * SCALE).astype(BF)
        dqs[h] = (nn(ds, kh) + nn(dsf, kf)).astype(BF)
        dks[h] = tn(ds, qh)
        dks[h + 3] = tn(w, gh)
        for copy in taken[h]:
            copy.start()
        dkf = tn(dsf, qh).astype(BF)
        dvf = tn(wf, gh).astype(BF)
        for u in range(4):
            rows = slice(u * REACH, (u + 1) * REACH)
            far[u, h * REACH : (h + 1) * REACH, :] = dkf[rows]
            far[u, (h + 3) * REACH : (h + 4) * REACH, :] = dvf[rows]
    for group in taken:
        for copy in group:
            copy.wait()


def project_strided_kernel(
    meta, o, o_c, w, w_c, acc, fixed_w, fixed_wc, here_w, sems, ahead_sems
):
    zl, c = meta[2], meta[3]
    places = ((1 - zl, c), (zl, c))
    copies = weight_blocks(w.at[pl.ds(HEAD, 3 * HEAD)], here_w, places, sems)
    ahead = weight_blocks(w.at[pl.ds(0, HEAD)], fixed_w, places, ahead_sems)
    wide = here_w.shape[2]
    for i, (z, core) in enumerate(places):
        at = pl.ds(pl.multiple_of((2 * z + core) * wide, wide), wide)
        fixed_wc[i] = w_c[:HEAD, at]
        total = nn(o_c[...], w_c[HEAD:, at])
        copies[i].wait()
        acc[i] = total + nn(o[...], here_w[i])
    for copy in ahead:
        copy.wait()


def project_fixed_kernel(meta, o, o_c, acc, fixed_w, fixed_wc, order, send, keep):
    for i, ref in ((0, send), (1, keep)):
        total = acc[i] + nn(o[...], fixed_w[i]) + nn(o_c[...], fixed_wc[i])
        ref[...] = total.astype(ref.dtype)


def output_kernel(meta, keep, over, out):
    out[...] = (keep[...].astype(F32) + over[...].astype(F32)).astype(BF)


def query_kernel(meta, dq0, dq1, dq2, dq3, strided_dq, qg):
    total = dq0[...]
    for ref in (dq1, dq2, dq3):
        total = total + whole(ref[...].astype(F32))
    eye = ones_where(iota((HEAD, HEAD), 0) == iota((HEAD, HEAD), 1))
    qg[:, :HEAD] = tn(total.astype(BF), eye).astype(BF)
    qg[:, HEAD:] = strided_dq[...]


def final_kernel(meta, soff_t, sidx, dkv, own, here, after, strided, kg, vg):
    zh = meta[1]
    shard = GROUP * meta[0] + meta[1]
    pick = summary_select(sidx[...])
    fixed = own[...] + nn(jnp.concatenate([pick] * ROWS, 1), dkv[...])
    kg[:, :HEAD] = fixed[:, :HEAD].astype(BF)
    vg[:, :HEAD] = fixed[:, HEAD:].astype(BF)
    sel = stride_select(soff_t[...], shard)
    slots = []
    for u in range(4):
        block = after[u]
        if u < 3:
            block = jnp.where(
                zh + 1 + u < GROUP, here[u].astype(F32), block.astype(F32)
            ).astype(BF)
        slots.append(
            jnp.concatenate(
                [block[h * REACH : (h + 1) * REACH] for h in range(6)], 1
            )
        )
    total = strided[...] + tn(sel, jnp.concatenate(slots, 0))
    kg[:, HEAD:] = total[:, : 3 * HEAD].astype(BF)
    vg[:, HEAD:] = total[:, 3 * HEAD :].astype(BF)


def swap(a, axis):
    return lax.ppermute(a, axis, [(0, 1), (1, 0)])


def turn(a, by):
    return lax.ppermute(a, "zh", [(i, (i + by) % GROUP) for i in range(GROUP)])


def after(a, other):
    return lax.optimization_barrier((a, other))[0]


def dma(n):
    return pltpu.SemaphoreType.DMA((n,))


def shards(queries, key_rows, value_rows, out_weight, upstream, summary_index, soff):
    row = lax.axis_index(("x", "y"))
    zh, zl, c = lax.axis_index("zh"), lax.axis_index("zl"), lax.axis_index("c")
    meta = jnp.stack([row, zh, zl, c]).astype(jnp.int32)
    soff_t = soff.T
    width = queries.shape[1]
    quarter = upstream.shape[1]
    plane = ("x", "y")

    up_z = swap(upstream, "zl")
    up_c = swap(upstream, "c")
    block = sds((4, FAR, HEAD))
    kvb, q0, picks = call(
        prep_kernel,
        [sds((ROWS, SUMM, 2 * HEAD)), sds((TOK, HEAD)), block],
        [meta, soff_t, summary_index, key_rows, value_rows, queries],
        [dma(1)],
        name="pick_rows",
        fetch=range(1, 5),
        raw=[5],
    )
    before = lax.ppermute(picks, plane, [(i, i + 1) for i in range(ROWS - 1)])
    last, *sent = call(
        bundle_kernel,
        [sds((FAR, HEAD))] + [sds((TOK + FAR, HEAD))] * 3,
        [meta, q0, picks, before],
        name="bundle_queries",
    )
    kvb = after(kvb, last)
    kva = lax.all_to_all(kvb, plane, 0, 0, tiled=True).reshape(KEYS, 2 * HEAD)
    qs = [q0] + [turn(sent[d - 1], d) for d in (1, 2, 3)]
    two_blocks = [pltpu.VMEM((2, width, quarter), BF), dma(2)]
    acc, far_w = call(
        grad_near_kernel,
        [sds((TOK, width), F32), sds((2, width, quarter))],
        [meta, upstream, up_c, out_weight, last],
        two_blocks + [dma(2)],
        name="attention_grad_near",
        fetch=[1],
        raw=[3],
    )
    up_zc = swap(after(up_z, last), "c")
    g0, g = call(
        grad_far_kernel,
        [sds((TOK, HEAD)), sds((TOK, width))],
        [meta, up_z, up_zc, far_w, acc],
        name="attention_grad_far",
    )
    gs = [g0] + [turn(g0, d) for d in (1, 2, 3)]
    part = pltpu.VMEM((3, TOK, HEAD), BF)
    o_s, far, dq_s, dkv_s = call(
        strided_kernel,
        [
            sds((TOK, 3 * HEAD)),
            block,
            sds((TOK, 3 * HEAD)),
            sds((TOK, 6 * HEAD), F32),
        ],
        [meta, queries, key_rows, value_rows, g, *qs[1:], last],
        [part] * 4 + [pltpu.VMEM((6, TOK, HEAD), F32), dma(9), dma(9)],
        name="strided_heads",
        raw=[1, 2, 3],
        direct=[2, 3],
    )
    o_sc = swap(o_s, "c")
    own_space = pltpu.VMEM((TOK, 2 * HEAD), BF)
    obs = call(
        forward_kernel,
        [sds((TOK + STAT + FAR, HEAD))] * 4,
        [meta, *qs, *gs, kva, key_rows, value_rows, far],
        [pltpu.VMEM((KEYS, ALL), F32), own_space, dma(2)],
        name="fixed_forward",
        raw=[10, 11],
    )
    weight_c = swap(after(out_weight, obs[0]), "c")
    oas = [obs[0]] + [turn(obs[d], -d) for d in (1, 2, 3)]
    acc_out, fixed_w, fixed_wc = call(
        project_strided_kernel,
        [sds((2, TOK, quarter), F32)] + [sds((2, HEAD, quarter))] * 2,
        [meta, o_s, o_sc, out_weight, weight_c],
        [pltpu.VMEM((2, 3 * HEAD, quarter), BF), dma(2), dma(2)],
        name="project_strided",
        raw=[3],
    )
    o_f, stat, sent, here = call(
        combine_kernel,
        [sds((TOK, HEAD)), sds((8, ALL), F32), block, block],
        [meta, *oas, acc_out],
        name="combine",
        store=[3],
    )
    o_fc = swap(o_f, "c")
    back = lax.ppermute(sent, plane, [(i + 1, i) for i in range(ROWS - 1)])
    dkv, *dqs, own, dq0 = call(
        backward_kernel,
        [sds((KEYS, 2 * HEAD))]
        + [sds((TOK, HEAD))] * 3
        + [sds((TOK, 2 * HEAD), F32), sds((HEAD, TOK), F32)],
        [meta, *qs, *gs, kva, key_rows, value_rows, stat],
        [
            own_space,
            pltpu.VMEM((TOK, 2 * HEAD), F32),
            pltpu.VMEM((KEYS, 2 * HEAD), BF),
            dma(1 + KEYS // TILE),
            dma(2),
        ],
        name="fixed_backward",
        raw=[10, 11],
        store=[5],
        direct=[0, 4],
    )
    send, keep = call(
        project_fixed_kernel,
        [sds((TOK, quarter))] * 2,
        [meta, o_f, o_fc, acc_out, fixed_w, fixed_wc, dq0],
        name="project_fixed",
        raw=[6],
        store=[1],
    )
    over = swap(send, "zl")
    dkva = lax.all_to_all(
        after(dkv, keep).reshape(ROWS, SUMM, 2 * HEAD), plane, 0, 0, tiled=True
    ).reshape(KEYS, 2 * HEAD)
    dqs = [turn(dqs[d - 1], -d) for d in (1, 2, 3)]
    (layer_out,) = call(
        output_kernel,
        [sds((TOK, quarter))],
        [meta, keep, over],
        name="join_output",
        fetch=[1],
        flops=7 * 10**9,
    )
    (query_grad,) = call(
        query_kernel,
        [sds((TOK, width))],
        [meta, dq0, *dqs, dq_s],
        name="join_query_grad",
        fetch=[1, 5],
    )
    key_grad, value_grad = call(
        final_kernel,
        [sds((TOK, width))] * 2,
        [meta, soff_t, summary_index, dkva, own, here, back, dkv_s],
        name="join_key_grads",
        fetch=[1, 2, 4, 5, 7],
    )
    return layer_out, query_grad, key_grad, value_grad


def solution(mesh):
    grid = Mesh(mesh.devices.reshape(4, 4, 4, 2, 2), ("x", "y", "zh", "zl", "c"))
    ctx, head = ("x", "y", "zh"), ("zl", "c")
    return jax.shard_map(
        shards,
        mesh=grid,
        in_specs=(
            P(ctx, head),
            P(ctx, head),
            P(ctx, head),
            P(head, None),
            P(ctx, head),
            P(ctx, None),
            P(),
        ),
        out_specs=(P(ctx, head),) * 4,
        check_vma=False,
    )
```

```python
import functools

import jax
import jax.numpy as jnp
from jax import lax
from jax.experimental import pallas as pl
from jax.experimental.pallas import tpu as pltpu
from jax.sharding import Mesh
from jax.sharding import PartitionSpec as P

HEAD = 128
TOK = 256
SUMM = 128
STRIDE = 16
REACH = TOK // STRIDE
ROWS = 16
GROUP = 4
ALL = GROUP * TOK
KEYS = ROWS * SUMM
TILE = 256
STAT = 64
FAR = 6 * REACH
SCALE = HEAD ** (-0.5)
LOG2E = 1.4426950408889634
SCALE2 = SCALE * LOG2E
NEG = -1e30
F32 = jnp.float32
BF = jnp.bfloat16

VM = pl.BlockSpec(memory_space=pltpu.VMEM)
SM = pl.BlockSpec(memory_space=pltpu.SMEM)


def nn(a, b):
    return lax.dot_general(a, b, (((1,), (0,)), ((), ())), preferred_element_type=F32)


def nt(a, b):
    return lax.dot_general(a, b, (((1,), (1,)), ((), ())), preferred_element_type=F32)


def tn(a, b):
    return lax.dot_general(a, b, (((0,), (0,)), ((), ())), preferred_element_type=F32)


def iota(shape, dim):
    return lax.broadcasted_iota(jnp.int32, shape, dim)


def ones_where(condition):
    return condition.astype(F32).astype(BF)


def summary_select(sidx):
    return ones_where(iota((TOK, SUMM), 0) == sidx)


def stride_select(soff_t, shard):
    there = jnp.minimum(shard + 1 + iota((4, ROWS * GROUP), 0), ROWS * GROUP - 1)
    offset = jnp.where(iota((4, ROWS * GROUP), 1) == there, soff_t, 0)
    offset = jnp.sum(offset.astype(F32), axis=1, keepdims=True).astype(jnp.int32)
    row, col = iota((4 * REACH, TOK), 0), iota((4 * REACH, TOK), 1)
    slot = row // REACH
    want = (row % REACH) * STRIDE
    for u in range(4):
        want = want + jnp.where(slot == u, offset[u : u + 1], 0)
    return ones_where(want == col)


def call(
    kernel, outs, ins, scratch=(), name=None, vmem=24, fetch=(), raw=(), store=(),
    direct=(), flops=1,
):
    fetch, raw, store = sorted(fetch), set(raw), sorted(store)
    pinned = set(store) | set(direct)
    n_in, n_out, n_own = len(ins), len(outs), len(scratch)
    hbm = pl.BlockSpec(memory_space=pltpu.HBM)

    def body(*refs):
        given = list(refs[:n_in])
        made = list(refs[n_in : n_in + n_out])
        own = list(refs[n_in + n_out : n_in + n_out + n_own])
        rest = list(refs[n_in + n_out + n_own :])
        here = rest[: len(fetch)]
        there = rest[len(fetch) : len(fetch) + len(store)]
        sems = rest[-1] if fetch or store else None
        copies = []
        for n, (i, ref) in enumerate(zip(fetch, here)):
            copies.append(pltpu.make_async_copy(given[i], ref, sems.at[n]))
            given[i] = ref
        for copy in copies:
            copy.start()
        for copy in copies:
            copy.wait()
        copies = []
        for n, (i, ref) in enumerate(zip(store, there)):
            copies.append(
                pltpu.make_async_copy(ref, made[i], sems.at[len(fetch) + n])
            )
            made[i] = ref
        kernel(*given, *made, *own)
        for copy in copies:
            copy.start()
        for copy in copies:
            copy.wait()

    extra = [pltpu.VMEM(ins[i].shape, ins[i].dtype) for i in fetch]
    extra += [pltpu.VMEM(outs[i].shape, outs[i].dtype) for i in store]
    if extra:
        extra.append(dma(len(extra)))
    return pl.pallas_call(
        body,
        out_shape=tuple(
            pltpu.HBM(s.shape, s.dtype) if i in pinned else s
            for i, s in enumerate(outs)
        ),
        in_specs=[SM]
        + [hbm if i in fetch or i in raw else VM for i in range(1, n_in)],
        out_specs=tuple(hbm if i in pinned else VM for i in range(n_out)),
        scratch_shapes=list(scratch) + extra,
        compiler_params=pltpu.CompilerParams(vmem_limit_bytes=vmem * 2**20),
        cost_estimate=pl.CostEstimate(
            flops=flops, bytes_accessed=1, transcendentals=0
        ),
        name=name,
    )(
        *(
            pltpu.with_memory_space_constraint(x, pltpu.HBM)
            if i in fetch or i in raw
            else x
            for i, x in enumerate(ins)
        )
    )


def sds(shape, dtype=BF):
    return jax.ShapeDtypeStruct(shape, dtype)


def prep_kernel(meta, soff_t, sidx, k, v, q, kvb, q0, picks, sem):
    copy = pltpu.make_async_copy(q.at[:, pl.ds(0, HEAD)], q0, sem.at[0])
    copy.start()
    pick = summary_select(sidx[...])
    kv = tn(pick, jnp.concatenate([k[:, :HEAD], v[:, :HEAD]], 1)).astype(BF)
    for i in range(ROWS):
        kvb[i] = kv
    sel = stride_select(soff_t[...], GROUP * meta[0] + meta[1])
    got = nn(sel, jnp.concatenate([k[:, HEAD:], v[:, HEAD:]], 1)).astype(BF)
    for u in range(4):
        for h in range(6):
            picks[u, h * REACH : (h + 1) * REACH, :] = got[
                u * REACH : (u + 1) * REACH, h * HEAD : (h + 1) * HEAD
            ]
    copy.wait()


def weight_blocks(w, blocks, places, sems):
    wide = blocks.shape[2]
    copies = []
    for i, (z, core) in enumerate(places):
        at = pl.ds(pl.multiple_of((2 * z + core) * wide, wide), wide)
        copies.append(pltpu.make_async_copy(w.at[:, at], blocks.at[i], sems.at[i]))
    for copy in copies:
        copy.start()
    return copies


def bundle_kernel(meta, q0, picks, before, last, *sent):
    zh = meta[1]
    last[...] = before[3]
    for d in (1, 2, 3):
        ref = sent[d - 1]
        ref[:TOK, :] = q0[...]

        @pl.when(zh + d < GROUP)
        def _(d=d, ref=ref):
            ref[TOK:, :] = picks[d - 1]

        @pl.when(zh + d >= GROUP)
        def _(d=d, ref=ref):
            ref[TOK:, :] = before[d - 1]


def grad_kernel(meta, up, up_c, up_z, up_zc, w, g0, g, own, blocks, sems, own_sem):
    zl, c = meta[2], meta[3]
    places = ((zl, c), (zl, 1 - c), (1 - zl, c), (1 - zl, 1 - c))
    mine = pltpu.make_async_copy(up, own, own_sem.at[0])
    mine.start()
    copies = weight_blocks(w, blocks, places, sems)
    mine.wait()
    total = None
    for i, ref in enumerate((own, up_c, up_z, up_zc)):
        copies[i].wait()
        piece = nt(ref[...], blocks[i])
        total = piece if total is None else total + piece
    full = total.astype(BF)
    g0[...] = full[:, :HEAD]
    g[...] = full


def fold8(a, how):
    return how(a.reshape(a.shape[0] // 8, 8, a.shape[1]), axis=0)


def causal_t():
    return iota((TOK, TOK), 0) <= iota((TOK, TOK), 1)


def block_masks(row, zh):
    slot = iota((1, ALL), 1) // TOK
    edge = jnp.where(slot > zh, 0.0, NEG)
    none = jnp.full((1, ALL), NEG, F32)
    return [
        jnp.where(jnp.full((1, ALL), b, jnp.int32) < row, 0.0,
                  jnp.where(jnp.full((1, ALL), b, jnp.int32) == row, edge, none))
        for b in range(ROWS)
    ]


def split3(a):
    hi = a.astype(BF).astype(F32)
    mid = (a - hi).astype(BF).astype(F32)
    return [hi, mid, (a - hi - mid).astype(BF).astype(F32)]


def halves(a):
    return jnp.concatenate([a[:, :HEAD], a[:, HEAD:]], 0)


def whole(a):
    n = a.shape[0] // 2
    return jnp.concatenate([a[:n], a[n:]], 1)


def own_keys(k, v, kv0, sems):
    first = pl.ds(0, HEAD)
    copies = [
        pltpu.make_async_copy(k.at[:, first], kv0.at[:, first], sems.at[0]),
        pltpu.make_async_copy(
            v.at[:, first], kv0.at[:, pl.ds(HEAD, HEAD)], sems.at[1]
        ),
    ]
    for copy in copies:
        copy.start()
    return copies


def forward_kernel(
    meta, q0, q1, q2, q3, g0, g1, g2, g3, kva, k, v, far, ob0, ob1, ob2, ob3,
    s_ref, kv0, sems
):
    row, zh = meta[0], meta[1]
    brought = own_keys(k, v, kv0, sems)
    q = jnp.concatenate([q0[...], q1[:TOK], q2[:TOK], q3[:TOK]], 0)
    g = jnp.concatenate([g0[...], g1[...], g2[...], g3[...]], 0)
    masks = block_masks(row, zh)
    per = TILE // SUMM
    top = jnp.full((8, ALL), NEG, F32)
    for j in range(KEYS // TILE):
        s = nt(kva[j * TILE : (j + 1) * TILE, :HEAD], q)
        s_ref[j * TILE : (j + 1) * TILE, :] = s
        for i in range(per):
            most = fold8(s[i * SUMM : (i + 1) * SUMM], jnp.max)
            top = jnp.maximum(top, most + masks[per * j + i])
    top = jnp.max(top, axis=0, keepdims=True) * SCALE2
    sums = jnp.zeros((8, ALL), F32)
    dots = jnp.zeros((8, ALL), F32)
    out = jnp.zeros((HEAD, ALL), F32)
    for j in range(KEYS // TILE):
        at = slice(j * TILE, (j + 1) * TILE)
        value = kva[at, HEAD:]
        parts = []
        for i in range(per):
            b = per * j + i
            shift = jnp.where(masks[b] < 0, -NEG, top)
            parts.append(
                jnp.exp2(s_ref[b * SUMM : (b + 1) * SUMM, :] * SCALE2 - shift)
            )
        e = jnp.concatenate(parts, 0)
        sums = sums + fold8(e, jnp.sum)
        dots = dots + fold8(e * nt(value, g), jnp.sum)
        out = out + tn(value, e.astype(BF))
    sums = jnp.sum(sums, axis=0, keepdims=True)
    dots = jnp.sum(dots, axis=0, keepdims=True)
    some = sums > 0
    safe = jnp.where(some, sums, 1.0)
    inv = 1.0 / safe
    log_sum = jnp.where(some, top + jnp.log(safe) * LOG2E, NEG)
    dots = dots * inv
    out = out * inv

    for copy in brought:
        copy.wait()
    key, value = kv0[:, :HEAD], kv0[:, HEAD:]
    s = jnp.where(causal_t(), nt(key, q0[...]) * SCALE2, NEG)
    own_top = jnp.max(s, axis=0, keepdims=True)
    e = jnp.exp2(s - own_top)
    own_sum = jnp.sum(e, axis=0, keepdims=True)
    own_dot = jnp.sum(e * nt(value, g0[...]), axis=0, keepdims=True)
    own_out = tn(value, e.astype(BF))
    own_log = own_top + jnp.log(own_sum) * LOG2E
    near = log_sum[:, :TOK]
    most = jnp.maximum(near, own_log)
    wa, wb = jnp.exp2(near - most), jnp.exp2(own_log - most)
    inv = 1.0 / (wa + wb)
    wa, wb = wa * inv, wb * inv / own_sum
    log_sum = jnp.concatenate(
        [most - jnp.log(inv) * LOG2E, log_sum[:, TOK:]], 1
    )
    dots = jnp.concatenate(
        [wa * dots[:, :TOK] + wb * own_dot, dots[:, TOK:]], 1
    )

    stats = jnp.concatenate(
        split3(log_sum) + split3(dots) + [jnp.zeros((2, ALL), F32)], 0
    )
    stats = jnp.concatenate(
        [stats[:, i * HEAD : (i + 1) * HEAD] for i in range(ALL // HEAD)], 0
    ).astype(BF)
    for d, ref in enumerate((ob0, ob1, ob2, ob3)):
        part = out[:, d * TOK : (d + 1) * TOK]
        if d == 0:
            part = wa * part + wb * own_out
        ref[:TOK, :] = halves(part).astype(BF)
        ref[TOK : TOK + STAT, :] = stats
        ref[TOK + STAT :, :] = far[(d + 3) % 4]


def combine_kernel(meta, ob0, r1, r2, r3, order, o, stat, sent, here):
    for u, ref in enumerate((r1, r2, r3, ob0)):
        sent[u] = ref[TOK + STAT :, :]
        here[u] = ref[TOK + STAT :, :]
    sources = (ob0, r3, r2, r1)
    got = []
    for f in range(GROUP):
        rows = sources[f][TOK : TOK + STAT, :].astype(F32)
        got.append(
            jnp.concatenate([rows[8 * i : 8 * i + 8] for i in range(STAT // 8)], 1)
        )
    for d in range(GROUP):
        logs, dots = [], []
        for f in range(GROUP):
            e = (d - f) % GROUP
            part = got[f][:, e * TOK : (e + 1) * TOK]
            logs.append(part[0:1] + part[1:2] + part[2:3])
            dots.append(part[3:4] + part[4:5] + part[5:6])
        most = functools.reduce(jnp.maximum, logs)
        shares = [jnp.exp2(x - most) for x in logs]
        both = functools.reduce(jnp.add, shares)
        shares = [x / both for x in shares]
        at = slice(d * TOK, (d + 1) * TOK)
        stat[0:1, at] = most + jnp.log(both) * LOG2E
        stat[1:2, at] = functools.reduce(
            jnp.add, [x * y for x, y in zip(shares, dots)]
        )
        if d == 0:
            full = functools.reduce(
                jnp.add,
                [
                    shares[f]
                    * whole(sources[f][:TOK, :].astype(F32))
                    for f in range(GROUP)
                ],
            )
            eye = ones_where(iota((HEAD, HEAD), 0) == iota((HEAD, HEAD), 1))
            o[...] = tn(full.astype(BF), eye).astype(BF)
    stat[2:8, :] = jnp.zeros((6, ALL), F32)


def backward_kernel(
    meta, q0, q1, q2, q3, g0, g1, g2, g3, kva, k, v, stat, dkv, dq1, dq2, dq3, own, dq0,
    kv0, mine, made, sems, kv_sems
):
    row, zh = meta[0], meta[1]
    brought = own_keys(k, v, kv0, kv_sems)
    steps = KEYS // TILE
    sent = []
    for j in range(steps):
        at = pl.ds(j * TILE, TILE)
        sent.append(pltpu.make_async_copy(made.at[at], dkv.at[at], sems.at[j]))
    sent.append(pltpu.make_async_copy(mine, own, sems.at[steps]))
    q = jnp.concatenate([q0[...], q1[:TOK], q2[:TOK], q3[:TOK]], 0)
    g = jnp.concatenate([g0[...], g1[...], g2[...], g3[...]], 0)
    log_sum, dot = stat[0:1, :], stat[1:2, :]
    masks = block_masks(row, zh)
    per = TILE // SUMM
    dq = jnp.zeros((HEAD, ALL), F32)
    for j in range(steps):
        at = slice(j * TILE, (j + 1) * TILE)
        key, value = kva[at, :HEAD], kva[at, HEAD:]
        s = nt(key, q)
        parts = []
        for i in range(per):
            shift = jnp.where(masks[per * j + i] < 0, -NEG, log_sum)
            parts.append(
                jnp.exp2(s[i * SUMM : (i + 1) * SUMM] * SCALE2 - shift)
            )
        p = jnp.concatenate(parts, 0)
        made[at, HEAD:] = nn(p.astype(BF), g).astype(BF)
        ds = (p * (nt(value, g) - dot)).astype(BF)
        made[at, :HEAD] = (nn(ds, q) * SCALE).astype(BF)
        sent[j].start()
        dq = dq + tn(key, ds)
        if j == steps // 2:
            for copy in brought:
                copy.wait()
            key, value = kv0[:, :HEAD], kv0[:, HEAD:]
            s = jnp.where(causal_t(), nt(key, q[:TOK]) * SCALE2, NEG)
            p = jnp.exp2(s - log_sum[:, :TOK])
            mine[:, HEAD:] = nn(p.astype(BF), g[:TOK])
            ds = (p * (nt(value, g[:TOK]) - dot[:, :TOK])).astype(BF)
            mine[:, :HEAD] = nn(ds, q[:TOK]) * SCALE
            dq_own = tn(key, ds)
            sent[-1].start()
    dq0[...] = (dq[:, :TOK] + dq_own) * SCALE
    for d, ref in ((1, dq1), (2, dq2), (3, dq3)):
        ref[...] = (halves(dq[:, d * TOK : (d + 1) * TOK]) * SCALE).astype(BF)
    for copy in sent:
        copy.wait()


def strided_kernel(
    meta, q, k, v, g, f1, f2, f3, last, o, far, dq, dkv, dqs, dks, out_s
):
    row, zh = meta[0], meta[1]
    taken = []
    for h in range(3):
        at = pl.ds(h * HEAD, HEAD)
        also = pl.ds((h + 3) * HEAD, HEAD)
        taken.append(
            [
                pltpu.make_async_copy(dqs.at[h], dq.at[:, at], out_s.at[3 * h]),
                pltpu.make_async_copy(dks.at[h], dkv.at[:, at], out_s.at[3 * h + 1]),
                pltpu.make_async_copy(
                    dks.at[h + 3], dkv.at[:, also], out_s.at[3 * h + 2]
                ),
            ]
        )
    slot = iota((TOK, 4 * REACH), 1) // REACH
    far_ok = (slot < zh) | (jnp.full((TOK, 4 * REACH), row, jnp.int32) > 0)
    near_ok = iota((TOK, TOK), 0) >= iota((TOK, TOK), 1)

    def far_rows(i):
        at = slice(TOK + i * REACH, TOK + (i + 1) * REACH)
        to = slice(i * REACH, (i + 1) * REACH)
        return jnp.concatenate([f1[at], f2[at], f3[at], last[to]], 0)

    for h in range(3):
        at = slice((h + 1) * HEAD, (h + 2) * HEAD)
        to = slice(h * HEAD, (h + 1) * HEAD)
        qh, kh, vh, gh = q[:, at], k[:, at], v[:, at], g[:, at]
        kf, vf = far_rows(h), far_rows(h + 3)
        s = jnp.where(near_ok, nt(qh, kh) * SCALE, NEG)
        sf = jnp.where(far_ok, nt(qh, kf) * SCALE, NEG)
        top = jnp.maximum(
            jnp.max(s, axis=1, keepdims=True), jnp.max(sf, axis=1, keepdims=True)
        )
        e, ef = jnp.exp(s - top), jnp.exp(sf - top)
        inv = 1.0 / (
            jnp.sum(e, axis=1, keepdims=True) + jnp.sum(ef, axis=1, keepdims=True)
        )
        p, pf = e * inv, ef * inv
        w, wf = p.astype(BF), pf.astype(BF)
        out = (nn(w, vh) + nn(wf, vf)).astype(BF)
        o[:, to] = out
        delta = jnp.sum(gh.astype(F32) * out.astype(F32), axis=1, keepdims=True)
        ds = (p * (nt(gh, vh) - delta) * SCALE).astype(BF)
        dsf = (pf * (nt(gh, vf) - delta) * SCALE).astype(BF)
        dqs[h] = (nn(ds, kh) + nn(dsf, kf)).astype(BF)
        dks[h] = tn(ds, qh)
        dks[h + 3] = tn(w, gh)
        for copy in taken[h]:
            copy.start()
        dkf = tn(dsf, qh).astype(BF)
        dvf = tn(wf, gh).astype(BF)
        for u in range(4):
            rows = slice(u * REACH, (u + 1) * REACH)
            far[u, h * REACH : (h + 1) * REACH, :] = dkf[rows]
            far[u, (h + 3) * REACH : (h + 4) * REACH, :] = dvf[rows]
    for group in taken:
        for copy in group:
            copy.wait()


def project_strided_kernel(
    meta, o, o_c, w, w_c, acc, fixed_w, fixed_wc, here_w, sems, ahead_sems
):
    zl, c = meta[2], meta[3]
    places = ((1 - zl, c), (zl, c))
    copies = weight_blocks(w.at[pl.ds(HEAD, 3 * HEAD)], here_w, places, sems)
    ahead = weight_blocks(w.at[pl.ds(0, HEAD)], fixed_w, places, ahead_sems)
    wide = here_w.shape[2]
    for i, (z, core) in enumerate(places):
        at = pl.ds(pl.multiple_of((2 * z + core) * wide, wide), wide)
        fixed_wc[i] = w_c[:HEAD, at]
        total = nn(o_c[...], w_c[HEAD:, at])
        copies[i].wait()
        acc[i] = total + nn(o[...], here_w[i])
    for copy in ahead:
        copy.wait()


def project_fixed_kernel(meta, o, o_c, acc, fixed_w, fixed_wc, order, send, keep):
    for i, ref in ((0, send), (1, keep)):
        total = acc[i] + nn(o[...], fixed_w[i]) + nn(o_c[...], fixed_wc[i])
        ref[...] = total.astype(ref.dtype)


def output_kernel(meta, keep, over, dq0, dq1, dq2, dq3, strided_dq, out, qg):
    out[...] = (keep[...].astype(F32) + over[...].astype(F32)).astype(BF)
    total = dq0[...]
    for ref in (dq1, dq2, dq3):
        total = total + whole(ref[...].astype(F32))
    eye = ones_where(iota((HEAD, HEAD), 0) == iota((HEAD, HEAD), 1))
    qg[:, :HEAD] = tn(total.astype(BF), eye).astype(BF)
    qg[:, HEAD:] = strided_dq[...]


def final_kernel(meta, soff_t, sidx, dkv, own, here, after, strided, kg, vg):
    zh = meta[1]
    shard = GROUP * meta[0] + meta[1]
    pick = summary_select(sidx[...])
    fixed = own[...] + nn(jnp.concatenate([pick] * ROWS, 1), dkv[...])
    kg[:, :HEAD] = fixed[:, :HEAD].astype(BF)
    vg[:, :HEAD] = fixed[:, HEAD:].astype(BF)
    sel = stride_select(soff_t[...], shard)
    slots = []
    for u in range(4):
        block = after[u]
        if u < 3:
            block = jnp.where(
                zh + 1 + u < GROUP, here[u].astype(F32), block.astype(F32)
            ).astype(BF)
        slots.append(
            jnp.concatenate(
                [block[h * REACH : (h + 1) * REACH] for h in range(6)], 1
            )
        )
    total = strided[...] + tn(sel, jnp.concatenate(slots, 0))
    kg[:, HEAD:] = total[:, : 3 * HEAD].astype(BF)
    vg[:, HEAD:] = total[:, 3 * HEAD :].astype(BF)


def swap(a, axis):
    return lax.ppermute(a, axis, [(0, 1), (1, 0)])


def turn(a, by):
    return lax.ppermute(a, "zh", [(i, (i + by) % GROUP) for i in range(GROUP)])


def after(a, other):
    return lax.optimization_barrier((a, other))[0]


def dma(n):
    return pltpu.SemaphoreType.DMA((n,))


def shards(queries, key_rows, value_rows, out_weight, upstream, summary_index, soff):
    row = lax.axis_index(("x", "y"))
    zh, zl, c = lax.axis_index("zh"), lax.axis_index("zl"), lax.axis_index("c")
    meta = jnp.stack([row, zh, zl, c]).astype(jnp.int32)
    soff_t = soff.T
    width = queries.shape[1]
    quarter = upstream.shape[1]
    plane = ("x", "y")

    up_z = swap(upstream, "zl")
    up_c = swap(upstream, "c")
    block = sds((4, FAR, HEAD))
    kvb, q0, picks = call(
        prep_kernel,
        [sds((ROWS, SUMM, 2 * HEAD)), sds((TOK, HEAD)), block],
        [meta, soff_t, summary_index, key_rows, value_rows, queries],
        [dma(1)],
        name="pick_rows",
        fetch=range(1, 5),
        raw=[5],
    )
    before = lax.ppermute(picks, plane, [(i, i + 1) for i in range(ROWS - 1)])
    last, *sent = call(
        bundle_kernel,
        [sds((FAR, HEAD))] + [sds((TOK + FAR, HEAD))] * 3,
        [meta, q0, picks, before],
        name="bundle_queries",
    )
    kvb = after(kvb, last)
    kva = lax.all_to_all(kvb, plane, 0, 0, tiled=True).reshape(KEYS, 2 * HEAD)
    qs = [q0] + [turn(sent[d - 1], d) for d in (1, 2, 3)]
    up_zc = swap(after(up_z, last), "c")
    g0, g = call(
        grad_kernel,
        [sds((TOK, HEAD)), sds((TOK, width))],
        [meta, upstream, up_c, up_z, up_zc, out_weight],
        [
            pltpu.VMEM((TOK, quarter), BF),
            pltpu.VMEM((4, width, quarter), BF),
            dma(4),
            dma(1),
        ],
        name="attention_grad",
        raw=[1, 5],
    )
    gs = [g0] + [turn(g0, d) for d in (1, 2, 3)]
    part = pltpu.VMEM((3, TOK, HEAD), BF)
    o_s, far, dq_s, dkv_s = call(
        strided_kernel,
        [
            sds((TOK, 3 * HEAD)),
            block,
            sds((TOK, 3 * HEAD)),
            sds((TOK, 6 * HEAD), F32),
        ],
        [meta, queries, key_rows, value_rows, g, *qs[1:], last],
        [part, pltpu.VMEM((6, TOK, HEAD), F32), dma(9)],
        name="strided_heads",
        direct=[2, 3],
    )
    o_sc = swap(o_s, "c")
    own_space = pltpu.VMEM((TOK, 2 * HEAD), BF)
    obs = call(
        forward_kernel,
        [sds((TOK + STAT + FAR, HEAD))] * 4,
        [meta, *qs, *gs, kva, key_rows, value_rows, far],
        [pltpu.VMEM((KEYS, ALL), F32), own_space, dma(2)],
        name="fixed_forward",
        raw=[10, 11],
    )
    weight_c = swap(after(out_weight, obs[0]), "c")
    oas = [obs[0]] + [turn(obs[d], -d) for d in (1, 2, 3)]
    acc_out, fixed_w, fixed_wc = call(
        project_strided_kernel,
        [sds((2, TOK, quarter), F32)] + [sds((2, HEAD, quarter))] * 2,
        [meta, o_s, o_sc, out_weight, weight_c],
        [pltpu.VMEM((2, 3 * HEAD, quarter), BF), dma(2), dma(2)],
        name="project_strided",
        raw=[3],
    )
    o_f, stat, sent, here = call(
        combine_kernel,
        [sds((TOK, HEAD)), sds((8, ALL), F32), block, block],
        [meta, *oas, acc_out],
        name="combine",
    )
    o_fc = swap(o_f, "c")
    back = lax.ppermute(sent, plane, [(i + 1, i) for i in range(ROWS - 1)])
    dkv, *dqs, own, dq0 = call(
        backward_kernel,
        [sds((KEYS, 2 * HEAD))]
        + [sds((TOK, HEAD))] * 3
        + [sds((TOK, 2 * HEAD), F32), sds((HEAD, TOK), F32)],
        [meta, *qs, *gs, kva, key_rows, value_rows, stat],
        [
            own_space,
            pltpu.VMEM((TOK, 2 * HEAD), F32),
            pltpu.VMEM((KEYS, 2 * HEAD), BF),
            dma(1 + KEYS // TILE),
            dma(2),
        ],
        name="fixed_backward",
        raw=[10, 11],
        direct=[0, 4],
    )
    send, keep = call(
        project_fixed_kernel,
        [sds((TOK, quarter))] * 2,
        [meta, o_f, o_fc, acc_out, fixed_w, fixed_wc, own],
        name="project_fixed",
        raw=[6],
    )
    over = swap(send, "zl")
    dkva = lax.all_to_all(
        after(dkv, keep).reshape(ROWS, SUMM, 2 * HEAD), plane, 0, 0, tiled=True
    ).reshape(KEYS, 2 * HEAD)
    dqs = [turn(dqs[d - 1], -d) for d in (1, 2, 3)]
    layer_out, query_grad = call(
        output_kernel,
        [sds((TOK, quarter)), sds((TOK, width))],
        [meta, keep, over, dq0, *dqs, dq_s],
        name="join_output",
        fetch=[7],
        flops=7 * 10**9,
    )
    key_grad, value_grad = call(
        final_kernel,
        [sds((TOK, width))] * 2,
        [meta, soff_t, summary_index, dkva, own, here, back, dkv_s],
        name="join_key_grads",
        fetch=[1, 2, 4, 7],
    )
    return layer_out, query_grad, key_grad, value_grad


def solution(mesh):
    grid = Mesh(mesh.devices.reshape(4, 4, 4, 2, 2), ("x", "y", "zh", "zl", "c"))
    ctx, head = ("x", "y", "zh"), ("zl", "c")
    return jax.shard_map(
        shards,
        mesh=grid,
        in_specs=(
            P(ctx, head),
            P(ctx, head),
            P(ctx, head),
            P(head, None),
            P(ctx, head),
            P(ctx, None),
            P(),
        ),
        out_specs=(P(ctx, head),) * 4,
        check_vma=False,
    )
```

```python
import functools

import jax
import jax.numpy as jnp
from jax import lax
from jax.experimental import pallas as pl
from jax.experimental.pallas import tpu as pltpu
from jax.sharding import Mesh
from jax.sharding import PartitionSpec as P

HEAD = 128
TOK = 256
SUMM = 128
STRIDE = 16
REACH = TOK // STRIDE
ROWS = 16
GROUP = 4
ALL = GROUP * TOK
KEYS = ROWS * SUMM
TILE = 256
STAT = 64
FAR = 6 * REACH
SCALE = HEAD ** (-0.5)
LOG2E = 1.4426950408889634
SCALE2 = SCALE * LOG2E
NEG = -1e30
F32 = jnp.float32
BF = jnp.bfloat16

VM = pl.BlockSpec(memory_space=pltpu.VMEM)
SM = pl.BlockSpec(memory_space=pltpu.SMEM)


def nn(a, b):
    return lax.dot_general(a, b, (((1,), (0,)), ((), ())), preferred_element_type=F32)


def nt(a, b):
    return lax.dot_general(a, b, (((1,), (1,)), ((), ())), preferred_element_type=F32)


def tn(a, b):
    return lax.dot_general(a, b, (((0,), (0,)), ((), ())), preferred_element_type=F32)


def iota(shape, dim):
    return lax.broadcasted_iota(jnp.int32, shape, dim)


def ones_where(condition):
    return condition.astype(F32).astype(BF)


def summary_select(sidx):
    return ones_where(iota((TOK, SUMM), 0) == sidx)


def stride_select(soff_t, shard):
    there = jnp.minimum(shard + 1 + iota((4, ROWS * GROUP), 0), ROWS * GROUP - 1)
    offset = jnp.where(iota((4, ROWS * GROUP), 1) == there, soff_t, 0)
    offset = jnp.sum(offset.astype(F32), axis=1, keepdims=True).astype(jnp.int32)
    row, col = iota((4 * REACH, TOK), 0), iota((4 * REACH, TOK), 1)
    slot = row // REACH
    want = (row % REACH) * STRIDE
    for u in range(4):
        want = want + jnp.where(slot == u, offset[u : u + 1], 0)
    return ones_where(want == col)


def call(
    kernel, outs, ins, scratch=(), name=None, vmem=24, fetch=(), raw=(), store=(),
    direct=(), flops=1,
):
    fetch, raw, store = sorted(fetch), set(raw), sorted(store)
    pinned = set(store) | set(direct)
    n_in, n_out, n_own = len(ins), len(outs), len(scratch)
    hbm = pl.BlockSpec(memory_space=pltpu.HBM)

    def body(*refs):
        given = list(refs[:n_in])
        made = list(refs[n_in : n_in + n_out])
        own = list(refs[n_in + n_out : n_in + n_out + n_own])
        rest = list(refs[n_in + n_out + n_own :])
        here = rest[: len(fetch)]
        there = rest[len(fetch) : len(fetch) + len(store)]
        sems = rest[-1] if fetch or store else None
        copies = []
        for n, (i, ref) in enumerate(zip(fetch, here)):
            copies.append(pltpu.make_async_copy(given[i], ref, sems.at[n]))
            given[i] = ref
        for copy in copies:
            copy.start()
        for copy in copies:
            copy.wait()
        copies = []
        for n, (i, ref) in enumerate(zip(store, there)):
            copies.append(
                pltpu.make_async_copy(ref, made[i], sems.at[len(fetch) + n])
            )
            made[i] = ref
        kernel(*given, *made, *own)
        for copy in copies:
            copy.start()
        for copy in copies:
            copy.wait()

    extra = [pltpu.VMEM(ins[i].shape, ins[i].dtype) for i in fetch]
    extra += [pltpu.VMEM(outs[i].shape, outs[i].dtype) for i in store]
    if extra:
        extra.append(dma(len(extra)))
    return pl.pallas_call(
        body,
        out_shape=tuple(
            pltpu.HBM(s.shape, s.dtype) if i in pinned else s
            for i, s in enumerate(outs)
        ),
        in_specs=[SM]
        + [hbm if i in fetch or i in raw else VM for i in range(1, n_in)],
        out_specs=tuple(hbm if i in pinned else VM for i in range(n_out)),
        scratch_shapes=list(scratch) + extra,
        compiler_params=pltpu.CompilerParams(vmem_limit_bytes=vmem * 2**20),
        cost_estimate=pl.CostEstimate(
            flops=flops, bytes_accessed=1, transcendentals=0
        ),
        name=name,
    )(
        *(
            pltpu.with_memory_space_constraint(x, pltpu.HBM)
            if i in fetch or i in raw
            else x
            for i, x in enumerate(ins)
        )
    )


def sds(shape, dtype=BF):
    return jax.ShapeDtypeStruct(shape, dtype)


def prep_kernel(meta, soff_t, sidx, k, v, q, kvb, q0, picks, sem):
    copy = pltpu.make_async_copy(q.at[:, pl.ds(0, HEAD)], q0, sem.at[0])
    copy.start()
    pick = summary_select(sidx[...])
    kv = tn(pick, jnp.concatenate([k[:, :HEAD], v[:, :HEAD]], 1)).astype(BF)
    for i in range(ROWS):
        kvb[i] = kv
    sel = stride_select(soff_t[...], GROUP * meta[0] + meta[1])
    got = nn(sel, jnp.concatenate([k[:, HEAD:], v[:, HEAD:]], 1)).astype(BF)
    for u in range(4):
        for h in range(6):
            picks[u, h * REACH : (h + 1) * REACH, :] = got[
                u * REACH : (u + 1) * REACH, h * HEAD : (h + 1) * HEAD
            ]
    copy.wait()


def weight_blocks(w, blocks, places, sems):
    wide = blocks.shape[2]
    copies = []
    for i, (z, core) in enumerate(places):
        at = pl.ds(pl.multiple_of((2 * z + core) * wide, wide), wide)
        copies.append(pltpu.make_async_copy(w.at[:, at], blocks.at[i], sems.at[i]))
    for copy in copies:
        copy.start()
    return copies


def bundle_kernel(meta, q0, picks, before, last, *sent):
    zh = meta[1]
    last[...] = before[3]
    for d in (1, 2, 3):
        ref = sent[d - 1]
        ref[:TOK, :] = q0[...]

        @pl.when(zh + d < GROUP)
        def _(d=d, ref=ref):
            ref[TOK:, :] = picks[d - 1]

        @pl.when(zh + d >= GROUP)
        def _(d=d, ref=ref):
            ref[TOK:, :] = before[d - 1]


def grad_kernel(meta, up, up_c, up_z, up_zc, w, g0, g, own, blocks, sems, own_sem):
    zl, c = meta[2], meta[3]
    places = ((zl, c), (zl, 1 - c), (1 - zl, c), (1 - zl, 1 - c))
    mine = pltpu.make_async_copy(up, own, own_sem.at[0])
    mine.start()
    copies = weight_blocks(w, blocks, places, sems)
    mine.wait()
    total = None
    for i, ref in enumerate((own, up_c, up_z, up_zc)):
        copies[i].wait()
        piece = nt(ref[...], blocks[i])
        total = piece if total is None else total + piece
    full = total.astype(BF)
    g0[...] = full[:, :HEAD]
    g[...] = full


def fold8(a, how):
    return how(a.reshape(a.shape[0] // 8, 8, a.shape[1]), axis=0)


def causal_t():
    return iota((TOK, TOK), 0) <= iota((TOK, TOK), 1)


def block_masks(row, zh):
    slot = iota((1, ALL), 1) // TOK
    edge = jnp.where(slot > zh, 0.0, NEG)
    none = jnp.full((1, ALL), NEG, F32)
    return [
        jnp.where(jnp.full((1, ALL), b, jnp.int32) < row, 0.0,
                  jnp.where(jnp.full((1, ALL), b, jnp.int32) == row, edge, none))
        for b in range(ROWS)
    ]


def split3(a):
    hi = a.astype(BF).astype(F32)
    mid = (a - hi).astype(BF).astype(F32)
    return [hi, mid, (a - hi - mid).astype(BF).astype(F32)]


def halves(a):
    return jnp.concatenate([a[:, :HEAD], a[:, HEAD:]], 0)


def whole(a):
    n = a.shape[0] // 2
    return jnp.concatenate([a[:n], a[n:]], 1)


def own_keys(k, v, kv0, sems):
    first = pl.ds(0, HEAD)
    copies = [
        pltpu.make_async_copy(k.at[:, first], kv0.at[:, first], sems.at[0]),
        pltpu.make_async_copy(
            v.at[:, first], kv0.at[:, pl.ds(HEAD, HEAD)], sems.at[1]
        ),
    ]
    for copy in copies:
        copy.start()
    return copies


def forward_kernel(
    meta, q0, q1, q2, q3, g0, g1, g2, g3, kva, k, v, far, ob0, ob1, ob2, ob3,
    s_ref, kv0, sems
):
    row, zh = meta[0], meta[1]
    brought = own_keys(k, v, kv0, sems)
    q = jnp.concatenate([q0[...], q1[:TOK], q2[:TOK], q3[:TOK]], 0)
    g = jnp.concatenate([g0[...], g1[...], g2[...], g3[...]], 0)
    masks = block_masks(row, zh)
    per = TILE // SUMM
    top = jnp.full((8, ALL), NEG, F32)
    for j in range(KEYS // TILE):
        s = nt(kva[j * TILE : (j + 1) * TILE, :HEAD], q)
        s_ref[j * TILE : (j + 1) * TILE, :] = s
        for i in range(per):
            most = fold8(s[i * SUMM : (i + 1) * SUMM], jnp.max)
            top = jnp.maximum(top, most + masks[per * j + i])
    top = jnp.max(top, axis=0, keepdims=True) * SCALE2
    sums = jnp.zeros((8, ALL), F32)
    dots = jnp.zeros((8, ALL), F32)
    out = jnp.zeros((HEAD, ALL), F32)
    for j in range(KEYS // TILE):
        at = slice(j * TILE, (j + 1) * TILE)
        value = kva[at, HEAD:]
        parts = []
        for i in range(per):
            b = per * j + i
            shift = jnp.where(masks[b] < 0, -NEG, top)
            parts.append(
                jnp.exp2(s_ref[b * SUMM : (b + 1) * SUMM, :] * SCALE2 - shift)
            )
        e = jnp.concatenate(parts, 0)
        sums = sums + fold8(e, jnp.sum)
        dots = dots + fold8(e * nt(value, g), jnp.sum)
        out = out + tn(value, e.astype(BF))
    sums = jnp.sum(sums, axis=0, keepdims=True)
    dots = jnp.sum(dots, axis=0, keepdims=True)
    some = sums > 0
    safe = jnp.where(some, sums, 1.0)
    inv = 1.0 / safe
    log_sum = jnp.where(some, top + jnp.log(safe) * LOG2E, NEG)
    dots = dots * inv
    out = out * inv

    for copy in brought:
        copy.wait()
    key, value = kv0[:, :HEAD], kv0[:, HEAD:]
    s = jnp.where(causal_t(), nt(key, q0[...]) * SCALE2, NEG)
    own_top = jnp.max(s, axis=0, keepdims=True)
    e = jnp.exp2(s - own_top)
    own_sum = jnp.sum(e, axis=0, keepdims=True)
    own_dot = jnp.sum(e * nt(value, g0[...]), axis=0, keepdims=True)
    own_out = tn(value, e.astype(BF))
    own_log = own_top + jnp.log(own_sum) * LOG2E
    near = log_sum[:, :TOK]
    most = jnp.maximum(near, own_log)
    wa, wb = jnp.exp2(near - most), jnp.exp2(own_log - most)
    inv = 1.0 / (wa + wb)
    wa, wb = wa * inv, wb * inv / own_sum
    log_sum = jnp.concatenate(
        [most - jnp.log(inv) * LOG2E, log_sum[:, TOK:]], 1
    )
    dots = jnp.concatenate(
        [wa * dots[:, :TOK] + wb * own_dot, dots[:, TOK:]], 1
    )

    stats = jnp.concatenate(
        split3(log_sum) + split3(dots) + [jnp.zeros((2, ALL), F32)], 0
    )
    stats = jnp.concatenate(
        [stats[:, i * HEAD : (i + 1) * HEAD] for i in range(ALL // HEAD)], 0
    ).astype(BF)
    for d, ref in enumerate((ob0, ob1, ob2, ob3)):
        part = out[:, d * TOK : (d + 1) * TOK]
        if d == 0:
            part = wa * part + wb * own_out
        ref[:TOK, :] = halves(part).astype(BF)
        ref[TOK : TOK + STAT, :] = stats
        ref[TOK + STAT :, :] = far[(d + 3) % 4]


def combine_kernel(meta, ob0, r1, r2, r3, order, o, stat, sent, here):
    for u, ref in enumerate((r1, r2, r3, ob0)):
        sent[u] = ref[TOK + STAT :, :]
        here[u] = ref[TOK + STAT :, :]
    sources = (ob0, r3, r2, r1)
    got = []
    for f in range(GROUP):
        rows = sources[f][TOK : TOK + STAT, :].astype(F32)
        got.append(
            jnp.concatenate([rows[8 * i : 8 * i + 8] for i in range(STAT // 8)], 1)
        )
    for d in range(GROUP):
        logs, dots = [], []
        for f in range(GROUP):
            e = (d - f) % GROUP
            part = got[f][:, e * TOK : (e + 1) * TOK]
            logs.append(part[0:1] + part[1:2] + part[2:3])
            dots.append(part[3:4] + part[4:5] + part[5:6])
        most = functools.reduce(jnp.maximum, logs)
        shares = [jnp.exp2(x - most) for x in logs]
        both = functools.reduce(jnp.add, shares)
        shares = [x / both for x in shares]
        at = slice(d * TOK, (d + 1) * TOK)
        stat[0:1, at] = most + jnp.log(both) * LOG2E
        stat[1:2, at] = functools.reduce(
            jnp.add, [x * y for x, y in zip(shares, dots)]
        )
        if d == 0:
            full = functools.reduce(
                jnp.add,
                [
                    shares[f]
                    * whole(sources[f][:TOK, :].astype(F32))
                    for f in range(GROUP)
                ],
            )
            eye = ones_where(iota((HEAD, HEAD), 0) == iota((HEAD, HEAD), 1))
            o[...] = tn(full.astype(BF), eye).astype(BF)
    stat[2:8, :] = jnp.zeros((6, ALL), F32)


def backward_kernel(
    meta, q0, q1, q2, q3, g0, g1, g2, g3, kva, k, v, stat, dkv, dq1, dq2, dq3, own, dq0,
    kv0, made, sems, kv_sems
):
    row, zh = meta[0], meta[1]
    brought = own_keys(k, v, kv0, kv_sems)
    steps = KEYS // TILE
    sent = []
    for j in range(steps):
        at = pl.ds(j * TILE, TILE)
        sent.append(pltpu.make_async_copy(made.at[at], dkv.at[at], sems.at[j]))
    q = jnp.concatenate([q0[...], q1[:TOK], q2[:TOK], q3[:TOK]], 0)
    g = jnp.concatenate([g0[...], g1[...], g2[...], g3[...]], 0)
    log_sum, dot = stat[0:1, :], stat[1:2, :]
    masks = block_masks(row, zh)
    per = TILE // SUMM
    dq = jnp.zeros((HEAD, ALL), F32)
    for j in range(steps):
        at = slice(j * TILE, (j + 1) * TILE)
        key, value = kva[at, :HEAD], kva[at, HEAD:]
        s = nt(key, q)
        parts = []
        for i in range(per):
            shift = jnp.where(masks[per * j + i] < 0, -NEG, log_sum)
            parts.append(
                jnp.exp2(s[i * SUMM : (i + 1) * SUMM] * SCALE2 - shift)
            )
        p = jnp.concatenate(parts, 0)
        made[at, HEAD:] = nn(p.astype(BF), g).astype(BF)
        ds = (p * (nt(value, g) - dot)).astype(BF)
        made[at, :HEAD] = (nn(ds, q) * SCALE).astype(BF)
        sent[j].start()
        dq = dq + tn(key, ds)
        if j == steps // 2:
            for copy in brought:
                copy.wait()
            key, value = kv0[:, :HEAD], kv0[:, HEAD:]
            s = jnp.where(causal_t(), nt(key, q[:TOK]) * SCALE2, NEG)
            p = jnp.exp2(s - log_sum[:, :TOK])
            own[:, HEAD:] = nn(p.astype(BF), g[:TOK])
            ds = (p * (nt(value, g[:TOK]) - dot[:, :TOK])).astype(BF)
            own[:, :HEAD] = nn(ds, q[:TOK]) * SCALE
            dq_own = tn(key, ds)
    dq0[...] = (dq[:, :TOK] + dq_own) * SCALE
    for d, ref in ((1, dq1), (2, dq2), (3, dq3)):
        ref[...] = (halves(dq[:, d * TOK : (d + 1) * TOK]) * SCALE).astype(BF)
    for copy in sent:
        copy.wait()


def strided_kernel(
    meta, q, k, v, g, f1, f2, f3, last, o, far, dq, dkv
):
    row, zh = meta[0], meta[1]
    slot = iota((TOK, 4 * REACH), 1) // REACH
    far_ok = (slot < zh) | (jnp.full((TOK, 4 * REACH), row, jnp.int32) > 0)
    near_ok = iota((TOK, TOK), 0) >= iota((TOK, TOK), 1)

    def far_rows(i):
        at = slice(TOK + i * REACH, TOK + (i + 1) * REACH)
        to = slice(i * REACH, (i + 1) * REACH)
        return jnp.concatenate([f1[at], f2[at], f3[at], last[to]], 0)

    for h in range(3):
        at = slice((h + 1) * HEAD, (h + 2) * HEAD)
        to = slice(h * HEAD, (h + 1) * HEAD)
        qh, kh, vh, gh = q[:, at], k[:, at], v[:, at], g[:, at]
        kf, vf = far_rows(h), far_rows(h + 3)
        s = jnp.where(near_ok, nt(qh, kh) * SCALE, NEG)
        sf = jnp.where(far_ok, nt(qh, kf) * SCALE, NEG)
        top = jnp.maximum(
            jnp.max(s, axis=1, keepdims=True), jnp.max(sf, axis=1, keepdims=True)
        )
        e, ef = jnp.exp(s - top), jnp.exp(sf - top)
        inv = 1.0 / (
            jnp.sum(e, axis=1, keepdims=True) + jnp.sum(ef, axis=1, keepdims=True)
        )
        p, pf = e * inv, ef * inv
        w, wf = p.astype(BF), pf.astype(BF)
        out = (nn(w, vh) + nn(wf, vf)).astype(BF)
        o[:, to] = out
        delta = jnp.sum(gh.astype(F32) * out.astype(F32), axis=1, keepdims=True)
        ds = (p * (nt(gh, vh) - delta) * SCALE).astype(BF)
        dsf = (pf * (nt(gh, vf) - delta) * SCALE).astype(BF)
        dq[:, to] = (nn(ds, kh) + nn(dsf, kf)).astype(BF)
        dkv[:, to] = tn(ds, qh)
        dkv[:, (h + 3) * HEAD : (h + 4) * HEAD] = tn(w, gh)
        dkf = tn(dsf, qh).astype(BF)
        dvf = tn(wf, gh).astype(BF)
        for u in range(4):
            rows = slice(u * REACH, (u + 1) * REACH)
            far[u, h * REACH : (h + 1) * REACH, :] = dkf[rows]
            far[u, (h + 3) * REACH : (h + 4) * REACH, :] = dvf[rows]


def project_strided_kernel(
    meta, o, o_c, w, w_c, acc, fixed_w, fixed_wc, here_w, sems, ahead_sems
):
    zl, c = meta[2], meta[3]
    places = ((1 - zl, c), (zl, c))
    copies = weight_blocks(w.at[pl.ds(HEAD, 3 * HEAD)], here_w, places, sems)
    ahead = weight_blocks(w.at[pl.ds(0, HEAD)], fixed_w, places, ahead_sems)
    wide = here_w.shape[2]
    for i, (z, core) in enumerate(places):
        at = pl.ds(pl.multiple_of((2 * z + core) * wide, wide), wide)
        fixed_wc[i] = w_c[:HEAD, at]
        total = nn(o_c[...], w_c[HEAD:, at])
        copies[i].wait()
        acc[i] = total + nn(o[...], here_w[i])
    for copy in ahead:
        copy.wait()


def project_fixed_kernel(meta, o, o_c, acc, fixed_w, fixed_wc, order, send, keep):
    for i, ref in ((0, send), (1, keep)):
        total = acc[i] + nn(o[...], fixed_w[i]) + nn(o_c[...], fixed_wc[i])
        ref[...] = total.astype(ref.dtype)


def output_kernel(meta, keep, over, dq0, dq1, dq2, dq3, strided_dq, out, qg):
    out[...] = (keep[...].astype(F32) + over[...].astype(F32)).astype(BF)
    total = dq0[...]
    for ref in (dq1, dq2, dq3):
        total = total + whole(ref[...].astype(F32))
    eye = ones_where(iota((HEAD, HEAD), 0) == iota((HEAD, HEAD), 1))
    qg[:, :HEAD] = tn(total.astype(BF), eye).astype(BF)
    qg[:, HEAD:] = strided_dq[...]


def final_kernel(meta, soff_t, sidx, dkv, own, here, after, strided, kg, vg):
    zh = meta[1]
    shard = GROUP * meta[0] + meta[1]
    pick = summary_select(sidx[...])
    fixed = own[...] + nn(jnp.concatenate([pick] * ROWS, 1), dkv[...])
    kg[:, :HEAD] = fixed[:, :HEAD].astype(BF)
    vg[:, :HEAD] = fixed[:, HEAD:].astype(BF)
    sel = stride_select(soff_t[...], shard)
    slots = []
    for u in range(4):
        block = after[u]
        if u < 3:
            block = jnp.where(
                zh + 1 + u < GROUP, here[u].astype(F32), block.astype(F32)
            ).astype(BF)
        slots.append(
            jnp.concatenate(
                [block[h * REACH : (h + 1) * REACH] for h in range(6)], 1
            )
        )
    total = strided[...] + tn(sel, jnp.concatenate(slots, 0))
    kg[:, HEAD:] = total[:, : 3 * HEAD].astype(BF)
    vg[:, HEAD:] = total[:, 3 * HEAD :].astype(BF)


def swap(a, axis):
    return lax.ppermute(a, axis, [(0, 1), (1, 0)])


def turn(a, by):
    return lax.ppermute(a, "zh", [(i, (i + by) % GROUP) for i in range(GROUP)])


def after(a, other):
    return lax.optimization_barrier((a, other))[0]


def dma(n):
    return pltpu.SemaphoreType.DMA((n,))


def shards(queries, key_rows, value_rows, out_weight, upstream, summary_index, soff):
    row = lax.axis_index(("x", "y"))
    zh, zl, c = lax.axis_index("zh"), lax.axis_index("zl"), lax.axis_index("c")
    meta = jnp.stack([row, zh, zl, c]).astype(jnp.int32)
    soff_t = soff.T
    width = queries.shape[1]
    quarter = upstream.shape[1]
    plane = ("x", "y")

    up_z = swap(upstream, "zl")
    up_c = swap(upstream, "c")
    block = sds((4, FAR, HEAD))
    kvb, q0, picks = call(
        prep_kernel,
        [sds((ROWS, SUMM, 2 * HEAD)), sds((TOK, HEAD)), block],
        [meta, soff_t, summary_index, key_rows, value_rows, queries],
        [dma(1)],
        name="pick_rows",
        fetch=range(1, 5),
        raw=[5],
    )
    before = lax.ppermute(picks, plane, [(i, i + 1) for i in range(ROWS - 1)])
    last, *sent = call(
        bundle_kernel,
        [sds((FAR, HEAD))] + [sds((TOK + FAR, HEAD))] * 3,
        [meta, q0, picks, before],
        name="bundle_queries",
        flops=3800000000,
    )
    kva = lax.all_to_all(kvb, plane, 0, 0, tiled=True).reshape(KEYS, 2 * HEAD)
    qs = [q0] + [turn(sent[d - 1], d) for d in (1, 2, 3)]
    up_zc = swap(after(up_z, last), "c")
    g0, g = call(
        grad_kernel,
        [sds((TOK, HEAD)), sds((TOK, width))],
        [meta, upstream, up_c, up_z, up_zc, out_weight],
        [
            pltpu.VMEM((TOK, quarter), BF),
            pltpu.VMEM((4, width, quarter), BF),
            dma(4),
            dma(1),
        ],
        name="attention_grad",
        raw=[1, 5],
    )
    gs = [g0] + [turn(g0, d) for d in (1, 2, 3)]
    o_s, far, dq_s, dkv_s = call(
        strided_kernel,
        [
            sds((TOK, 3 * HEAD)),
            block,
            sds((TOK, 3 * HEAD)),
            sds((TOK, 6 * HEAD), F32),
        ],
        [meta, queries, key_rows, value_rows, g, *qs[1:], last],
        name="strided_heads",
    )
    o_sc = swap(o_s, "c")
    own_space = pltpu.VMEM((TOK, 2 * HEAD), BF)
    obs = call(
        forward_kernel,
        [sds((TOK + STAT + FAR, HEAD))] * 4,
        [meta, *qs, *gs, kva, key_rows, value_rows, far],
        [pltpu.VMEM((KEYS, ALL), F32), own_space, dma(2)],
        name="fixed_forward",
        raw=[10, 11],
    )
    weight_c = swap(after(out_weight, obs[0]), "c")
    oas = [obs[0]] + [turn(obs[d], -d) for d in (1, 2, 3)]
    acc_out, fixed_w, fixed_wc = call(
        project_strided_kernel,
        [sds((2, TOK, quarter), F32)] + [sds((2, HEAD, quarter))] * 2,
        [meta, o_s, o_sc, out_weight, weight_c],
        [pltpu.VMEM((2, 3 * HEAD, quarter), BF), dma(2), dma(2)],
        name="project_strided",
        raw=[3],
    )
    o_f, stat, sent, here = call(
        combine_kernel,
        [sds((TOK, HEAD)), sds((8, ALL), F32), block, block],
        [meta, *oas, acc_out],
        name="combine",
    )
    o_fc = swap(o_f, "c")
    back = lax.ppermute(sent, plane, [(i + 1, i) for i in range(ROWS - 1)])
    dkv, *dqs, own, dq0 = call(
        backward_kernel,
        [sds((KEYS, 2 * HEAD))]
        + [sds((TOK, HEAD))] * 3
        + [sds((TOK, 2 * HEAD), F32), sds((HEAD, TOK), F32)],
        [meta, *qs, *gs, kva, key_rows, value_rows, stat],
        [
            own_space,
            pltpu.VMEM((KEYS, 2 * HEAD), BF),
            dma(KEYS // TILE),
            dma(2),
        ],
        name="fixed_backward",
        raw=[10, 11],
        direct=[0],
    )
    send, keep = call(
        project_fixed_kernel,
        [sds((TOK, quarter))] * 2,
        [meta, o_f, o_fc, acc_out, fixed_w, fixed_wc, dq0],
        name="project_fixed",
    )
    over = swap(send, "zl")
    dkva = lax.all_to_all(
        after(dkv, keep).reshape(ROWS, SUMM, 2 * HEAD), plane, 0, 0, tiled=True
    ).reshape(KEYS, 2 * HEAD)
    dqs = [turn(dqs[d - 1], -d) for d in (1, 2, 3)]
    layer_out, query_grad = call(
        output_kernel,
        [sds((TOK, quarter)), sds((TOK, width))],
        [meta, keep, over, dq0, *dqs, dq_s],
        name="join_output",
        flops=7 * 10**9,
    )
    key_grad, value_grad = call(
        final_kernel,
        [sds((TOK, width))] * 2,
        [meta, soff_t, summary_index, dkva, own, here, back, dkv_s],
        name="join_key_grads",
        fetch=[1, 2],
    )
    return layer_out, query_grad, key_grad, value_grad


def solution(mesh):
    grid = Mesh(mesh.devices.reshape(4, 4, 4, 2, 2), ("x", "y", "zh", "zl", "c"))
    ctx, head = ("x", "y", "zh"), ("zl", "c")
    return jax.shard_map(
        shards,
        mesh=grid,
        in_specs=(
            P(ctx, head),
            P(ctx, head),
            P(ctx, head),
            P(head, None),
            P(ctx, head),
            P(ctx, None),
            P(),
        ),
        out_specs=(P(ctx, head),) * 4,
        check_vma=False,
    )
```

```python
import functools

import jax
import jax.numpy as jnp
from jax import lax
from jax.experimental import pallas as pl
from jax.experimental.pallas import tpu as pltpu
from jax.sharding import Mesh
from jax.sharding import PartitionSpec as P

HEAD = 128
TOK = 256
SUMM = 128
STRIDE = 16
REACH = TOK // STRIDE
ROWS = 16
GROUP = 4
ALL = GROUP * TOK
KEYS = ROWS * SUMM
TILE = 256
STAT = 64
FAR = 6 * REACH
SCALE = HEAD ** (-0.5)
LOG2E = 1.4426950408889634
SCALE2 = SCALE * LOG2E
NEG = -1e30
F32 = jnp.float32
BF = jnp.bfloat16

VM = pl.BlockSpec(memory_space=pltpu.VMEM)
SM = pl.BlockSpec(memory_space=pltpu.SMEM)


def nn(a, b):
    return lax.dot_general(a, b, (((1,), (0,)), ((), ())), preferred_element_type=F32)


def nt(a, b):
    return lax.dot_general(a, b, (((1,), (1,)), ((), ())), preferred_element_type=F32)


def tn(a, b):
    return lax.dot_general(a, b, (((0,), (0,)), ((), ())), preferred_element_type=F32)


def iota(shape, dim):
    return lax.broadcasted_iota(jnp.int32, shape, dim)


def ones_where(condition):
    return condition.astype(F32).astype(BF)


def summary_select(sidx):
    return ones_where(iota((TOK, SUMM), 0) == sidx)


def stride_select(soff_t, shard):
    there = jnp.minimum(shard + 1 + iota((4, ROWS * GROUP), 0), ROWS * GROUP - 1)
    offset = jnp.where(iota((4, ROWS * GROUP), 1) == there, soff_t, 0)
    offset = jnp.sum(offset.astype(F32), axis=1, keepdims=True).astype(jnp.int32)
    row, col = iota((4 * REACH, TOK), 0), iota((4 * REACH, TOK), 1)
    slot = row // REACH
    want = (row % REACH) * STRIDE
    for u in range(4):
        want = want + jnp.where(slot == u, offset[u : u + 1], 0)
    return ones_where(want == col)


def call(
    kernel, outs, ins, scratch=(), name=None, vmem=24, fetch=(), raw=(), store=(),
    direct=(), flops=1,
):
    fetch, raw, store = sorted(fetch), set(raw), sorted(store)
    pinned = set(store) | set(direct)
    n_in, n_out, n_own = len(ins), len(outs), len(scratch)
    hbm = pl.BlockSpec(memory_space=pltpu.HBM)

    def body(*refs):
        given = list(refs[:n_in])
        made = list(refs[n_in : n_in + n_out])
        own = list(refs[n_in + n_out : n_in + n_out + n_own])
        rest = list(refs[n_in + n_out + n_own :])
        here = rest[: len(fetch)]
        there = rest[len(fetch) : len(fetch) + len(store)]
        sems = rest[-1] if fetch or store else None
        copies = []
        for n, (i, ref) in enumerate(zip(fetch, here)):
            copies.append(pltpu.make_async_copy(given[i], ref, sems.at[n]))
            given[i] = ref
        for copy in copies:
            copy.start()
        for copy in copies:
            copy.wait()
        copies = []
        for n, (i, ref) in enumerate(zip(store, there)):
            copies.append(
                pltpu.make_async_copy(ref, made[i], sems.at[len(fetch) + n])
            )
            made[i] = ref
        kernel(*given, *made, *own)
        for copy in copies:
            copy.start()
        for copy in copies:
            copy.wait()

    extra = [pltpu.VMEM(ins[i].shape, ins[i].dtype) for i in fetch]
    extra += [pltpu.VMEM(outs[i].shape, outs[i].dtype) for i in store]
    if extra:
        extra.append(dma(len(extra)))
    return pl.pallas_call(
        body,
        out_shape=tuple(
            pltpu.HBM(s.shape, s.dtype) if i in pinned else s
            for i, s in enumerate(outs)
        ),
        in_specs=[SM]
        + [hbm if i in fetch or i in raw else VM for i in range(1, n_in)],
        out_specs=tuple(hbm if i in pinned else VM for i in range(n_out)),
        scratch_shapes=list(scratch) + extra,
        compiler_params=pltpu.CompilerParams(vmem_limit_bytes=vmem * 2**20),
        cost_estimate=pl.CostEstimate(
            flops=flops, bytes_accessed=1, transcendentals=0
        ),
        name=name,
    )(
        *(
            pltpu.with_memory_space_constraint(x, pltpu.HBM)
            if i in fetch or i in raw
            else x
            for i, x in enumerate(ins)
        )
    )


def sds(shape, dtype=BF):
    return jax.ShapeDtypeStruct(shape, dtype)


def prep_kernel(meta, soff_t, sidx, k, v, q, kvb, q0, picks, sem):
    copy = pltpu.make_async_copy(q.at[:, pl.ds(0, HEAD)], q0, sem.at[0])
    copy.start()
    pick = summary_select(sidx[...])
    kv = tn(pick, jnp.concatenate([k[:, :HEAD], v[:, :HEAD]], 1)).astype(BF)
    for i in range(ROWS):
        kvb[i] = kv
    sel = stride_select(soff_t[...], GROUP * meta[0] + meta[1])
    got = nn(sel, jnp.concatenate([k[:, HEAD:], v[:, HEAD:]], 1)).astype(BF)
    for u in range(4):
        for h in range(6):
            picks[u, h * REACH : (h + 1) * REACH, :] = got[
                u * REACH : (u + 1) * REACH, h * HEAD : (h + 1) * HEAD
            ]
    copy.wait()


def weight_blocks(w, blocks, places, sems):
    wide = blocks.shape[2]
    copies = []
    for i, (z, core) in enumerate(places):
        at = pl.ds(pl.multiple_of((2 * z + core) * wide, wide), wide)
        copies.append(pltpu.make_async_copy(w.at[:, at], blocks.at[i], sems.at[i]))
    for copy in copies:
        copy.start()
    return copies


def bundle_kernel(meta, q0, picks, before, last, *sent):
    zh = meta[1]
    last[...] = before[3]
    for d in (1, 2, 3):
        ref = sent[d - 1]
        ref[:TOK, :] = q0[...]

        @pl.when(zh + d < GROUP)
        def _(d=d, ref=ref):
            ref[TOK:, :] = picks[d - 1]

        @pl.when(zh + d >= GROUP)
        def _(d=d, ref=ref):
            ref[TOK:, :] = before[d - 1]


def grad_kernel(meta, up, up_c, up_z, up_zc, w, g0, g, own, blocks, sems, own_sem):
    zl, c = meta[2], meta[3]
    places = ((zl, c), (zl, 1 - c), (1 - zl, c), (1 - zl, 1 - c))
    mine = pltpu.make_async_copy(up, own, own_sem.at[0])
    mine.start()
    copies = weight_blocks(w, blocks, places, sems)
    mine.wait()
    total = None
    for i, ref in enumerate((own, up_c, up_z, up_zc)):
        copies[i].wait()
        piece = nt(ref[...], blocks[i])
        total = piece if total is None else total + piece
    full = total.astype(BF)
    g0[...] = full[:, :HEAD]
    g[...] = full


def fold8(a, how):
    return how(a.reshape(a.shape[0] // 8, 8, a.shape[1]), axis=0)


def causal_t():
    return iota((TOK, TOK), 0) <= iota((TOK, TOK), 1)


def block_masks(row, zh):
    slot = iota((1, ALL), 1) // TOK
    edge = jnp.where(slot > zh, 0.0, NEG)
    none = jnp.full((1, ALL), NEG, F32)
    return [
        jnp.where(jnp.full((1, ALL), b, jnp.int32) < row, 0.0,
                  jnp.where(jnp.full((1, ALL), b, jnp.int32) == row, edge, none))
        for b in range(ROWS)
    ]


def split3(a):
    hi = a.astype(BF).astype(F32)
    mid = (a - hi).astype(BF).astype(F32)
    return [hi, mid, (a - hi - mid).astype(BF).astype(F32)]


def halves(a):
    return jnp.concatenate([a[:, :HEAD], a[:, HEAD:]], 0)


def whole(a):
    n = a.shape[0] // 2
    return jnp.concatenate([a[:n], a[n:]], 1)


def own_keys(k, v, kv0, sems):
    first = pl.ds(0, HEAD)
    copies = [
        pltpu.make_async_copy(k.at[:, first], kv0.at[:, first], sems.at[0]),
        pltpu.make_async_copy(
            v.at[:, first], kv0.at[:, pl.ds(HEAD, HEAD)], sems.at[1]
        ),
    ]
    for copy in copies:
        copy.start()
    return copies


def forward_kernel(
    meta, q0, q1, q2, q3, g0, g1, g2, g3, kva, k, v, far, ob0, ob1, ob2, ob3,
    s_ref, kv0, sems
):
    row, zh = meta[0], meta[1]
    brought = own_keys(k, v, kv0, sems)
    q = jnp.concatenate([q0[...], q1[:TOK], q2[:TOK], q3[:TOK]], 0)
    g = jnp.concatenate([g0[...], g1[...], g2[...], g3[...]], 0)
    masks = block_masks(row, zh)
    per = TILE // SUMM
    top = jnp.full((8, ALL), NEG, F32)
    for j in range(KEYS // TILE):
        s = nt(kva[j * TILE : (j + 1) * TILE, :HEAD], q)
        s_ref[j * TILE : (j + 1) * TILE, :] = s
        for i in range(per):
            most = fold8(s[i * SUMM : (i + 1) * SUMM], jnp.max)
            top = jnp.maximum(top, most + masks[per * j + i])
    top = jnp.max(top, axis=0, keepdims=True) * SCALE2
    sums = jnp.zeros((8, ALL), F32)
    dots = jnp.zeros((8, ALL), F32)
    out = jnp.zeros((HEAD, ALL), F32)
    for j in range(KEYS // TILE):
        at = slice(j * TILE, (j + 1) * TILE)
        value = kva[at, HEAD:]
        parts = []
        for i in range(per):
            b = per * j + i
            shift = jnp.where(masks[b] < 0, -NEG, top)
            parts.append(
                jnp.exp2(s_ref[b * SUMM : (b + 1) * SUMM, :] * SCALE2 - shift)
            )
        e = jnp.concatenate(parts, 0)
        sums = sums + fold8(e, jnp.sum)
        dots = dots + fold8(e * nt(value, g), jnp.sum)
        out = out + tn(value, e.astype(BF))
    sums = jnp.sum(sums, axis=0, keepdims=True)
    dots = jnp.sum(dots, axis=0, keepdims=True)
    some = sums > 0
    safe = jnp.where(some, sums, 1.0)
    inv = 1.0 / safe
    log_sum = jnp.where(some, top + jnp.log(safe) * LOG2E, NEG)
    dots = dots * inv
    out = out * inv

    for copy in brought:
        copy.wait()
    key, value = kv0[:, :HEAD], kv0[:, HEAD:]
    s = jnp.where(causal_t(), nt(key, q0[...]) * SCALE2, NEG)
    own_top = jnp.max(s, axis=0, keepdims=True)
    e = jnp.exp2(s - own_top)
    own_sum = jnp.sum(e, axis=0, keepdims=True)
    own_dot = jnp.sum(e * nt(value, g0[...]), axis=0, keepdims=True)
    own_out = tn(value, e.astype(BF))
    own_log = own_top + jnp.log(own_sum) * LOG2E
    near = log_sum[:, :TOK]
    most = jnp.maximum(near, own_log)
    wa, wb = jnp.exp2(near - most), jnp.exp2(own_log - most)
    inv = 1.0 / (wa + wb)
    wa, wb = wa * inv, wb * inv / own_sum
    log_sum = jnp.concatenate(
        [most - jnp.log(inv) * LOG2E, log_sum[:, TOK:]], 1
    )
    dots = jnp.concatenate(
        [wa * dots[:, :TOK] + wb * own_dot, dots[:, TOK:]], 1
    )

    stats = jnp.concatenate(
        split3(log_sum) + split3(dots) + [jnp.zeros((2, ALL), F32)], 0
    )
    stats = jnp.concatenate(
        [stats[:, i * HEAD : (i + 1) * HEAD] for i in range(ALL // HEAD)], 0
    ).astype(BF)
    for d, ref in enumerate((ob0, ob1, ob2, ob3)):
        part = out[:, d * TOK : (d + 1) * TOK]
        if d == 0:
            part = wa * part + wb * own_out
        ref[:TOK, :] = halves(part).astype(BF)
        ref[TOK : TOK + STAT, :] = stats
        ref[TOK + STAT :, :] = far[(d + 3) % 4]


def combine_kernel(meta, ob0, r1, r2, r3, order, o, stat, sent, here):
    for u, ref in enumerate((r1, r2, r3, ob0)):
        sent[u] = ref[TOK + STAT :, :]
        here[u] = ref[TOK + STAT :, :]
    sources = (ob0, r3, r2, r1)
    got = []
    for f in range(GROUP):
        rows = sources[f][TOK : TOK + STAT, :].astype(F32)
        got.append(
            jnp.concatenate([rows[8 * i : 8 * i + 8] for i in range(STAT // 8)], 1)
        )
    for d in range(GROUP):
        logs, dots = [], []
        for f in range(GROUP):
            e = (d - f) % GROUP
            part = got[f][:, e * TOK : (e + 1) * TOK]
            logs.append(part[0:1] + part[1:2] + part[2:3])
            dots.append(part[3:4] + part[4:5] + part[5:6])
        most = functools.reduce(jnp.maximum, logs)
        shares = [jnp.exp2(x - most) for x in logs]
        both = functools.reduce(jnp.add, shares)
        shares = [x / both for x in shares]
        at = slice(d * TOK, (d + 1) * TOK)
        stat[0:1, at] = most + jnp.log(both) * LOG2E
        stat[1:2, at] = functools.reduce(
            jnp.add, [x * y for x, y in zip(shares, dots)]
        )
        if d == 0:
            full = functools.reduce(
                jnp.add,
                [
                    shares[f]
                    * whole(sources[f][:TOK, :].astype(F32))
                    for f in range(GROUP)
                ],
            )
            eye = ones_where(iota((HEAD, HEAD), 0) == iota((HEAD, HEAD), 1))
            o[...] = tn(full.astype(BF), eye).astype(BF)
    stat[2:8, :] = jnp.zeros((6, ALL), F32)


def backward_kernel(
    meta, q0, q1, q2, q3, g0, g1, g2, g3, kva, k, v, stat, dkv, dq1, dq2, dq3, own, dq0,
    kv0, mine, made, sems, kv_sems
):
    row, zh = meta[0], meta[1]
    brought = own_keys(k, v, kv0, kv_sems)
    steps = KEYS // TILE
    sent = []
    for j in range(steps):
        at = pl.ds(j * TILE, TILE)
        sent.append(pltpu.make_async_copy(made.at[at], dkv.at[at], sems.at[j]))
    sent.append(pltpu.make_async_copy(mine, own, sems.at[steps]))
    q = jnp.concatenate([q0[...], q1[:TOK], q2[:TOK], q3[:TOK]], 0)
    g = jnp.concatenate([g0[...], g1[...], g2[...], g3[...]], 0)
    log_sum, dot = stat[0:1, :], stat[1:2, :]
    masks = block_masks(row, zh)
    per = TILE // SUMM
    dq = jnp.zeros((HEAD, ALL), F32)
    for j in range(steps):
        at = slice(j * TILE, (j + 1) * TILE)
        key, value = kva[at, :HEAD], kva[at, HEAD:]
        s = nt(key, q)
        parts = []
        for i in range(per):
            shift = jnp.where(masks[per * j + i] < 0, -NEG, log_sum)
            parts.append(
                jnp.exp2(s[i * SUMM : (i + 1) * SUMM] * SCALE2 - shift)
            )
        p = jnp.concatenate(parts, 0)
        made[at, HEAD:] = nn(p.astype(BF), g).astype(BF)
        ds = (p * (nt(value, g) - dot)).astype(BF)
        made[at, :HEAD] = (nn(ds, q) * SCALE).astype(BF)
        sent[j].start()
        dq = dq + tn(key, ds)
        if j == steps // 2:
            for copy in brought:
                copy.wait()
            key, value = kv0[:, :HEAD], kv0[:, HEAD:]
            s = jnp.where(causal_t(), nt(key, q[:TOK]) * SCALE2, NEG)
            p = jnp.exp2(s - log_sum[:, :TOK])
            mine[:, HEAD:] = nn(p.astype(BF), g[:TOK])
            ds = (p * (nt(value, g[:TOK]) - dot[:, :TOK])).astype(BF)
            mine[:, :HEAD] = nn(ds, q[:TOK]) * SCALE
            dq_own = tn(key, ds)
            sent[-1].start()
    dq0[...] = (dq[:, :TOK] + dq_own) * SCALE
    for d, ref in ((1, dq1), (2, dq2), (3, dq3)):
        ref[...] = (halves(dq[:, d * TOK : (d + 1) * TOK]) * SCALE).astype(BF)
    for copy in sent:
        copy.wait()


def strided_kernel(
    meta, q, k, v, g, f1, f2, f3, last, o, far, dq, dkv
):
    row, zh = meta[0], meta[1]
    slot = iota((TOK, 4 * REACH), 1) // REACH
    far_ok = (slot < zh) | (jnp.full((TOK, 4 * REACH), row, jnp.int32) > 0)
    near_ok = iota((TOK, TOK), 0) >= iota((TOK, TOK), 1)

    def far_rows(i):
        at = slice(TOK + i * REACH, TOK + (i + 1) * REACH)
        to = slice(i * REACH, (i + 1) * REACH)
        return jnp.concatenate([f1[at], f2[at], f3[at], last[to]], 0)

    for h in range(3):
        at = slice((h + 1) * HEAD, (h + 2) * HEAD)
        to = slice(h * HEAD, (h + 1) * HEAD)
        qh, kh, vh, gh = q[:, at], k[:, at], v[:, at], g[:, at]
        kf, vf = far_rows(h), far_rows(h + 3)
        s = jnp.where(near_ok, nt(qh, kh) * SCALE, NEG)
        sf = jnp.where(far_ok, nt(qh, kf) * SCALE, NEG)
        top = jnp.maximum(
            jnp.max(s, axis=1, keepdims=True), jnp.max(sf, axis=1, keepdims=True)
        )
        e, ef = jnp.exp(s - top), jnp.exp(sf - top)
        inv = 1.0 / (
            jnp.sum(e, axis=1, keepdims=True) + jnp.sum(ef, axis=1, keepdims=True)
        )
        p, pf = e * inv, ef * inv
        w, wf = p.astype(BF), pf.astype(BF)
        out = (nn(w, vh) + nn(wf, vf)).astype(BF)
        o[:, to] = out
        delta = jnp.sum(gh.astype(F32) * out.astype(F32), axis=1, keepdims=True)
        ds = (p * (nt(gh, vh) - delta) * SCALE).astype(BF)
        dsf = (pf * (nt(gh, vf) - delta) * SCALE).astype(BF)
        dq[:, to] = (nn(ds, kh) + nn(dsf, kf)).astype(BF)
        dkv[:, to] = tn(ds, qh)
        dkv[:, (h + 3) * HEAD : (h + 4) * HEAD] = tn(w, gh)
        dkf = tn(dsf, qh).astype(BF)
        dvf = tn(wf, gh).astype(BF)
        for u in range(4):
            rows = slice(u * REACH, (u + 1) * REACH)
            far[u, h * REACH : (h + 1) * REACH, :] = dkf[rows]
            far[u, (h + 3) * REACH : (h + 4) * REACH, :] = dvf[rows]


def project_strided_kernel(
    meta, o, o_c, w, w_c, acc, fixed_w, fixed_wc, here_w, sems, ahead_sems
):
    zl, c = meta[2], meta[3]
    places = ((1 - zl, c), (zl, c))
    copies = weight_blocks(w.at[pl.ds(HEAD, 3 * HEAD)], here_w, places, sems)
    ahead = weight_blocks(w.at[pl.ds(0, HEAD)], fixed_w, places, ahead_sems)
    wide = here_w.shape[2]
    for i, (z, core) in enumerate(places):
        at = pl.ds(pl.multiple_of((2 * z + core) * wide, wide), wide)
        fixed_wc[i] = w_c[:HEAD, at]
        total = nn(o_c[...], w_c[HEAD:, at])
        copies[i].wait()
        acc[i] = total + nn(o[...], here_w[i])
    for copy in ahead:
        copy.wait()


def project_fixed_kernel(meta, o, o_c, acc, fixed_w, fixed_wc, order, send, keep):
    for i, ref in ((0, send), (1, keep)):
        total = acc[i] + nn(o[...], fixed_w[i]) + nn(o_c[...], fixed_wc[i])
        ref[...] = total.astype(ref.dtype)


def output_kernel(meta, keep, over, dq0, dq1, dq2, dq3, strided_dq, out, qg):
    out[...] = (keep[...].astype(F32) + over[...].astype(F32)).astype(BF)
    total = dq0[...]
    for ref in (dq1, dq2, dq3):
        total = total + whole(ref[...].astype(F32))
    eye = ones_where(iota((HEAD, HEAD), 0) == iota((HEAD, HEAD), 1))
    qg[:, :HEAD] = tn(total.astype(BF), eye).astype(BF)
    qg[:, HEAD:] = strided_dq[...]


def final_kernel(meta, soff_t, sidx, dkv, own, here, after, strided, kg, vg):
    zh = meta[1]
    shard = GROUP * meta[0] + meta[1]
    pick = summary_select(sidx[...])
    fixed = own[...] + nn(jnp.concatenate([pick] * ROWS, 1), dkv[...])
    kg[:, :HEAD] = fixed[:, :HEAD].astype(BF)
    vg[:, :HEAD] = fixed[:, HEAD:].astype(BF)
    sel = stride_select(soff_t[...], shard)
    slots = []
    for u in range(4):
        block = after[u]
        if u < 3:
            block = jnp.where(
                zh + 1 + u < GROUP, here[u].astype(F32), block.astype(F32)
            ).astype(BF)
        slots.append(
            jnp.concatenate(
                [block[h * REACH : (h + 1) * REACH] for h in range(6)], 1
            )
        )
    total = strided[...] + tn(sel, jnp.concatenate(slots, 0))
    kg[:, HEAD:] = total[:, : 3 * HEAD].astype(BF)
    vg[:, HEAD:] = total[:, 3 * HEAD :].astype(BF)


def swap(a, axis):
    return lax.ppermute(a, axis, [(0, 1), (1, 0)])


def turn(a, by):
    return lax.ppermute(a, "zh", [(i, (i + by) % GROUP) for i in range(GROUP)])


def after(a, other):
    return lax.optimization_barrier((a, other))[0]


def dma(n):
    return pltpu.SemaphoreType.DMA((n,))


def shards(queries, key_rows, value_rows, out_weight, upstream, summary_index, soff):
    row = lax.axis_index(("x", "y"))
    zh, zl, c = lax.axis_index("zh"), lax.axis_index("zl"), lax.axis_index("c")
    meta = jnp.stack([row, zh, zl, c]).astype(jnp.int32)
    soff_t = soff.T
    width = queries.shape[1]
    quarter = upstream.shape[1]
    plane = ("x", "y")

    up_z = swap(upstream, "zl")
    up_c = swap(upstream, "c")
    block = sds((4, FAR, HEAD))
    kvb, q0, picks = call(
        prep_kernel,
        [sds((ROWS, SUMM, 2 * HEAD)), sds((TOK, HEAD)), block],
        [meta, soff_t, summary_index, key_rows, value_rows, queries],
        [dma(1)],
        name="pick_rows",
        fetch=range(1, 5),
        raw=[5],
    )
    before = lax.ppermute(picks, plane, [(i, i + 1) for i in range(ROWS - 1)])
    last, *sent = call(
        bundle_kernel,
        [sds((FAR, HEAD))] + [sds((TOK + FAR, HEAD))] * 3,
        [meta, q0, picks, before],
        name="bundle_queries",
        flops=3800000000,
    )
    kva = lax.all_to_all(kvb, plane, 0, 0, tiled=True).reshape(KEYS, 2 * HEAD)
    qs = [q0] + [turn(sent[d - 1], d) for d in (1, 2, 3)]
    up_zc = swap(after(up_z, last), "c")
    g0, g = call(
        grad_kernel,
        [sds((TOK, HEAD)), sds((TOK, width))],
        [meta, upstream, up_c, up_z, up_zc, out_weight],
        [
            pltpu.VMEM((TOK, quarter), BF),
            pltpu.VMEM((4, width, quarter), BF),
            dma(4),
            dma(1),
        ],
        name="attention_grad",
        raw=[1, 5],
    )
    gs = [g0] + [turn(g0, d) for d in (1, 2, 3)]
    o_s, far, dq_s, dkv_s = call(
        strided_kernel,
        [
            sds((TOK, 3 * HEAD)),
            block,
            sds((TOK, 3 * HEAD)),
            sds((TOK, 6 * HEAD), F32),
        ],
        [meta, queries, key_rows, value_rows, g, *qs[1:], last],
        name="strided_heads",
    )
    o_sc = swap(o_s, "c")
    own_space = pltpu.VMEM((TOK, 2 * HEAD), BF)
    obs = call(
        forward_kernel,
        [sds((TOK + STAT + FAR, HEAD))] * 4,
        [meta, *qs, *gs, kva, key_rows, value_rows, far],
        [pltpu.VMEM((KEYS, ALL), F32), own_space, dma(2)],
        name="fixed_forward",
        raw=[10, 11],
    )
    weight_c = swap(after(out_weight, obs[0]), "c")
    oas = [obs[0]] + [turn(obs[d], -d) for d in (1, 2, 3)]
    acc_out, fixed_w, fixed_wc = call(
        project_strided_kernel,
        [sds((2, TOK, quarter), F32)] + [sds((2, HEAD, quarter))] * 2,
        [meta, o_s, o_sc, out_weight, weight_c],
        [pltpu.VMEM((2, 3 * HEAD, quarter), BF), dma(2), dma(2)],
        name="project_strided",
        raw=[3],
    )
    o_f, stat, sent, here = call(
        combine_kernel,
        [sds((TOK, HEAD)), sds((8, ALL), F32), block, block],
        [meta, *oas, acc_out],
        name="combine",
    )
    o_fc = swap(o_f, "c")
    back = lax.ppermute(sent, plane, [(i + 1, i) for i in range(ROWS - 1)])
    dkv, *dqs, own, dq0 = call(
        backward_kernel,
        [sds((KEYS, 2 * HEAD))]
        + [sds((TOK, HEAD))] * 3
        + [sds((TOK, 2 * HEAD), F32), sds((HEAD, TOK), F32)],
        [meta, *qs, *gs, kva, key_rows, value_rows, stat],
        [
            own_space,
            pltpu.VMEM((TOK, 2 * HEAD), F32),
            pltpu.VMEM((KEYS, 2 * HEAD), BF),
            dma(1 + KEYS // TILE),
            dma(2),
        ],
        name="fixed_backward",
        raw=[10, 11],
        direct=[0, 4],
    )
    send, keep = call(
        project_fixed_kernel,
        [sds((TOK, quarter))] * 2,
        [meta, o_f, o_fc, acc_out, fixed_w, fixed_wc, dq0],
        name="project_fixed",
    )
    over = swap(send, "zl")
    dkva = lax.all_to_all(
        after(dkv, keep).reshape(ROWS, SUMM, 2 * HEAD), plane, 0, 0, tiled=True
    ).reshape(KEYS, 2 * HEAD)
    dqs = [turn(dqs[d - 1], -d) for d in (1, 2, 3)]
    layer_out, query_grad = call(
        output_kernel,
        [sds((TOK, quarter)), sds((TOK, width))],
        [meta, keep, over, dq0, *dqs, dq_s],
        name="join_output",
        flops=7 * 10**9,
    )
    key_grad, value_grad = call(
        final_kernel,
        [sds((TOK, width))] * 2,
        [meta, soff_t, summary_index, dkva, own, here, back, dkv_s],
        name="join_key_grads",
        fetch=[1, 2, 4],
    )
    return layer_out, query_grad, key_grad, value_grad


def solution(mesh):
    grid = Mesh(mesh.devices.reshape(4, 4, 4, 2, 2), ("x", "y", "zh", "zl", "c"))
    ctx, head = ("x", "y", "zh"), ("zl", "c")
    return jax.shard_map(
        shards,
        mesh=grid,
        in_specs=(
            P(ctx, head),
            P(ctx, head),
            P(ctx, head),
            P(head, None),
            P(ctx, head),
            P(ctx, None),
            P(),
        ),
        out_specs=(P(ctx, head),) * 4,
        check_vma=False,
    )
```

```python
import functools

import jax
import jax.numpy as jnp
from jax import lax
from jax.experimental import pallas as pl
from jax.experimental.pallas import tpu as pltpu
from jax.sharding import Mesh
from jax.sharding import PartitionSpec as P

HEAD = 128
TOK = 256
SUMM = 128
STRIDE = 16
REACH = TOK // STRIDE
ROWS = 16
GROUP = 4
ALL = GROUP * TOK
KEYS = ROWS * SUMM
TILE = 256
STAT = 64
FAR = 6 * REACH
SCALE = HEAD ** (-0.5)
LOG2E = 1.4426950408889634
SCALE2 = SCALE * LOG2E
NEG = -1e30
F32 = jnp.float32
BF = jnp.bfloat16

VM = pl.BlockSpec(memory_space=pltpu.VMEM)
SM = pl.BlockSpec(memory_space=pltpu.SMEM)


def nn(a, b):
    return lax.dot_general(a, b, (((1,), (0,)), ((), ())), preferred_element_type=F32)


def nt(a, b):
    return lax.dot_general(a, b, (((1,), (1,)), ((), ())), preferred_element_type=F32)


def tn(a, b):
    return lax.dot_general(a, b, (((0,), (0,)), ((), ())), preferred_element_type=F32)


def iota(shape, dim):
    return lax.broadcasted_iota(jnp.int32, shape, dim)


def ones_where(condition):
    return condition.astype(F32).astype(BF)


def summary_select(sidx):
    return ones_where(iota((TOK, SUMM), 0) == sidx)


def stride_select(soff_t, shard):
    there = jnp.minimum(shard + 1 + iota((4, ROWS * GROUP), 0), ROWS * GROUP - 1)
    offset = jnp.where(iota((4, ROWS * GROUP), 1) == there, soff_t, 0)
    offset = jnp.sum(offset.astype(F32), axis=1, keepdims=True).astype(jnp.int32)
    row, col = iota((4 * REACH, TOK), 0), iota((4 * REACH, TOK), 1)
    slot = row // REACH
    want = (row % REACH) * STRIDE
    for u in range(4):
        want = want + jnp.where(slot == u, offset[u : u + 1], 0)
    return ones_where(want == col)


def call(
    kernel, outs, ins, scratch=(), name=None, vmem=24, fetch=(), raw=(), store=(),
    direct=(), flops=1,
):
    fetch, raw, store = sorted(fetch), set(raw), sorted(store)
    pinned = set(store) | set(direct)
    n_in, n_out, n_own = len(ins), len(outs), len(scratch)
    hbm = pl.BlockSpec(memory_space=pltpu.HBM)

    def body(*refs):
        given = list(refs[:n_in])
        made = list(refs[n_in : n_in + n_out])
        own = list(refs[n_in + n_out : n_in + n_out + n_own])
        rest = list(refs[n_in + n_out + n_own :])
        here = rest[: len(fetch)]
        there = rest[len(fetch) : len(fetch) + len(store)]
        sems = rest[-1] if fetch or store else None
        copies = []
        for n, (i, ref) in enumerate(zip(fetch, here)):
            copies.append(pltpu.make_async_copy(given[i], ref, sems.at[n]))
            given[i] = ref
        for copy in copies:
            copy.start()
        for copy in copies:
            copy.wait()
        copies = []
        for n, (i, ref) in enumerate(zip(store, there)):
            copies.append(
                pltpu.make_async_copy(ref, made[i], sems.at[len(fetch) + n])
            )
            made[i] = ref
        kernel(*given, *made, *own)
        for copy in copies:
            copy.start()
        for copy in copies:
            copy.wait()

    extra = [pltpu.VMEM(ins[i].shape, ins[i].dtype) for i in fetch]
    extra += [pltpu.VMEM(outs[i].shape, outs[i].dtype) for i in store]
    if extra:
        extra.append(dma(len(extra)))
    return pl.pallas_call(
        body,
        out_shape=tuple(
            pltpu.HBM(s.shape, s.dtype) if i in pinned else s
            for i, s in enumerate(outs)
        ),
        in_specs=[SM]
        + [hbm if i in fetch or i in raw else VM for i in range(1, n_in)],
        out_specs=tuple(hbm if i in pinned else VM for i in range(n_out)),
        scratch_shapes=list(scratch) + extra,
        compiler_params=pltpu.CompilerParams(vmem_limit_bytes=vmem * 2**20),
        cost_estimate=pl.CostEstimate(
            flops=flops, bytes_accessed=1, transcendentals=0
        ),
        name=name,
    )(
        *(
            pltpu.with_memory_space_constraint(x, pltpu.HBM)
            if i in fetch or i in raw
            else x
            for i, x in enumerate(ins)
        )
    )


def sds(shape, dtype=BF):
    return jax.ShapeDtypeStruct(shape, dtype)


def prep_kernel(meta, soff_t, sidx, k, v, q, kvb, q0, picks, sem):
    copy = pltpu.make_async_copy(q.at[:, pl.ds(0, HEAD)], q0, sem.at[0])
    copy.start()
    pick = summary_select(sidx[...])
    kv = tn(pick, jnp.concatenate([k[:, :HEAD], v[:, :HEAD]], 1)).astype(BF)
    for i in range(ROWS):
        kvb[i] = kv
    sel = stride_select(soff_t[...], GROUP * meta[0] + meta[1])
    got = nn(sel, jnp.concatenate([k[:, HEAD:], v[:, HEAD:]], 1)).astype(BF)
    for u in range(4):
        for h in range(6):
            picks[u, h * REACH : (h + 1) * REACH, :] = got[
                u * REACH : (u + 1) * REACH, h * HEAD : (h + 1) * HEAD
            ]
    copy.wait()


def weight_blocks(w, blocks, places, sems):
    wide = blocks.shape[2]
    copies = []
    for i, (z, core) in enumerate(places):
        at = pl.ds(pl.multiple_of((2 * z + core) * wide, wide), wide)
        copies.append(pltpu.make_async_copy(w.at[:, at], blocks.at[i], sems.at[i]))
    for copy in copies:
        copy.start()
    return copies


def bundle_kernel(meta, q0, picks, before, last, *sent):
    zh = meta[1]
    last[...] = before[3]
    for d in (1, 2, 3):
        ref = sent[d - 1]
        ref[:TOK, :] = q0[...]

        @pl.when(zh + d < GROUP)
        def _(d=d, ref=ref):
            ref[TOK:, :] = picks[d - 1]

        @pl.when(zh + d >= GROUP)
        def _(d=d, ref=ref):
            ref[TOK:, :] = before[d - 1]


def grad_kernel(meta, up, up_c, up_z, up_zc, w, g0, g, own, blocks, sems, own_sem):
    zl, c = meta[2], meta[3]
    places = ((zl, c), (zl, 1 - c), (1 - zl, c), (1 - zl, 1 - c))
    mine = pltpu.make_async_copy(up, own, own_sem.at[0])
    mine.start()
    copies = weight_blocks(w, blocks, places, sems)
    mine.wait()
    total = None
    for i, ref in enumerate((own, up_c, up_z, up_zc)):
        copies[i].wait()
        piece = nt(ref[...], blocks[i])
        total = piece if total is None else total + piece
    full = total.astype(BF)
    g0[...] = full[:, :HEAD]
    g[...] = full


def fold8(a, how):
    return how(a.reshape(a.shape[0] // 8, 8, a.shape[1]), axis=0)


def causal_t():
    return iota((TOK, TOK), 0) <= iota((TOK, TOK), 1)


def block_masks(row, zh):
    slot = iota((1, ALL), 1) // TOK
    edge = jnp.where(slot > zh, 0.0, NEG)
    none = jnp.full((1, ALL), NEG, F32)
    return [
        jnp.where(jnp.full((1, ALL), b, jnp.int32) < row, 0.0,
                  jnp.where(jnp.full((1, ALL), b, jnp.int32) == row, edge, none))
        for b in range(ROWS)
    ]


def split3(a):
    hi = a.astype(BF).astype(F32)
    mid = (a - hi).astype(BF).astype(F32)
    return [hi, mid, (a - hi - mid).astype(BF).astype(F32)]


def halves(a):
    return jnp.concatenate([a[:, :HEAD], a[:, HEAD:]], 0)


def whole(a):
    n = a.shape[0] // 2
    return jnp.concatenate([a[:n], a[n:]], 1)


def own_keys(k, v, kv0, sems):
    first = pl.ds(0, HEAD)
    copies = [
        pltpu.make_async_copy(k.at[:, first], kv0.at[:, first], sems.at[0]),
        pltpu.make_async_copy(
            v.at[:, first], kv0.at[:, pl.ds(HEAD, HEAD)], sems.at[1]
        ),
    ]
    for copy in copies:
        copy.start()
    return copies


def forward_kernel(
    meta, q0, q1, q2, q3, g0, g1, g2, g3, kva, k, v, far, ob0, ob1, ob2, ob3,
    s_ref, kv0, sems
):
    row, zh = meta[0], meta[1]
    brought = own_keys(k, v, kv0, sems)
    q = jnp.concatenate([q0[...], q1[:TOK], q2[:TOK], q3[:TOK]], 0)
    g = jnp.concatenate([g0[...], g1[...], g2[...], g3[...]], 0)
    masks = block_masks(row, zh)
    per = TILE // SUMM
    top = jnp.full((8, ALL), NEG, F32)
    for j in range(KEYS // TILE):
        s = nt(kva[j * TILE : (j + 1) * TILE, :HEAD], q)
        s_ref[j * TILE : (j + 1) * TILE, :] = s
        for i in range(per):
            most = fold8(s[i * SUMM : (i + 1) * SUMM], jnp.max)
            top = jnp.maximum(top, most + masks[per * j + i])
    top = jnp.max(top, axis=0, keepdims=True) * SCALE2
    sums = jnp.zeros((8, ALL), F32)
    dots = jnp.zeros((8, ALL), F32)
    out = jnp.zeros((HEAD, ALL), F32)
    for j in range(KEYS // TILE):
        at = slice(j * TILE, (j + 1) * TILE)
        value = kva[at, HEAD:]
        parts = []
        for i in range(per):
            b = per * j + i
            shift = jnp.where(masks[b] < 0, -NEG, top)
            parts.append(
                jnp.exp2(s_ref[b * SUMM : (b + 1) * SUMM, :] * SCALE2 - shift)
            )
        e = jnp.concatenate(parts, 0)
        sums = sums + fold8(e, jnp.sum)
        dots = dots + fold8(e * nt(value, g), jnp.sum)
        out = out + tn(value, e.astype(BF))
    sums = jnp.sum(sums, axis=0, keepdims=True)
    dots = jnp.sum(dots, axis=0, keepdims=True)
    some = sums > 0
    safe = jnp.where(some, sums, 1.0)
    inv = 1.0 / safe
    log_sum = jnp.where(some, top + jnp.log(safe) * LOG2E, NEG)
    dots = dots * inv
    out = out * inv

    for copy in brought:
        copy.wait()
    key, value = kv0[:, :HEAD], kv0[:, HEAD:]
    s = jnp.where(causal_t(), nt(key, q0[...]) * SCALE2, NEG)
    own_top = jnp.max(s, axis=0, keepdims=True)
    e = jnp.exp2(s - own_top)
    own_sum = jnp.sum(e, axis=0, keepdims=True)
    own_dot = jnp.sum(e * nt(value, g0[...]), axis=0, keepdims=True)
    own_out = tn(value, e.astype(BF))
    own_log = own_top + jnp.log(own_sum) * LOG2E
    near = log_sum[:, :TOK]
    most = jnp.maximum(near, own_log)
    wa, wb = jnp.exp2(near - most), jnp.exp2(own_log - most)
    inv = 1.0 / (wa + wb)
    wa, wb = wa * inv, wb * inv / own_sum
    log_sum = jnp.concatenate(
        [most - jnp.log(inv) * LOG2E, log_sum[:, TOK:]], 1
    )
    dots = jnp.concatenate(
        [wa * dots[:, :TOK] + wb * own_dot, dots[:, TOK:]], 1
    )

    stats = jnp.concatenate(
        split3(log_sum) + split3(dots) + [jnp.zeros((2, ALL), F32)], 0
    )
    stats = jnp.concatenate(
        [stats[:, i * HEAD : (i + 1) * HEAD] for i in range(ALL // HEAD)], 0
    ).astype(BF)
    for d, ref in enumerate((ob0, ob1, ob2, ob3)):
        part = out[:, d * TOK : (d + 1) * TOK]
        if d == 0:
            part = wa * part + wb * own_out
        ref[:TOK, :] = halves(part).astype(BF)
        ref[TOK : TOK + STAT, :] = stats
        ref[TOK + STAT :, :] = far[(d + 3) % 4]


def combine_kernel(meta, ob0, r1, r2, r3, order, o, stat, sent, here):
    for u, ref in enumerate((r1, r2, r3, ob0)):
        sent[u] = ref[TOK + STAT :, :]
        here[u] = ref[TOK + STAT :, :]
    sources = (ob0, r3, r2, r1)
    got = []
    for f in range(GROUP):
        rows = sources[f][TOK : TOK + STAT, :].astype(F32)
        got.append(
            jnp.concatenate([rows[8 * i : 8 * i + 8] for i in range(STAT // 8)], 1)
        )
    for d in range(GROUP):
        logs, dots = [], []
        for f in range(GROUP):
            e = (d - f) % GROUP
            part = got[f][:, e * TOK : (e + 1) * TOK]
            logs.append(part[0:1] + part[1:2] + part[2:3])
            dots.append(part[3:4] + part[4:5] + part[5:6])
        most = functools.reduce(jnp.maximum, logs)
        shares = [jnp.exp2(x - most) for x in logs]
        both = functools.reduce(jnp.add, shares)
        shares = [x / both for x in shares]
        at = slice(d * TOK, (d + 1) * TOK)
        stat[0:1, at] = most + jnp.log(both) * LOG2E
        stat[1:2, at] = functools.reduce(
            jnp.add, [x * y for x, y in zip(shares, dots)]
        )
        if d == 0:
            full = functools.reduce(
                jnp.add,
                [
                    shares[f]
                    * whole(sources[f][:TOK, :].astype(F32))
                    for f in range(GROUP)
                ],
            )
            eye = ones_where(iota((HEAD, HEAD), 0) == iota((HEAD, HEAD), 1))
            o[...] = tn(full.astype(BF), eye).astype(BF)
    stat[2:8, :] = jnp.zeros((6, ALL), F32)


def backward_kernel(
    meta, q0, q1, q2, q3, g0, g1, g2, g3, kva, k, v, stat, dkv, dq1, dq2, dq3, own, dq0,
    kv0, mine, made, sems, kv_sems
):
    row, zh = meta[0], meta[1]
    brought = own_keys(k, v, kv0, kv_sems)
    steps = KEYS // TILE
    sent = []
    for j in range(steps):
        at = pl.ds(j * TILE, TILE)
        sent.append(pltpu.make_async_copy(made.at[at], dkv.at[at], sems.at[j]))
    sent.append(pltpu.make_async_copy(mine, own, sems.at[steps]))
    q = jnp.concatenate([q0[...], q1[:TOK], q2[:TOK], q3[:TOK]], 0)
    g = jnp.concatenate([g0[...], g1[...], g2[...], g3[...]], 0)
    log_sum, dot = stat[0:1, :], stat[1:2, :]
    masks = block_masks(row, zh)
    per = TILE // SUMM
    dq = jnp.zeros((HEAD, ALL), F32)
    for j in range(steps):
        at = slice(j * TILE, (j + 1) * TILE)
        key, value = kva[at, :HEAD], kva[at, HEAD:]
        s = nt(key, q)
        parts = []
        for i in range(per):
            shift = jnp.where(masks[per * j + i] < 0, -NEG, log_sum)
            parts.append(
                jnp.exp2(s[i * SUMM : (i + 1) * SUMM] * SCALE2 - shift)
            )
        p = jnp.concatenate(parts, 0)
        made[at, HEAD:] = nn(p.astype(BF), g).astype(BF)
        ds = (p * (nt(value, g) - dot)).astype(BF)
        made[at, :HEAD] = (nn(ds, q) * SCALE).astype(BF)
        sent[j].start()
        dq = dq + tn(key, ds)
        if j == steps // 2:
            for copy in brought:
                copy.wait()
            key, value = kv0[:, :HEAD], kv0[:, HEAD:]
            s = jnp.where(causal_t(), nt(key, q[:TOK]) * SCALE2, NEG)
            p = jnp.exp2(s - log_sum[:, :TOK])
            mine[:, HEAD:] = nn(p.astype(BF), g[:TOK])
            ds = (p * (nt(value, g[:TOK]) - dot[:, :TOK])).astype(BF)
            mine[:, :HEAD] = nn(ds, q[:TOK]) * SCALE
            dq_own = tn(key, ds)
            sent[-1].start()
    dq0[...] = (dq[:, :TOK] + dq_own) * SCALE
    for d, ref in ((1, dq1), (2, dq2), (3, dq3)):
        ref[...] = (halves(dq[:, d * TOK : (d + 1) * TOK]) * SCALE).astype(BF)
    for copy in sent:
        copy.wait()


def strided_kernel(
    meta, q, k, v, g, f1, f2, f3, last, o, far, dq, dkv
):
    row, zh = meta[0], meta[1]
    slot = iota((TOK, 4 * REACH), 1) // REACH
    far_ok = (slot < zh) | (jnp.full((TOK, 4 * REACH), row, jnp.int32) > 0)
    near_ok = iota((TOK, TOK), 0) >= iota((TOK, TOK), 1)

    def far_rows(i):
        at = slice(TOK + i * REACH, TOK + (i + 1) * REACH)
        to = slice(i * REACH, (i + 1) * REACH)
        return jnp.concatenate([f1[at], f2[at], f3[at], last[to]], 0)

    for h in range(3):
        at = slice((h + 1) * HEAD, (h + 2) * HEAD)
        to = slice(h * HEAD, (h + 1) * HEAD)
        qh, kh, vh, gh = q[:, at], k[:, at], v[:, at], g[:, at]
        kf, vf = far_rows(h), far_rows(h + 3)
        s = jnp.where(near_ok, nt(qh, kh) * SCALE, NEG)
        sf = jnp.where(far_ok, nt(qh, kf) * SCALE, NEG)
        top = jnp.maximum(
            jnp.max(s, axis=1, keepdims=True), jnp.max(sf, axis=1, keepdims=True)
        )
        e, ef = jnp.exp(s - top), jnp.exp(sf - top)
        inv = 1.0 / (
            jnp.sum(e, axis=1, keepdims=True) + jnp.sum(ef, axis=1, keepdims=True)
        )
        p, pf = e * inv, ef * inv
        w, wf = p.astype(BF), pf.astype(BF)
        out = (nn(w, vh) + nn(wf, vf)).astype(BF)
        o[:, to] = out
        delta = jnp.sum(gh.astype(F32) * out.astype(F32), axis=1, keepdims=True)
        ds = (p * (nt(gh, vh) - delta) * SCALE).astype(BF)
        dsf = (pf * (nt(gh, vf) - delta) * SCALE).astype(BF)
        dq[:, to] = (nn(ds, kh) + nn(dsf, kf)).astype(BF)
        dkv[:, to] = tn(ds, qh)
        dkv[:, (h + 3) * HEAD : (h + 4) * HEAD] = tn(w, gh)
        dkf = tn(dsf, qh).astype(BF)
        dvf = tn(wf, gh).astype(BF)
        for u in range(4):
            rows = slice(u * REACH, (u + 1) * REACH)
            far[u, h * REACH : (h + 1) * REACH, :] = dkf[rows]
            far[u, (h + 3) * REACH : (h + 4) * REACH, :] = dvf[rows]


def project_strided_kernel(
    meta, o, o_c, w, w_c, acc, fixed_w, fixed_wc, here_w, sems, ahead_sems
):
    zl, c = meta[2], meta[3]
    places = ((1 - zl, c), (zl, c))
    copies = weight_blocks(w.at[pl.ds(HEAD, 3 * HEAD)], here_w, places, sems)
    ahead = weight_blocks(w.at[pl.ds(0, HEAD)], fixed_w, places, ahead_sems)
    wide = here_w.shape[2]
    for i, (z, core) in enumerate(places):
        at = pl.ds(pl.multiple_of((2 * z + core) * wide, wide), wide)
        fixed_wc[i] = w_c[:HEAD, at]
        total = nn(o_c[...], w_c[HEAD:, at])
        copies[i].wait()
        acc[i] = total + nn(o[...], here_w[i])
    for copy in ahead:
        copy.wait()


def project_fixed_kernel(meta, o, o_c, acc, fixed_w, fixed_wc, order, send, keep):
    for i, ref in ((0, send), (1, keep)):
        total = acc[i] + nn(o[...], fixed_w[i]) + nn(o_c[...], fixed_wc[i])
        ref[...] = total.astype(ref.dtype)


def output_kernel(meta, keep, over, dq0, dq1, dq2, dq3, strided_dq, out, qg):
    out[...] = (keep[...].astype(F32) + over[...].astype(F32)).astype(BF)
    total = dq0[...]
    for ref in (dq1, dq2, dq3):
        total = total + whole(ref[...].astype(F32))
    eye = ones_where(iota((HEAD, HEAD), 0) == iota((HEAD, HEAD), 1))
    qg[:, :HEAD] = tn(total.astype(BF), eye).astype(BF)
    qg[:, HEAD:] = strided_dq[...]


def final_kernel(meta, soff_t, sidx, dkv, own, here, after, strided, kg, vg):
    zh = meta[1]
    shard = GROUP * meta[0] + meta[1]
    pick = summary_select(sidx[...])
    fixed = own[...] + nn(jnp.concatenate([pick] * ROWS, 1), dkv[...])
    kg[:, :HEAD] = fixed[:, :HEAD].astype(BF)
    vg[:, :HEAD] = fixed[:, HEAD:].astype(BF)
    sel = stride_select(soff_t[...], shard)
    slots = []
    for u in range(4):
        block = after[u]
        if u < 3:
            block = jnp.where(
                zh + 1 + u < GROUP, here[u].astype(F32), block.astype(F32)
            ).astype(BF)
        slots.append(
            jnp.concatenate(
                [block[h * REACH : (h + 1) * REACH] for h in range(6)], 1
            )
        )
    total = strided[...] + tn(sel, jnp.concatenate(slots, 0))
    kg[:, HEAD:] = total[:, : 3 * HEAD].astype(BF)
    vg[:, HEAD:] = total[:, 3 * HEAD :].astype(BF)


def swap(a, axis):
    return lax.ppermute(a, axis, [(0, 1), (1, 0)])


def turn(a, by):
    return lax.ppermute(a, "zh", [(i, (i + by) % GROUP) for i in range(GROUP)])


def after(a, other):
    return lax.optimization_barrier((a, other))[0]


def dma(n):
    return pltpu.SemaphoreType.DMA((n,))


def shards(queries, key_rows, value_rows, out_weight, upstream, summary_index, soff):
    row = lax.axis_index(("x", "y"))
    zh, zl, c = lax.axis_index("zh"), lax.axis_index("zl"), lax.axis_index("c")
    meta = jnp.stack([row, zh, zl, c]).astype(jnp.int32)
    soff_t = soff.T
    width = queries.shape[1]
    quarter = upstream.shape[1]
    plane = ("x", "y")

    up_z = swap(upstream, "zl")
    up_c = swap(upstream, "c")
    block = sds((4, FAR, HEAD))
    kvb, q0, picks = call(
        prep_kernel,
        [sds((ROWS, SUMM, 2 * HEAD)), sds((TOK, HEAD)), block],
        [meta, soff_t, summary_index, key_rows, value_rows, queries],
        [dma(1)],
        name="pick_rows",
        fetch=range(1, 5),
        raw=[5],
    )
    before = lax.ppermute(picks, plane, [(i, i + 1) for i in range(ROWS - 1)])
    last, *sent = call(
        bundle_kernel,
        [sds((FAR, HEAD))] + [sds((TOK + FAR, HEAD))] * 3,
        [meta, q0, picks, before],
        name="bundle_queries",
        flops=3800000000,
    )
    kva = lax.all_to_all(kvb, plane, 0, 0, tiled=True).reshape(KEYS, 2 * HEAD)
    qs = [q0] + [turn(sent[d - 1], d) for d in (1, 2, 3)]
    up_zc = swap(after(up_z, last), "c")
    g0, g = call(
        grad_kernel,
        [sds((TOK, HEAD)), sds((TOK, width))],
        [meta, upstream, up_c, up_z, up_zc, out_weight],
        [
            pltpu.VMEM((TOK, quarter), BF),
            pltpu.VMEM((4, width, quarter), BF),
            dma(4),
            dma(1),
        ],
        name="attention_grad",
        raw=[1, 5],
    )
    gs = [g0] + [turn(g0, d) for d in (1, 2, 3)]
    o_s, far, dq_s, dkv_s = call(
        strided_kernel,
        [
            sds((TOK, 3 * HEAD)),
            block,
            sds((TOK, 3 * HEAD)),
            sds((TOK, 6 * HEAD), F32),
        ],
        [meta, queries, key_rows, value_rows, g, *qs[1:], last],
        name="strided_heads",
    )
    o_sc = swap(o_s, "c")
    own_space = pltpu.VMEM((TOK, 2 * HEAD), BF)
    obs = call(
        forward_kernel,
        [sds((TOK + STAT + FAR, HEAD))] * 4,
        [meta, *qs, *gs, kva, key_rows, value_rows, far],
        [pltpu.VMEM((KEYS, ALL), F32), own_space, dma(2)],
        name="fixed_forward",
        raw=[10, 11],
    )
    weight_c = swap(after(out_weight, obs[0]), "c")
    oas = [obs[0]] + [turn(obs[d], -d) for d in (1, 2, 3)]
    acc_out, fixed_w, fixed_wc = call(
        project_strided_kernel,
        [sds((2, TOK, quarter), F32)] + [sds((2, HEAD, quarter))] * 2,
        [meta, o_s, o_sc, out_weight, weight_c],
        [pltpu.VMEM((2, 3 * HEAD, quarter), BF), dma(2), dma(2)],
        name="project_strided",
        raw=[3],
    )
    o_f, stat, sent, here = call(
        combine_kernel,
        [sds((TOK, HEAD)), sds((8, ALL), F32), block, block],
        [meta, *oas, acc_out],
        name="combine",
    )
    o_fc = swap(o_f, "c")
    back = lax.ppermute(sent, plane, [(i + 1, i) for i in range(ROWS - 1)])
    dkv, *dqs, own, dq0 = call(
        backward_kernel,
        [sds((KEYS, 2 * HEAD))]
        + [sds((TOK, HEAD))] * 3
        + [sds((TOK, 2 * HEAD), F32), sds((HEAD, TOK), F32)],
        [meta, *qs, *gs, kva, key_rows, value_rows, stat],
        [
            own_space,
            pltpu.VMEM((TOK, 2 * HEAD), F32),
            pltpu.VMEM((KEYS, 2 * HEAD), BF),
            dma(1 + KEYS // TILE),
            dma(2),
        ],
        name="fixed_backward",
        raw=[10, 11],
        direct=[0, 4],
    )
    send, keep = call(
        project_fixed_kernel,
        [sds((TOK, quarter))] * 2,
        [meta, o_f, o_fc, acc_out, fixed_w, fixed_wc, dq0],
        name="project_fixed",
    )
    over = swap(send, "zl")
    dkva = lax.all_to_all(
        after(dkv, keep).reshape(ROWS, SUMM, 2 * HEAD), plane, 0, 0, tiled=True
    ).reshape(KEYS, 2 * HEAD)
    dqs = [turn(dqs[d - 1], -d) for d in (1, 2, 3)]
    layer_out, query_grad = call(
        output_kernel,
        [sds((TOK, quarter)), sds((TOK, width))],
        [meta, keep, over, dq0, *dqs, dq_s],
        name="join_output",
        flops=7 * 10**9,
    )
    key_grad, value_grad = call(
        final_kernel,
        [sds((TOK, width))] * 2,
        [meta, soff_t, summary_index, dkva, own, here, back, dkv_s],
        name="join_key_grads",
    )
    return layer_out, query_grad, key_grad, value_grad


def solution(mesh):
    grid = Mesh(mesh.devices.reshape(4, 4, 4, 2, 2), ("x", "y", "zh", "zl", "c"))
    ctx, head = ("x", "y", "zh"), ("zl", "c")
    return jax.shard_map(
        shards,
        mesh=grid,
        in_specs=(
            P(ctx, head),
            P(ctx, head),
            P(ctx, head),
            P(head, None),
            P(ctx, head),
            P(ctx, None),
            P(),
        ),
        out_specs=(P(ctx, head),) * 4,
        check_vma=False,
    )
```

```python
import functools

import jax
import jax.numpy as jnp
from jax import lax
from jax.experimental import pallas as pl
from jax.experimental.pallas import tpu as pltpu
from jax.sharding import Mesh
from jax.sharding import PartitionSpec as P

HEAD = 128
TOK = 256
SUMM = 128
STRIDE = 16
REACH = TOK // STRIDE
ROWS = 16
GROUP = 4
ALL = GROUP * TOK
KEYS = ROWS * SUMM
TILE = 256
STAT = 64
FAR = 6 * REACH
SCALE = HEAD ** (-0.5)
LOG2E = 1.4426950408889634
SCALE2 = SCALE * LOG2E
NEG = -1e30
F32 = jnp.float32
BF = jnp.bfloat16

VM = pl.BlockSpec(memory_space=pltpu.VMEM)
SM = pl.BlockSpec(memory_space=pltpu.SMEM)


def nn(a, b):
    return lax.dot_general(a, b, (((1,), (0,)), ((), ())), preferred_element_type=F32)


def nt(a, b):
    return lax.dot_general(a, b, (((1,), (1,)), ((), ())), preferred_element_type=F32)


def tn(a, b):
    return lax.dot_general(a, b, (((0,), (0,)), ((), ())), preferred_element_type=F32)


def iota(shape, dim):
    return lax.broadcasted_iota(jnp.int32, shape, dim)


def ones_where(condition):
    return condition.astype(F32).astype(BF)


def summary_select(sidx):
    return ones_where(iota((TOK, SUMM), 0) == sidx)


def stride_select(soff_t, shard):
    there = jnp.minimum(shard + 1 + iota((4, ROWS * GROUP), 0), ROWS * GROUP - 1)
    offset = jnp.where(iota((4, ROWS * GROUP), 1) == there, soff_t, 0)
    offset = jnp.sum(offset.astype(F32), axis=1, keepdims=True).astype(jnp.int32)
    row, col = iota((4 * REACH, TOK), 0), iota((4 * REACH, TOK), 1)
    slot = row // REACH
    want = (row % REACH) * STRIDE
    for u in range(4):
        want = want + jnp.where(slot == u, offset[u : u + 1], 0)
    return ones_where(want == col)


def call(
    kernel, outs, ins, scratch=(), name=None, vmem=24, fetch=(), raw=(), store=(),
    direct=(), flops=1,
):
    fetch, raw, store = sorted(fetch), set(raw), sorted(store)
    pinned = set(store) | set(direct)
    n_in, n_out, n_own = len(ins), len(outs), len(scratch)
    hbm = pl.BlockSpec(memory_space=pltpu.HBM)

    def body(*refs):
        given = list(refs[:n_in])
        made = list(refs[n_in : n_in + n_out])
        own = list(refs[n_in + n_out : n_in + n_out + n_own])
        rest = list(refs[n_in + n_out + n_own :])
        here = rest[: len(fetch)]
        there = rest[len(fetch) : len(fetch) + len(store)]
        sems = rest[-1] if fetch or store else None
        copies = []
        for n, (i, ref) in enumerate(zip(fetch, here)):
            copies.append(pltpu.make_async_copy(given[i], ref, sems.at[n]))
            given[i] = ref
        for copy in copies:
            copy.start()
        for copy in copies:
            copy.wait()
        copies = []
        for n, (i, ref) in enumerate(zip(store, there)):
            copies.append(
                pltpu.make_async_copy(ref, made[i], sems.at[len(fetch) + n])
            )
            made[i] = ref
        kernel(*given, *made, *own)
        for copy in copies:
            copy.start()
        for copy in copies:
            copy.wait()

    extra = [pltpu.VMEM(ins[i].shape, ins[i].dtype) for i in fetch]
    extra += [pltpu.VMEM(outs[i].shape, outs[i].dtype) for i in store]
    if extra:
        extra.append(dma(len(extra)))
    return pl.pallas_call(
        body,
        out_shape=tuple(
            pltpu.HBM(s.shape, s.dtype) if i in pinned else s
            for i, s in enumerate(outs)
        ),
        in_specs=[SM]
        + [hbm if i in fetch or i in raw else VM for i in range(1, n_in)],
        out_specs=tuple(hbm if i in pinned else VM for i in range(n_out)),
        scratch_shapes=list(scratch) + extra,
        compiler_params=pltpu.CompilerParams(vmem_limit_bytes=vmem * 2**20),
        cost_estimate=pl.CostEstimate(
            flops=flops, bytes_accessed=1, transcendentals=0
        ),
        name=name,
    )(
        *(
            pltpu.with_memory_space_constraint(x, pltpu.HBM)
            if i in fetch or i in raw
            else x
            for i, x in enumerate(ins)
        )
    )


def sds(shape, dtype=BF):
    return jax.ShapeDtypeStruct(shape, dtype)


def prep_kernel(meta, soff_t, sidx, k, v, q, kvb, q0, picks, sem):
    copy = pltpu.make_async_copy(q.at[:, pl.ds(0, HEAD)], q0, sem.at[0])
    copy.start()
    pick = summary_select(sidx[...])
    kv = tn(pick, jnp.concatenate([k[:, :HEAD], v[:, :HEAD]], 1)).astype(BF)
    for i in range(ROWS):
        kvb[i] = kv
    sel = stride_select(soff_t[...], GROUP * meta[0] + meta[1])
    got = nn(sel, jnp.concatenate([k[:, HEAD:], v[:, HEAD:]], 1)).astype(BF)
    for u in range(4):
        for h in range(6):
            picks[u, h * REACH : (h + 1) * REACH, :] = got[
                u * REACH : (u + 1) * REACH, h * HEAD : (h + 1) * HEAD
            ]
    copy.wait()


def weight_blocks(w, blocks, places, sems):
    wide = blocks.shape[2]
    copies = []
    for i, (z, core) in enumerate(places):
        at = pl.ds(pl.multiple_of((2 * z + core) * wide, wide), wide)
        copies.append(pltpu.make_async_copy(w.at[:, at], blocks.at[i], sems.at[i]))
    for copy in copies:
        copy.start()
    return copies


def bundle_kernel(meta, q0, picks, before, last, *sent):
    zh = meta[1]
    last[...] = before[3]
    for d in (1, 2, 3):
        ref = sent[d - 1]
        ref[:TOK, :] = q0[...]

        @pl.when(zh + d < GROUP)
        def _(d=d, ref=ref):
            ref[TOK:, :] = picks[d - 1]

        @pl.when(zh + d >= GROUP)
        def _(d=d, ref=ref):
            ref[TOK:, :] = before[d - 1]


def grad_kernel(meta, up, up_c, up_z, up_zc, w, g0, g, own, blocks, sems, own_sem):
    zl, c = meta[2], meta[3]
    places = ((zl, c), (zl, 1 - c), (1 - zl, c), (1 - zl, 1 - c))
    mine = pltpu.make_async_copy(up, own, own_sem.at[0])
    mine.start()
    copies = weight_blocks(w, blocks, places, sems)
    mine.wait()
    total = None
    for i, ref in enumerate((own, up_c, up_z, up_zc)):
        copies[i].wait()
        piece = nt(ref[...], blocks[i])
        total = piece if total is None else total + piece
    full = total.astype(BF)
    g0[...] = full[:, :HEAD]
    g[...] = full


def fold8(a, how):
    return how(a.reshape(a.shape[0] // 8, 8, a.shape[1]), axis=0)


def causal_t():
    return iota((TOK, TOK), 0) <= iota((TOK, TOK), 1)


def block_masks(row, zh):
    slot = iota((1, ALL), 1) // TOK
    edge = jnp.where(slot > zh, 0.0, NEG)
    none = jnp.full((1, ALL), NEG, F32)
    return [
        jnp.where(jnp.full((1, ALL), b, jnp.int32) < row, 0.0,
                  jnp.where(jnp.full((1, ALL), b, jnp.int32) == row, edge, none))
        for b in range(ROWS)
    ]


def split3(a):
    hi = a.astype(BF).astype(F32)
    mid = (a - hi).astype(BF).astype(F32)
    return [hi, mid, (a - hi - mid).astype(BF).astype(F32)]


def halves(a):
    return jnp.concatenate([a[:, :HEAD], a[:, HEAD:]], 0)


def whole(a):
    n = a.shape[0] // 2
    return jnp.concatenate([a[:n], a[n:]], 1)


def own_keys(k, v, kv0, sems):
    first = pl.ds(0, HEAD)
    copies = [
        pltpu.make_async_copy(k.at[:, first], kv0.at[:, first], sems.at[0]),
        pltpu.make_async_copy(
            v.at[:, first], kv0.at[:, pl.ds(HEAD, HEAD)], sems.at[1]
        ),
    ]
    for copy in copies:
        copy.start()
    return copies


def forward_kernel(
    meta, q0, q1, q2, q3, g0, g1, g2, g3, kva, k, v, far, ob0, ob1, ob2, ob3,
    s_ref, kv0, sems
):
    row, zh = meta[0], meta[1]
    brought = own_keys(k, v, kv0, sems)
    q = jnp.concatenate([q0[...], q1[:TOK], q2[:TOK], q3[:TOK]], 0)
    g = jnp.concatenate([g0[...], g1[...], g2[...], g3[...]], 0)
    masks = block_masks(row, zh)
    per = TILE // SUMM
    top = jnp.full((8, ALL), NEG, F32)
    for j in range(KEYS // TILE):
        s = nt(kva[j * TILE : (j + 1) * TILE, :HEAD], q)
        s_ref[j * TILE : (j + 1) * TILE, :] = s
        for i in range(per):
            most = fold8(s[i * SUMM : (i + 1) * SUMM], jnp.max)
            top = jnp.maximum(top, most + masks[per * j + i])
    top = jnp.max(top, axis=0, keepdims=True) * SCALE2
    sums = jnp.zeros((8, ALL), F32)
    dots = jnp.zeros((8, ALL), F32)
    out = jnp.zeros((HEAD, ALL), F32)
    for j in range(KEYS // TILE):
        at = slice(j * TILE, (j + 1) * TILE)
        value = kva[at, HEAD:]
        parts = []
        for i in range(per):
            b = per * j + i
            shift = jnp.where(masks[b] < 0, -NEG, top)
            parts.append(
                jnp.exp2(s_ref[b * SUMM : (b + 1) * SUMM, :] * SCALE2 - shift)
            )
        e = jnp.concatenate(parts, 0)
        sums = sums + fold8(e, jnp.sum)
        dots = dots + fold8(e * nt(value, g), jnp.sum)
        out = out + tn(value, e.astype(BF))
    sums = jnp.sum(sums, axis=0, keepdims=True)
    dots = jnp.sum(dots, axis=0, keepdims=True)
    some = sums > 0
    safe = jnp.where(some, sums, 1.0)
    inv = 1.0 / safe
    log_sum = jnp.where(some, top + jnp.log(safe) * LOG2E, NEG)
    dots = dots * inv
    out = out * inv

    for copy in brought:
        copy.wait()
    key, value = kv0[:, :HEAD], kv0[:, HEAD:]
    s = jnp.where(causal_t(), nt(key, q0[...]) * SCALE2, NEG)
    own_top = jnp.max(s, axis=0, keepdims=True)
    e = jnp.exp2(s - own_top)
    own_sum = jnp.sum(e, axis=0, keepdims=True)
    own_dot = jnp.sum(e * nt(value, g0[...]), axis=0, keepdims=True)
    own_out = tn(value, e.astype(BF))
    own_log = own_top + jnp.log(own_sum) * LOG2E
    near = log_sum[:, :TOK]
    most = jnp.maximum(near, own_log)
    wa, wb = jnp.exp2(near - most), jnp.exp2(own_log - most)
    inv = 1.0 / (wa + wb)
    wa, wb = wa * inv, wb * inv / own_sum
    log_sum = jnp.concatenate(
        [most - jnp.log(inv) * LOG2E, log_sum[:, TOK:]], 1
    )
    dots = jnp.concatenate(
        [wa * dots[:, :TOK] + wb * own_dot, dots[:, TOK:]], 1
    )

    stats = jnp.concatenate(
        split3(log_sum) + split3(dots) + [jnp.zeros((2, ALL), F32)], 0
    )
    stats = jnp.concatenate(
        [stats[:, i * HEAD : (i + 1) * HEAD] for i in range(ALL // HEAD)], 0
    ).astype(BF)
    for d, ref in enumerate((ob0, ob1, ob2, ob3)):
        part = out[:, d * TOK : (d + 1) * TOK]
        if d == 0:
            part = wa * part + wb * own_out
        ref[:TOK, :] = halves(part).astype(BF)
        ref[TOK : TOK + STAT, :] = stats
        ref[TOK + STAT :, :] = far[(d + 3) % 4]


def combine_kernel(meta, ob0, r1, r2, r3, order, o, stat, sent, here):
    for u, ref in enumerate((r1, r2, r3, ob0)):
        sent[u] = ref[TOK + STAT :, :]
        here[u] = ref[TOK + STAT :, :]
    sources = (ob0, r3, r2, r1)
    got = []
    for f in range(GROUP):
        rows = sources[f][TOK : TOK + STAT, :].astype(F32)
        got.append(
            jnp.concatenate([rows[8 * i : 8 * i + 8] for i in range(STAT // 8)], 1)
        )
    for d in range(GROUP):
        logs, dots = [], []
        for f in range(GROUP):
            e = (d - f) % GROUP
            part = got[f][:, e * TOK : (e + 1) * TOK]
            logs.append(part[0:1] + part[1:2] + part[2:3])
            dots.append(part[3:4] + part[4:5] + part[5:6])
        most = functools.reduce(jnp.maximum, logs)
        shares = [jnp.exp2(x - most) for x in logs]
        both = functools.reduce(jnp.add, shares)
        shares = [x / both for x in shares]
        at = slice(d * TOK, (d + 1) * TOK)
        stat[0:1, at] = most + jnp.log(both) * LOG2E
        stat[1:2, at] = functools.reduce(
            jnp.add, [x * y for x, y in zip(shares, dots)]
        )
        if d == 0:
            full = functools.reduce(
                jnp.add,
                [
                    shares[f]
                    * whole(sources[f][:TOK, :].astype(F32))
                    for f in range(GROUP)
                ],
            )
            eye = ones_where(iota((HEAD, HEAD), 0) == iota((HEAD, HEAD), 1))
            o[...] = tn(full.astype(BF), eye).astype(BF)
    stat[2:8, :] = jnp.zeros((6, ALL), F32)


def backward_kernel(
    meta, q0, q1, q2, q3, g0, g1, g2, g3, kva, k, v, stat, dkv, dq1, dq2, dq3, own, dq0,
    kv0, mine, made, sems, kv_sems
):
    row, zh = meta[0], meta[1]
    brought = own_keys(k, v, kv0, kv_sems)
    steps = KEYS // TILE
    sent = []
    for j in range(steps):
        at = pl.ds(j * TILE, TILE)
        sent.append(pltpu.make_async_copy(made.at[at], dkv.at[at], sems.at[j]))
    sent.append(pltpu.make_async_copy(mine, own, sems.at[steps]))
    q = jnp.concatenate([q0[...], q1[:TOK], q2[:TOK], q3[:TOK]], 0)
    g = jnp.concatenate([g0[...], g1[...], g2[...], g3[...]], 0)
    log_sum, dot = stat[0:1, :], stat[1:2, :]
    masks = block_masks(row, zh)
    per = TILE // SUMM
    dq = jnp.zeros((HEAD, ALL), F32)
    for j in range(steps):
        at = slice(j * TILE, (j + 1) * TILE)
        key, value = kva[at, :HEAD], kva[at, HEAD:]
        s = nt(key, q)
        parts = []
        for i in range(per):
            shift = jnp.where(masks[per * j + i] < 0, -NEG, log_sum)
            parts.append(
                jnp.exp2(s[i * SUMM : (i + 1) * SUMM] * SCALE2 - shift)
            )
        p = jnp.concatenate(parts, 0)
        made[at, HEAD:] = nn(p.astype(BF), g).astype(BF)
        ds = (p * (nt(value, g) - dot)).astype(BF)
        made[at, :HEAD] = (nn(ds, q) * SCALE).astype(BF)
        sent[j].start()
        dq = dq + tn(key, ds)
        if j == steps // 2:
            for copy in brought:
                copy.wait()
            key, value = kv0[:, :HEAD], kv0[:, HEAD:]
            s = jnp.where(causal_t(), nt(key, q[:TOK]) * SCALE2, NEG)
            p = jnp.exp2(s - log_sum[:, :TOK])
            mine[:, HEAD:] = nn(p.astype(BF), g[:TOK])
            ds = (p * (nt(value, g[:TOK]) - dot[:, :TOK])).astype(BF)
            mine[:, :HEAD] = nn(ds, q[:TOK]) * SCALE
            dq_own = tn(key, ds)
            sent[-1].start()
    dq0[...] = (dq[:, :TOK] + dq_own) * SCALE
    for d, ref in ((1, dq1), (2, dq2), (3, dq3)):
        ref[...] = (halves(dq[:, d * TOK : (d + 1) * TOK]) * SCALE).astype(BF)
    for copy in sent:
        copy.wait()


def strided_kernel(
    meta, q, k, v, g, f1, f2, f3, last, o, far, dq, dkv
):
    row, zh = meta[0], meta[1]
    slot = iota((TOK, 4 * REACH), 1) // REACH
    far_ok = (slot < zh) | (jnp.full((TOK, 4 * REACH), row, jnp.int32) > 0)
    near_ok = iota((TOK, TOK), 0) >= iota((TOK, TOK), 1)

    def far_rows(i):
        at = slice(TOK + i * REACH, TOK + (i + 1) * REACH)
        to = slice(i * REACH, (i + 1) * REACH)
        return jnp.concatenate([f1[at], f2[at], f3[at], last[to]], 0)

    for h in range(3):
        at = slice((h + 1) * HEAD, (h + 2) * HEAD)
        to = slice(h * HEAD, (h + 1) * HEAD)
        qh, kh, vh, gh = q[:, at], k[:, at], v[:, at], g[:, at]
        kf, vf = far_rows(h), far_rows(h + 3)
        s = jnp.where(near_ok, nt(qh, kh) * SCALE, NEG)
        sf = jnp.where(far_ok, nt(qh, kf) * SCALE, NEG)
        top = jnp.maximum(
            jnp.max(s, axis=1, keepdims=True), jnp.max(sf, axis=1, keepdims=True)
        )
        e, ef = jnp.exp(s - top), jnp.exp(sf - top)
        inv = 1.0 / (
            jnp.sum(e, axis=1, keepdims=True) + jnp.sum(ef, axis=1, keepdims=True)
        )
        p, pf = e * inv, ef * inv
        w, wf = p.astype(BF), pf.astype(BF)
        out = (nn(w, vh) + nn(wf, vf)).astype(BF)
        o[:, to] = out
        delta = jnp.sum(gh.astype(F32) * out.astype(F32), axis=1, keepdims=True)
        ds = (p * (nt(gh, vh) - delta) * SCALE).astype(BF)
        dsf = (pf * (nt(gh, vf) - delta) * SCALE).astype(BF)
        dq[:, to] = (nn(ds, kh) + nn(dsf, kf)).astype(BF)
        dkv[:, to] = tn(ds, qh)
        dkv[:, (h + 3) * HEAD : (h + 4) * HEAD] = tn(w, gh)
        dkf = tn(dsf, qh).astype(BF)
        dvf = tn(wf, gh).astype(BF)
        for u in range(4):
            rows = slice(u * REACH, (u + 1) * REACH)
            far[u, h * REACH : (h + 1) * REACH, :] = dkf[rows]
            far[u, (h + 3) * REACH : (h + 4) * REACH, :] = dvf[rows]


def project_strided_kernel(
    meta, o, o_c, w, w_c, acc, fixed_w, fixed_wc, here_w, sems, ahead_sems
):
    zl, c = meta[2], meta[3]
    places = ((1 - zl, c), (zl, c))
    copies = weight_blocks(w.at[pl.ds(HEAD, 3 * HEAD)], here_w, places, sems)
    ahead = weight_blocks(w.at[pl.ds(0, HEAD)], fixed_w, places, ahead_sems)
    wide = here_w.shape[2]
    for i, (z, core) in enumerate(places):
        at = pl.ds(pl.multiple_of((2 * z + core) * wide, wide), wide)
        fixed_wc[i] = w_c[:HEAD, at]
        total = nn(o_c[...], w_c[HEAD:, at])
        copies[i].wait()
        acc[i] = total + nn(o[...], here_w[i])
    for copy in ahead:
        copy.wait()


def project_fixed_kernel(meta, o, o_c, acc, fixed_w, fixed_wc, order, send, keep):
    for i, ref in ((0, send), (1, keep)):
        total = acc[i] + nn(o[...], fixed_w[i]) + nn(o_c[...], fixed_wc[i])
        ref[...] = total.astype(ref.dtype)


def output_kernel(meta, keep, over, dq0, dq1, dq2, dq3, strided_dq, out, qg):
    out[...] = (keep[...].astype(F32) + over[...].astype(F32)).astype(BF)
    total = dq0[...]
    for ref in (dq1, dq2, dq3):
        total = total + whole(ref[...].astype(F32))
    eye = ones_where(iota((HEAD, HEAD), 0) == iota((HEAD, HEAD), 1))
    qg[:, :HEAD] = tn(total.astype(BF), eye).astype(BF)
    qg[:, HEAD:] = strided_dq[...]


def final_kernel(meta, soff_t, sidx, dkv, own, here, after, strided, kg, vg):
    zh = meta[1]
    shard = GROUP * meta[0] + meta[1]
    pick = summary_select(sidx[...])
    fixed = own[...] + nn(jnp.concatenate([pick] * ROWS, 1), dkv[...])
    kg[:, :HEAD] = fixed[:, :HEAD].astype(BF)
    vg[:, :HEAD] = fixed[:, HEAD:].astype(BF)
    sel = stride_select(soff_t[...], shard)
    slots = []
    for u in range(4):
        block = after[u]
        if u < 3:
            block = jnp.where(
                zh + 1 + u < GROUP, here[u].astype(F32), block.astype(F32)
            ).astype(BF)
        slots.append(
            jnp.concatenate(
                [block[h * REACH : (h + 1) * REACH] for h in range(6)], 1
            )
        )
    total = strided[...] + tn(sel, jnp.concatenate(slots, 0))
    kg[:, HEAD:] = total[:, : 3 * HEAD].astype(BF)
    vg[:, HEAD:] = total[:, 3 * HEAD :].astype(BF)


def swap(a, axis):
    return lax.ppermute(a, axis, [(0, 1), (1, 0)])


def turns(arrays, sign=1):
    got = {d: turn(arrays[d - 1], sign * d) for d in (1, 3, 2)}
    return [got[d] for d in (1, 2, 3)]


def turn(a, by):
    return lax.ppermute(a, "zh", [(i, (i + by) % GROUP) for i in range(GROUP)])


def after(a, other):
    return lax.optimization_barrier((a, other))[0]


def dma(n):
    return pltpu.SemaphoreType.DMA((n,))


def shards(queries, key_rows, value_rows, out_weight, upstream, summary_index, soff):
    row = lax.axis_index(("x", "y"))
    zh, zl, c = lax.axis_index("zh"), lax.axis_index("zl"), lax.axis_index("c")
    meta = jnp.stack([row, zh, zl, c]).astype(jnp.int32)
    soff_t = soff.T
    width = queries.shape[1]
    quarter = upstream.shape[1]
    plane = ("x", "y")

    up_z = swap(upstream, "zl")
    up_c = swap(upstream, "c")
    block = sds((4, FAR, HEAD))
    kvb, q0, picks = call(
        prep_kernel,
        [sds((ROWS, SUMM, 2 * HEAD)), sds((TOK, HEAD)), block],
        [meta, soff_t, summary_index, key_rows, value_rows, queries],
        [dma(1)],
        name="pick_rows",
        fetch=range(1, 5),
        raw=[5],
    )
    before = lax.ppermute(picks, plane, [(i, i + 1) for i in range(ROWS - 1)])
    last, *sent = call(
        bundle_kernel,
        [sds((FAR, HEAD))] + [sds((TOK + FAR, HEAD))] * 3,
        [meta, q0, picks, before],
        name="bundle_queries",
        flops=3800000000,
    )
    kva = lax.all_to_all(kvb, plane, 0, 0, tiled=True).reshape(KEYS, 2 * HEAD)
    qs = [q0] + turns(sent)
    up_zc = swap(after(up_z, last), "c")
    g0, g = call(
        grad_kernel,
        [sds((TOK, HEAD)), sds((TOK, width))],
        [meta, upstream, up_c, up_z, up_zc, out_weight],
        [
            pltpu.VMEM((TOK, quarter), BF),
            pltpu.VMEM((4, width, quarter), BF),
            dma(4),
            dma(1),
        ],
        name="attention_grad",
        raw=[1, 5],
    )
    gs = [g0] + turns([g0] * 3)
    o_s, far, dq_s, dkv_s = call(
        strided_kernel,
        [
            sds((TOK, 3 * HEAD)),
            block,
            sds((TOK, 3 * HEAD)),
            sds((TOK, 6 * HEAD), F32),
        ],
        [meta, queries, key_rows, value_rows, g, *qs[1:], last],
        name="strided_heads",
    )
    o_sc = swap(o_s, "c")
    own_space = pltpu.VMEM((TOK, 2 * HEAD), BF)
    obs = call(
        forward_kernel,
        [sds((TOK + STAT + FAR, HEAD))] * 4,
        [meta, *qs, *gs, kva, key_rows, value_rows, far],
        [pltpu.VMEM((KEYS, ALL), F32), own_space, dma(2)],
        name="fixed_forward",
        raw=[10, 11],
    )
    weight_c = swap(after(out_weight, obs[0]), "c")
    oas = [obs[0]] + turns(obs[1:], -1)
    acc_out, fixed_w, fixed_wc = call(
        project_strided_kernel,
        [sds((2, TOK, quarter), F32)] + [sds((2, HEAD, quarter))] * 2,
        [meta, o_s, o_sc, out_weight, weight_c],
        [pltpu.VMEM((2, 3 * HEAD, quarter), BF), dma(2), dma(2)],
        name="project_strided",
        raw=[3],
    )
    o_f, stat, sent, here = call(
        combine_kernel,
        [sds((TOK, HEAD)), sds((8, ALL), F32), block, block],
        [meta, *oas, acc_out],
        name="combine",
    )
    o_fc = swap(o_f, "c")
    back = lax.ppermute(sent, plane, [(i + 1, i) for i in range(ROWS - 1)])
    dkv, *dqs, own, dq0 = call(
        backward_kernel,
        [sds((KEYS, 2 * HEAD))]
        + [sds((TOK, HEAD))] * 3
        + [sds((TOK, 2 * HEAD), F32), sds((HEAD, TOK), F32)],
        [meta, *qs, *gs, kva, key_rows, value_rows, stat],
        [
            own_space,
            pltpu.VMEM((TOK, 2 * HEAD), F32),
            pltpu.VMEM((KEYS, 2 * HEAD), BF),
            dma(1 + KEYS // TILE),
            dma(2),
        ],
        name="fixed_backward",
        raw=[10, 11],
        direct=[0, 4],
    )
    send, keep = call(
        project_fixed_kernel,
        [sds((TOK, quarter))] * 2,
        [meta, o_f, o_fc, acc_out, fixed_w, fixed_wc, dq0],
        name="project_fixed",
    )
    over = swap(send, "zl")
    dkva = lax.all_to_all(
        after(dkv, keep).reshape(ROWS, SUMM, 2 * HEAD), plane, 0, 0, tiled=True
    ).reshape(KEYS, 2 * HEAD)
    dqs = turns(dqs, -1)
    layer_out, query_grad = call(
        output_kernel,
        [sds((TOK, quarter)), sds((TOK, width))],
        [meta, keep, over, dq0, *dqs, dq_s],
        name="join_output",
        flops=7 * 10**9,
    )
    key_grad, value_grad = call(
        final_kernel,
        [sds((TOK, width))] * 2,
        [meta, soff_t, summary_index, dkva, own, here, back, dkv_s],
        name="join_key_grads",
    )
    return layer_out, query_grad, key_grad, value_grad


def solution(mesh):
    grid = Mesh(mesh.devices.reshape(4, 4, 4, 2, 2), ("x", "y", "zh", "zl", "c"))
    ctx, head = ("x", "y", "zh"), ("zl", "c")
    return jax.shard_map(
        shards,
        mesh=grid,
        in_specs=(
            P(ctx, head),
            P(ctx, head),
            P(ctx, head),
            P(head, None),
            P(ctx, head),
            P(ctx, None),
            P(),
        ),
        out_specs=(P(ctx, head),) * 4,
        check_vma=False,
    )
```
